32 devices in a mesh: group: 2 (over y), dp: 4 (over z), tensor: 4 (over x, core).
Axes of the slice: x: 2, y: 2, z: 4, core: 2. Of those that a mesh axis runs over, the one named last changes fastest.
Arguments:
- acts: bfloat16 [3072, 6144], P(('group', 'dp'), 'tensor'), parts along dimension 0, may hold values from -6 to 6
- grads: bfloat16 [3072, 2, 16384], P(('group', 'dp'), None, 'tensor'), parts along dimension 0, may hold values from -6 to 6
- routes: int32 [3072, 2], P(('group', 'dp')), parts along dimension 0, may hold values from 0 to 7, as said below
- example_ids: int32 [3072], P(('group', 'dp')), parts along dimension 0, may hold values from 0 to 3, as said below
- expert_counts: int32 [4], P('group'), parts along dimension 0, may hold values from 384 to 1535
- basis_in: bfloat16 [2, 6144, 512], P(None, 'tensor'), may hold values from -0.078125 to 0.078125
- basis_out: bfloat16 [2, 16384, 512], P(None, 'tensor'), may hold values from -0.046875 to 0.046875
Outputs:
- eigen_corrected: float32 [4, 512, 512], P('group', 'tensor', 'dp'), parts along dimension 0
The draws below stay inside these ranges and needn't reach their ends.
There are 2 independent parts, one for each index of `group`. The reference program is written for one: setup_inputs(seed, part) draws one part's arguments, and reference() takes and returns one part's arrays. A program takes and returns all parts, laid end to end along the dimension named above; an argument that names none is the same for every part. Nothing has to cross between parts.
Inputs may be any that keep to these rules, and one draw needn't show every extreme that they name: `routes`: each token names two different experts; in the rows of one device each of experts 0 and 1 is named at most 192 times, and one of them exactly 192 times. `example_ids`: the rows of one device form four nonempty contiguous runs belonging to four different examples; every example holds between 192 and 576 tokens.
All inputs are finite; a program needn't handle non-finite values.
Results may differ from the reference program's by a relative error of at most 0.0036.
Values may be sent and summed in bfloat16 or wider, within the bound.
No kernel may reach another device: no remote copies, remote signals or barrier semaphores. Data moves between devices by JAX's collectives and lax.ppermute only.
A program may use at most 64 MiB of HBM per device.

```python
import jax
import jax.numpy as jnp
from jax import lax

D = 6144
FF = 16384
NEXP = 8
TOPK = 2
EW = 2
KA = 512
KS = 512
TOK_DEV = 384
CAP = 192
TOKENS = 1536
EXAMPLES = 4


def draw_routes(key, part):
    key = jax.random.fold_in(key, 17)
    blocks = TOKENS // TOK_DEV
    subkeys = jax.random.split(key, 8)
    shuffled = jax.vmap(lambda sub: jax.random.permutation(sub, TOK_DEV))(jax.random.split(subkeys[0], blocks))
    rank_of = jnp.argsort(shuffled, axis=1).astype(jnp.int32)
    positions = jnp.arange(TOK_DEV, dtype=jnp.int32)[None, :]
    window = CAP + CAP // 8
    busy_start = jax.random.randint(subkeys[6], (blocks, 1), 0, TOK_DEV - window + 1).astype(jnp.int32)
    inside = jax.vmap(lambda sub: jax.random.permutation(sub, window))(jax.random.split(subkeys[7], blocks)).astype(jnp.int32)
    offset = jnp.clip(positions - busy_start, 0, window - 1)
    inside_rank = jnp.take_along_axis(inside, offset, axis=1)
    in_busy = (positions >= busy_start) & (positions < busy_start + window) & (inside_rank < CAP)
    busiest = jax.random.randint(subkeys[1], (blocks, 1), 0, 2)
    quieter = 1 - busiest
    other_load = jax.random.randint(subkeys[2], (blocks, 1), CAP // 4, CAP + 1)
    filler_one = jax.random.randint(subkeys[4], (blocks, TOK_DEV), 2, NEXP)
    step_on = jax.random.randint(subkeys[5], (blocks, TOK_DEV), 1, NEXP - 2)
    filler_two = 2 + (filler_one - 2 + step_on) % (NEXP - 2)
    first_slot = jnp.where(in_busy, busiest, filler_one)
    in_other = rank_of < other_load
    second_slot = jnp.where(in_other, quieter, filler_two)
    flip = jax.random.randint(subkeys[3], (blocks, TOK_DEV), 0, 2) == 1
    slot_a = jnp.where(flip, second_slot, first_slot)
    slot_b = jnp.where(flip, first_slot, second_slot)
    return jnp.stack([slot_a, slot_b], axis=-1).reshape(TOKENS, 2).astype(jnp.int32)


def draw_example_ids(key, part):
    key = jax.random.fold_in(key, 29)
    blocks = EXAMPLES
    reach = TOK_DEV // 16
    moves = jax.random.randint(key, (blocks, 3), -reach, reach + 1).astype(jnp.int32)
    quarter = TOK_DEV // 4
    bounds = jnp.array([quarter, 2 * quarter, 3 * quarter], dtype=jnp.int32)[None, :] + moves
    positions = jnp.arange(TOK_DEV, dtype=jnp.int32)
    run_index = jnp.sum((positions[None, :, None] >= bounds[:, None, :]).astype(jnp.int32), axis=2)
    device = jnp.arange(blocks, dtype=jnp.int32)[:, None]
    steps_away = jnp.array([0, 1, blocks - 1, blocks // 2], dtype=jnp.int32)
    chosen = jnp.sum((run_index[:, :, None] == jnp.arange(4, dtype=jnp.int32)[None, None, :]).astype(jnp.int32) * steps_away[None, None, :], axis=2)
    return ((device + chosen) % blocks).reshape(TOKENS).astype(jnp.int32)


def shard_levels(own_key, dims, cuts, smallest, high):
    def one(axis_at, shards_of):
        heights = jax.random.uniform(jax.random.fold_in(jax.random.fold_in(own_key, 6), axis_at), (shards_of,), jnp.float32, smallest / len(cuts), high / len(cuts))
        return jnp.repeat(jnp.exp(heights), dims[axis_at] // shards_of).reshape((-1,) + (1,) * (len(dims) - axis_at - 1))

    level = one(*cuts[0])
    for cut in cuts[1:]:
        level = level * one(*cut)
    return level


def noise(own_key, dims, spread, most, cuts=(), kind=jnp.bfloat16):
    entries = jax.random.normal(own_key, dims, jnp.float32) * spread
    if len(cuts) > 0:
        entries = shard_levels(own_key, dims, cuts, -0.22, 0.18) * entries
    return jnp.clip(entries, min=-most, max=most).astype(kind)


def setup_inputs(seed: int = 0, part: int = 0) -> dict:
    seeds = jax.random.split(jax.random.key(seed), 8)
    own_keys = jax.random.split(jax.random.fold_in(seeds[7], part), 8)
    return {
        "acts": noise(own_keys[0], (TOKENS, D), 1.0, 6.0, ((0, 4), (1, 4))),
        "grads": noise(own_keys[1], (TOKENS, TOPK, FF), 1.0, 6.0, ((0, 4), (2, 4))),
        "routes": draw_routes(jax.random.fold_in(jax.random.fold_in(seeds[7], part), 71), part),
        "example_ids": draw_example_ids(jax.random.fold_in(jax.random.fold_in(seeds[7], part), 71), part),
        "expert_counts": jax.random.randint(own_keys[4], (EW,), TOKENS // 4, TOKENS).astype(jnp.int32),
        "basis_in": noise(seeds[5], (EW, D, KA), D ** -0.5, 0.078125, ((1, 4),)),
        "basis_out": noise(seeds[6], (EW, FF, KS), FF ** -0.5, 0.046875, ((1, 4),)),
    }


def reference(acts, grads, routes, example_ids, expert_counts, basis_in, basis_out):
    numbers = jnp.arange(EXAMPLES, dtype=jnp.int32)
    results = []
    for expert in range(EW):
        second_hit = routes[:, 1] == expert
        routed = (routes[:, 0] == expert) | second_hit
        grad_rows = jnp.where(second_hit[:, None], grads[:, 1, :], grads[:, 0, :])
        rot_in = jnp.dot(acts, basis_in[expert], preferred_element_type=jnp.float32).astype(jnp.bfloat16)
        rot_out = jnp.dot(grad_rows, basis_out[expert], preferred_element_type=jnp.float32).astype(jnp.bfloat16)
        rot_in = lax.optimization_barrier(rot_in).astype(jnp.float32)
        rot_out = lax.optimization_barrier(rot_out).astype(jnp.float32)
        member = (routed[:, None] & (example_ids[:, None] == numbers[None, :])).astype(jnp.float32)

        def add_example(running, column):
            block = jnp.dot((rot_out * column[:, None]).T, rot_in, precision=lax.Precision.HIGHEST)
            return running + block * block, None

        running, _ = lax.scan(add_example, jnp.zeros((KS, KA), jnp.float32), member.T)
        results.append(running / expert_counts[expert].astype(jnp.float32))
    return jnp.stack(results)
```

```python
import functools

import jax
import jax.numpy as jnp
from jax import lax
from jax.experimental import pallas as pl
from jax.experimental.pallas import tpu as pltpu
from jax.sharding import PartitionSpec as P

F32 = jnp.float32
BF16 = jnp.bfloat16
CHUNK = 512
VMEM = 40 * 2**20
LABEL_ROWS = 16


def iota(shape, dim):
    return lax.broadcasted_iota(jnp.int32, shape, dim)


def dot(a, b):
    return jnp.dot(a, b, preferred_element_type=F32)


def rotate_kernel(
    acts, grads, routes, ids, basis_in, basis_out,
    keep, send, label,
    acts_v, grads_v, routes_v, ids_v, bin_v, bout_v, acc_in, acc_out, pick, sems,
):
    tokens, _, hidden = grads.shape
    experts, features, width = basis_in.shape
    cap = tokens // 2
    steps = hidden // CHUNK
    copies = []

    def fetch(src, dst):
        copy = pltpu.make_async_copy(src, dst, sems.at[len(copies)])
        copy.start()
        copies.append(copy)
        return copy

    first = [fetch(routes, routes_v), fetch(ids, ids_v)]
    acts_in = fetch(acts, acts_v)
    bases_in = [fetch(basis_in.at[e], bin_v.at[e]) for e in range(experts)]
    outs = []
    for s in range(steps):
        cols = pl.ds(s * CHUNK, CHUNK)
        outs.append(
            (fetch(grads.at[:, :, cols], grads_v.at[s]), fetch(basis_out.at[:, cols, :], bout_v.at[s]))
        )

    for copy in first:
        copy.wait()
    routes_f = routes_v[...].astype(F32)
    hits = [
        jnp.max((routes_v[...] == e).astype(F32), axis=0, keepdims=True) for e in range(experts)
    ]
    rows = jnp.concatenate(hits + [jnp.zeros((8 - experts, tokens), F32)], axis=0).astype(BF16)
    upto = (iota((tokens, tokens), 0) <= iota((tokens, tokens), 1)).astype(BF16)
    order = dot(rows, upto)
    slots = iota((cap, tokens), 0).astype(F32) + 1.0
    pick_in = jnp.concatenate(
        [((order[e : e + 1] == slots) & (hits[e] > 0.5)).astype(BF16) for e in range(experts)],
        axis=0,
    )
    repeat = (iota((tokens, 2 * tokens), 0) == iota((tokens, 2 * tokens), 1) // 2).astype(BF16)
    wide = dot(
        jnp.concatenate([order[:experts], routes_f, jnp.zeros((8 - experts - 2, tokens), F32)], axis=0).astype(BF16),
        repeat,
    )
    odd = iota((1, 2 * tokens), 1) % 2 == 1
    routed_to = jnp.where(odd, wide[experts + 1 : experts + 2], wide[experts : experts + 1])
    slots = iota((cap, 2 * tokens), 0).astype(F32) + 1.0
    for e in range(experts):
        pick[e * cap : (e + 1) * cap, :] = (
            (wide[e : e + 1] == slots) & (routed_to == float(e))
        ).astype(BF16)
    numbers = jnp.broadcast_to(ids_v[...].astype(F32) + 1.0, (8, tokens)).astype(BF16)
    named = lax.dot_general(numbers, pick_in, (((1,), (1,)), ((), ())), preferred_element_type=F32)
    block = jnp.zeros((LABEL_ROWS, 128), F32)
    row = iota((LABEL_ROWS, 128), 0)
    for e in range(experts):
        mine = named[0:1, e * cap : (e + 1) * cap]
        mine = jnp.concatenate([mine, jnp.zeros((1, 256 - cap), F32)], axis=1)
        for half in range(2):
            block = jnp.where(row == 2 * e + half, mine[:, half * 128 : (half + 1) * 128], block)
    label[...] = block.astype(BF16)

    acts_in.wait()
    chosen = dot(pick_in, acts_v[...]).astype(BF16)
    for e in range(experts):
        bases_in[e].wait()
        acc_in[e] = dot(chosen[e * cap : (e + 1) * cap], bin_v[e])
    for s in range(steps):
        for copy in outs[s]:
            copy.wait()
        chosen = dot(pick[...], grads_v[s].reshape(2 * tokens, CHUNK)).astype(BF16)
        for e in range(experts):
            part = dot(chosen[e * cap : (e + 1) * cap], bout_v[s, e])
            if s == 0:
                acc_out[e] = part
            else:
                acc_out[e] += part

    core = lax.rem(lax.axis_index("tensor"), 2)
    half = cap // 2
    at = 0
    for q in range(width // 128):
        for e in range(experts):
            for ref, which in ((keep, core), (send, 1 - core)):
                ref[at : at + half, :] = acc_in[
                    e, pl.ds(pl.multiple_of(which * half, 8), half), q * 128 : (q + 1) * 128
                ]
            at += half
    for x in range(width // 256):
        for e in range(experts):
            for ref, which in ((keep, core), (send, 1 - core)):
                ref[at : at + cap, :] = acc_out[
                    e, :, pl.ds(pl.multiple_of((2 * x + which) * 128, 128), 128)
                ]
            at += cap


def pair_kernel(kept, got, keep, send):
    inner = kept.shape[0] // 2
    outer = inner // 2
    x = lax.div(lax.axis_index("tensor"), 2)
    total = kept[:inner, :] + got[:inner, :]
    keep[:inner, :] = total
    send[:inner, :] = total.astype(BF16)
    mine = pl.ds(pl.multiple_of(inner + x * outer, 8), outer)
    keep[inner:, :] = kept[mine, :] + got[mine, :]
    other = pl.ds(pl.multiple_of(inner + (1 - x) * outer, 8), outer)
    send[inner:, :] = (kept[other, :] + got[other, :]).astype(BF16)


def payload_kernel(kept, got, label, *pays):
    dp = len(pays)
    outer = kept.shape[0] // 3
    slab = 2 * outer // dp
    d = lax.axis_index("dp")
    out = (kept[2 * outer :, :] + got[2 * outer :, :].astype(F32)).astype(BF16)
    for k, pay in enumerate(pays):
        rows = pl.ds(pl.multiple_of((d ^ k) * slab, 16), slab)
        pay[:slab, :] = (kept[rows, :] + got[rows, :].astype(F32)).astype(BF16)
        pay[slab : slab + outer, :] = out
        pay[slab + outer :, :] = label[...]


def block_kernel(dp, counts, *refs):
    own, sibling, result = refs[:dp], refs[dp : 2 * dp], refs[2 * dp]
    experts = result.shape[0]
    outer = (own[0].shape[0] - LABEL_ROWS) * 2 // 3
    slab = outer // 2
    cap = outer // experts
    half = cap // 2
    first = lax.rem(lax.axis_index("tensor"), 2) == 0
    for e in range(experts):
        total = None
        for k in range(dp):
            labels = own[k][slab + outer :, :].astype(F32)
            labels = jnp.concatenate(
                [labels[2 * e : 2 * e + 1], labels[2 * e + 1 : 2 * e + 2, : cap - 128]], axis=1
            )
            rows_out = own[k][slab + e * cap : slab + (e + 1) * cap, :].T
            mine = own[k][e * half : (e + 1) * half, :]
            theirs = sibling[k][e * half : (e + 1) * half, :]
            rows_in = jnp.concatenate(
                [jnp.where(first, mine, theirs), jnp.where(first, theirs, mine)], axis=0
            )
            masked = jnp.concatenate(
                [
                    jnp.where(labels == float(n + 1), rows_out, jnp.zeros_like(rows_out))
                    for n in range(dp)
                ],
                axis=0,
            )
            part = dot(masked, rows_in)
            total = part if total is None else total + part
        side = total.shape[0] // dp
        squares = total * total
        summed = squares[:side]
        for n in range(1, dp):
            summed = summed + squares[n * side : (n + 1) * side]
        result[e] = summed / counts[e].astype(F32)


def any_spec():
    return pl.BlockSpec(memory_space=pl.ANY)


def params():
    return pltpu.CompilerParams(vmem_limit_bytes=VMEM)


def fast(acts, grads, routes, example_ids, expert_counts, basis_in, basis_out):
    tokens, _, hidden = grads.shape
    experts, features, width = basis_in.shape
    cap = tokens // 2
    dp = lax.axis_size("dp")
    steps = hidden // CHUNK
    rows = 2 * experts * cap * width // 256
    f32_rows = jax.ShapeDtypeStruct((rows, 128), F32)
    copies = 2 + 1 + experts + 2 * steps
    keep, send, label = pl.pallas_call(
        rotate_kernel,
        out_shape=(f32_rows, f32_rows, jax.ShapeDtypeStruct((LABEL_ROWS, 128), BF16)),
        in_specs=[any_spec()] * 6,
        scratch_shapes=[
            pltpu.VMEM(acts.shape, BF16),
            pltpu.VMEM((steps, tokens, 2, CHUNK), BF16),
            pltpu.VMEM((2, tokens), jnp.int32),
            pltpu.VMEM((1, tokens), jnp.int32),
            pltpu.VMEM(basis_in.shape, BF16),
            pltpu.VMEM((steps, experts, CHUNK, width), BF16),
            pltpu.VMEM((experts, cap, width), F32),
            pltpu.VMEM((experts, cap, width), F32),
            pltpu.VMEM((experts * cap, 2 * tokens), BF16),
            pltpu.SemaphoreType.DMA((copies,)),
        ],
        compiler_params=params(),
        name="rotate",
    )(acts, grads, routes.T, example_ids.reshape(1, tokens), basis_in, basis_out)

    core = [(t, t ^ 1) for t in range(4)]
    across = [(t, t ^ 2) for t in range(4)]
    got = lax.ppermute(send, "tensor", core)
    shorter = rows * 3 // 4
    keep, send = pl.pallas_call(
        pair_kernel,
        out_shape=(
            jax.ShapeDtypeStruct((shorter, 128), F32),
            jax.ShapeDtypeStruct((shorter, 128), BF16),
        ),
        compiler_params=params(),
        name="pair",
    )(keep, got)
    got = lax.ppermute(send, "tensor", across)
    outer = shorter // 3
    pay_rows = 2 * outer // dp + outer + LABEL_ROWS
    pays = pl.pallas_call(
        payload_kernel,
        out_shape=[jax.ShapeDtypeStruct((pay_rows, 128), BF16)] * dp,
        compiler_params=params(),
        name="payload",
    )(keep, got, label)
    own = [pays[0]]
    for k in range(1, dp):
        own.append(lax.ppermute(pays[k], "dp", [(d, d ^ k) for d in range(dp)]))
    sibling = [lax.ppermute(pay, "tensor", core) for pay in own]
    return pl.pallas_call(
        functools.partial(block_kernel, dp),
        out_shape=jax.ShapeDtypeStruct((experts, 128, 128), F32),
        in_specs=[pl.BlockSpec(memory_space=pltpu.SMEM)]
        + [pl.BlockSpec(memory_space=pltpu.VMEM)] * (2 * dp),
        compiler_params=params(),
        name="blocks",
    )(expert_counts, *own, *sibling)


EX_DEV = 1


def compact(routes, expert, capacity):
    tok_count = routes.shape[0]
    second_hit = routes[:, 1] == expert
    routed = (routes[:, 0] == expert) | second_hit
    order = jnp.cumsum(routed.astype(jnp.int32)) - 1
    slots = jnp.arange(capacity, dtype=jnp.int32)
    match = routed[None, :] & (order[None, :] == slots[:, None])
    token_index = jnp.arange(tok_count, dtype=jnp.int32)
    positions = jnp.sum(jnp.where(match, token_index[None, :], 0), axis=1)
    filled = jnp.any(match, axis=1)
    return (positions, filled, second_hit[positions])


def general(acts, grads, routes, example_ids, expert_counts, basis_in, basis_out):
    capacity = acts.shape[0] // 2
    experts = basis_in.shape[0]
    parts_in, parts_out, label_rows = ([], [], [])
    for expert in range(experts):
        positions, filled, second = compact(routes, expert, capacity)
        chosen = grads[positions]
        grad_rows = jnp.where(second[:, None], chosen[:, 1, :], chosen[:, 0, :])
        parts_in.append(
            jnp.dot(acts[positions], basis_in[expert], preferred_element_type=jnp.float32)
        )
        parts_out.append(jnp.dot(grad_rows, basis_out[expert], preferred_element_type=jnp.float32))
        label_rows.append(jnp.where(filled, example_ids[positions], -1))
    part_in = jnp.stack(parts_in)
    part_out = jnp.stack(parts_out)
    labels = jnp.stack(label_rows)
    slice_width = basis_out.shape[2] // lax.axis_size("tensor")
    summed_in, summed_out = lax.psum((part_in, part_out), "tensor")
    rot_in = summed_in.astype(jnp.bfloat16)
    rot_out = lax.dynamic_slice_in_dim(
        summed_out.astype(jnp.bfloat16), lax.axis_index("tensor") * slice_width, slice_width, 2
    )
    owned_count = EX_DEV
    wanted = jnp.arange(lax.axis_size("dp") * owned_count, dtype=jnp.int32)
    onehot = (labels[:, :, None] == wanted[None, None, :]).astype(jnp.bfloat16)
    spread = onehot[:, :, :, None] * rot_out[:, :, None, :]
    owned_sums = lax.psum_scatter(
        jnp.einsum("ecnw,eca->newa", spread, rot_in, preferred_element_type=jnp.float32),
        "dp",
        scatter_dimension=0,
        tiled=True,
    )
    squared = jnp.sum(owned_sums * owned_sums, axis=0)
    totals = lax.psum_scatter(squared, "dp", scatter_dimension=2, tiled=True)
    return totals / expert_counts.astype(jnp.float32)[:, None, None]


def shards(*args):
    width = args[5].shape[2]
    fits = lax.axis_size("tensor") == 4 and lax.axis_size("dp") == 4 and width == 512
    return (fast if fits else general)(*args)


def solution(mesh):
    placed = (
        P(("group", "dp"), "tensor"),
        P(("group", "dp"), None, "tensor"),
        P(("group", "dp"), None),
        P(("group", "dp")),
        P("group"),
        P(None, "tensor", None),
        P(None, "tensor", None),
    )
    return jax.shard_map(
        shards, mesh=mesh, in_specs=placed, out_specs=P("group", "tensor", "dp"), check_vma=False
    )
```

```python
import functools

import jax
import jax.numpy as jnp
from jax import lax
from jax.experimental import pallas as pl
from jax.experimental.pallas import tpu as pltpu
from jax.sharding import PartitionSpec as P

F32 = jnp.float32
BF16 = jnp.bfloat16
CHUNK = 512
VMEM = 40 * 2**20
LABEL_ROWS = 16


def iota(shape, dim):
    return lax.broadcasted_iota(jnp.int32, shape, dim)


def dot(a, b):
    return jnp.dot(a, b, preferred_element_type=F32)


def fetcher(sems):
    count = iter(range(sems.shape[0]))

    def fetch(src, dst):
        copy = pltpu.make_async_copy(src, dst, sems.at[next(count)])
        copy.start()
        return copy

    return fetch


def rotate_in_kernel(
    acts, routes, ids, basis_in,
    keep, send, label, pick,
    acts_v, routes_v, ids_v, basis_v, acc, sems,
):
    tokens = acts.shape[0]
    experts, _, width = basis_in.shape
    cap = tokens // 2
    fetch = fetcher(sems)
    first = [fetch(routes, routes_v), fetch(ids, ids_v)]
    acts_in = fetch(acts, acts_v)
    bases = [fetch(basis_in.at[e], basis_v.at[e]) for e in range(experts)]
    for copy in first:
        copy.wait()
    hits = [
        jnp.max((routes_v[...] == e).astype(F32), axis=0, keepdims=True) for e in range(experts)
    ]
    rows = jnp.concatenate(hits + [jnp.zeros((8 - experts, tokens), F32)], axis=0).astype(BF16)
    upto = (iota((tokens, tokens), 0) <= iota((tokens, tokens), 1)).astype(BF16)
    order = dot(rows, upto)
    slots = iota((cap, tokens), 0).astype(F32) + 1.0
    pick_in = jnp.concatenate(
        [((order[e : e + 1] == slots) & (hits[e] > 0.5)).astype(BF16) for e in range(experts)],
        axis=0,
    )
    repeat = (iota((tokens, 2 * tokens), 0) == iota((tokens, 2 * tokens), 1) // 2).astype(BF16)
    wide = dot(
        jnp.concatenate(
            [order[:experts], routes_v[...].astype(F32), jnp.zeros((6 - experts, tokens), F32)],
            axis=0,
        ).astype(BF16),
        repeat,
    )
    odd = iota((1, 2 * tokens), 1) % 2 == 1
    routed_to = jnp.where(odd, wide[experts + 1 : experts + 2], wide[experts : experts + 1])
    slots = iota((cap, 2 * tokens), 0).astype(F32) + 1.0
    for e in range(experts):
        pick[e * cap : (e + 1) * cap, :] = (
            (wide[e : e + 1] == slots) & (routed_to == float(e))
        ).astype(BF16)
    numbers = jnp.broadcast_to(ids_v[...].astype(F32) + 1.0, (8, tokens)).astype(BF16)
    named = lax.dot_general(numbers, pick_in, (((1,), (1,)), ((), ())), preferred_element_type=F32)
    block = jnp.zeros((LABEL_ROWS, 128), F32)
    row = iota((LABEL_ROWS, 128), 0)
    half = cap // 2
    for at in range(2 * experts):
        mine = named[0:1, at * half : (at + 1) * half]
        mine = jnp.concatenate([mine, jnp.zeros((1, 128 - half), F32)], axis=1)
        block = jnp.where(row == at, mine, block)
    label[...] = block.astype(BF16)

    acts_in.wait()
    chosen = dot(pick_in, acts_v[...]).astype(BF16)
    for e in range(experts):
        bases[e].wait()
        acc[e] = dot(chosen[e * cap : (e + 1) * cap], basis_v[e])
    core = lax.rem(lax.axis_index("tensor"), 2)
    at = 0
    for q in range(width // 128):
        for e in range(experts):
            for ref, which in ((keep, core), (send, 1 - core)):
                ref[at : at + half, :] = acc[
                    e, pl.ds(pl.multiple_of(which * half, 8), half), q * 128 : (q + 1) * 128
                ]
            at += half


def rotate_out_kernel(grads, pick, basis_out, _, acc, grads_v, basis_v, sems):
    tokens, _, hidden = grads.shape
    experts, _, width = basis_out.shape
    cap = tokens // 2
    fetch = fetcher(sems)
    steps = hidden // CHUNK
    copies = []
    for s in range(steps):
        cols = pl.ds(s * CHUNK, CHUNK)
        copies.append(
            (fetch(grads.at[:, :, cols], grads_v.at[s]), fetch(basis_out.at[:, cols, :], basis_v.at[s]))
        )
    for s in range(steps):
        for copy in copies[s]:
            copy.wait()
        chosen = dot(pick[...], grads_v[s].reshape(2 * tokens, CHUNK)).astype(BF16)
        for e in range(experts):
            part = dot(chosen[e * cap : (e + 1) * cap], basis_v[s, e])
            if s == 0:
                acc[e] = part
            else:
                acc[e] += part


def split_out_kernel(acc, _, keep, send):
    experts, cap, width = acc.shape
    core = lax.rem(lax.axis_index("tensor"), 2)
    at = 0
    for x in range(width // 256):
        for e in range(experts):
            for ref, which in ((keep, core), (send, 1 - core)):
                ref[at : at + cap, :] = acc[
                    e, :, pl.ds(pl.multiple_of((2 * x + which) * 128, 128), 128)
                ]
            at += cap


def pair_in_kernel(kept, got, label, *pays):
    slab = kept.shape[0] // len(pays)
    d = lax.axis_index("dp")
    for k, pay in enumerate(pays):
        rows = pl.ds(pl.multiple_of((d ^ k) * slab, 16), slab)
        pay[:slab, :] = (kept[rows, :] + got[rows, :]).astype(BF16)
        pay[slab:, :] = label[...]


def pair_out_kernel(kept, got, keep, send):
    outer = keep.shape[0]
    x = lax.div(lax.axis_index("tensor"), 2)
    mine = pl.ds(pl.multiple_of(x * outer, 16), outer)
    keep[...] = kept[mine, :] + got[mine, :]
    other = pl.ds(pl.multiple_of((1 - x) * outer, 16), outer)
    send[...] = (kept[other, :] + got[other, :]).astype(BF16)


def round_kernel(kept, got, out):
    out[...] = (kept[...] + got[...].astype(F32)).astype(BF16)


def stack_kernel(*refs):
    *pieces, out = refs
    slab = pieces[0].shape[0] - LABEL_ROWS
    for k, piece in enumerate(pieces):
        out[k * slab : (k + 1) * slab, :] = piece[:slab, :]


def half_blocks(dp, e, which, rows, far, outs, pieces):
    half = rows.shape[0] // (2 * dp)
    slab = pieces[0].shape[0] - LABEL_ROWS
    rows_in, rows_out, labels = [], [], []
    for k in range(dp):
        at = pl.ds((2 * k + e) * half, half)
        rows_in.append((rows[at, :].astype(F32) + far[at, :].astype(F32)).astype(BF16))
        at = pl.ds(pl.multiple_of((2 * e + which) * half, 16), half)
        rows_out.append(outs[k][at, :])
        label = pieces[k][slab:, :].astype(F32)[2 * e : 2 * e + 2, :half]
        labels.append(jnp.where(which == 0, label[0:1], label[1:2]))
    rows_in = jnp.concatenate(rows_in, axis=0)
    rows_out = jnp.concatenate(rows_out, axis=0).T
    labels = jnp.concatenate(labels, axis=1)
    masked = [
        jnp.where(labels == float(n + 1), rows_out, jnp.zeros_like(rows_out)) for n in range(dp)
    ]
    return dot(jnp.concatenate(masked, axis=0), rows_in)


def first_blocks_kernel(dp, rows, far, *refs):
    outs, pieces, total = refs[:dp], refs[dp : 2 * dp], refs[2 * dp]
    core = lax.rem(lax.axis_index("tensor"), 2)
    for e in range(total.shape[0]):
        total[e] = half_blocks(dp, e, core, rows, far, outs, pieces)


def blocks_kernel(dp, counts, first, rows, far, *refs):
    outs, pieces, result = refs[:dp], refs[dp : 2 * dp], refs[2 * dp]
    core = lax.rem(lax.axis_index("tensor"), 2)
    for e in range(result.shape[0]):
        total = first[e] + half_blocks(dp, e, 1 - core, rows, far, outs, pieces)
        side = total.shape[0] // dp
        squares = total * total
        summed = squares[:side]
        for n in range(1, dp):
            summed = summed + squares[n * side : (n + 1) * side]
        result[e] = summed / counts[e].astype(F32)


def call(kernel, name, out_shape, specs=None, scratch=()):
    vmem = pl.BlockSpec(memory_space=pltpu.VMEM)
    return lambda *args: pl.pallas_call(
        kernel,
        out_shape=out_shape,
        in_specs=specs or [vmem] * len(args),
        scratch_shapes=scratch,
        compiler_params=pltpu.CompilerParams(vmem_limit_bytes=VMEM),
        cost_estimate=pl.CostEstimate(flops=1, bytes_accessed=1, transcendentals=0),
        name=name,
    )(*args)


def fast(acts, grads, routes, example_ids, expert_counts, basis_in, basis_out):
    tokens, _, hidden = grads.shape
    experts, features, width = basis_in.shape
    cap = tokens // 2
    dp = lax.axis_size("dp")
    steps = hidden // CHUNK
    wide = experts * cap
    half = wide * width // 256
    slab = half // dp
    hbm = pl.BlockSpec(memory_space=pltpu.HBM)
    vmem = pl.BlockSpec(memory_space=pltpu.VMEM)

    def pin(x):
        return pltpu.with_memory_space_constraint(x, pltpu.HBM)

    def rows(count, dtype):
        return jax.ShapeDtypeStruct((count, 128), dtype)

    core = [(t, t ^ 1) for t in range(4)]
    across = [(t, t ^ 2) for t in range(4)]
    others = [[(d, d ^ k) for d in range(dp)] for k in range(dp)]

    keep, send, label, pick = call(
        rotate_in_kernel,
        "rotate_in",
        (rows(half, F32), rows(half, F32), rows(LABEL_ROWS, BF16),
         jax.ShapeDtypeStruct((wide, 2 * tokens), BF16)),
        [hbm] * 4,
        [
            pltpu.VMEM(acts.shape, BF16),
            pltpu.VMEM((2, tokens), jnp.int32),
            pltpu.VMEM((1, tokens), jnp.int32),
            pltpu.VMEM(basis_in.shape, BF16),
            pltpu.VMEM((experts, cap, width), F32),
            pltpu.SemaphoreType.DMA((3 + experts,)),
        ],
    )(pin(acts), routes.T, example_ids.reshape(1, tokens), pin(basis_in))
    got = lax.ppermute(send, "tensor", core)
    pieces = call(pair_in_kernel, "pair_in", [rows(slab + LABEL_ROWS, BF16)] * dp)(keep, got, label)
    arrived = [pieces[0]] + [lax.ppermute(pieces[k], "dp", others[k]) for k in range(1, dp)]

    acc = call(
        rotate_out_kernel,
        "rotate_out",
        jax.ShapeDtypeStruct((experts, cap, width), F32),
        [hbm, vmem, hbm, vmem],
        [
            pltpu.VMEM((steps, tokens, 2, CHUNK), BF16),
            pltpu.VMEM((steps, experts, CHUNK, width), BF16),
            pltpu.SemaphoreType.DMA((2 * steps,)),
        ],
    )(pin(grads), pick, pin(basis_out), pieces[0])
    mine = call(stack_kernel, "stack_in", rows(half, BF16))(*arrived)
    keep, send = call(split_out_kernel, "split_out", (rows(half, F32), rows(half, F32)))(acc, mine)
    got = lax.ppermute(send, "tensor", core)
    keep, send = call(pair_out_kernel, "pair_out", (rows(half // 2, F32), rows(half // 2, BF16)))(
        keep, got
    )
    got = lax.ppermute(send, "tensor", across)
    out = call(round_kernel, "round_out", rows(half // 2, BF16))(keep, got)
    outs = [out] + [lax.ppermute(out, "dp", others[k]) for k in range(1, dp)]

    far = lax.ppermute(mine, "tensor", across)
    first = call(
        functools.partial(first_blocks_kernel, dp),
        "first_blocks",
        jax.ShapeDtypeStruct((experts, dp * 128, 128), F32),
    )(mine, far, *outs, *arrived)
    other = lax.ppermute(mine, "tensor", core)
    other_far = lax.ppermute(far, "tensor", core)
    return call(
        functools.partial(blocks_kernel, dp),
        "blocks",
        jax.ShapeDtypeStruct((experts, 128, 128), F32),
        [pl.BlockSpec(memory_space=pltpu.SMEM)] + [vmem] * (2 * dp + 3),
    )(expert_counts, first, other, other_far, *outs, *arrived)


EX_DEV = 1


def compact(routes, expert, capacity):
    tok_count = routes.shape[0]
    second_hit = routes[:, 1] == expert
    routed = (routes[:, 0] == expert) | second_hit
    order = jnp.cumsum(routed.astype(jnp.int32)) - 1
    slots = jnp.arange(capacity, dtype=jnp.int32)
    match = routed[None, :] & (order[None, :] == slots[:, None])
    token_index = jnp.arange(tok_count, dtype=jnp.int32)
    positions = jnp.sum(jnp.where(match, token_index[None, :], 0), axis=1)
    filled = jnp.any(match, axis=1)
    return (positions, filled, second_hit[positions])


def general(acts, grads, routes, example_ids, expert_counts, basis_in, basis_out):
    capacity = acts.shape[0] // 2
    experts = basis_in.shape[0]
    parts_in, parts_out, label_rows = ([], [], [])
    for expert in range(experts):
        positions, filled, second = compact(routes, expert, capacity)
        chosen = grads[positions]
        grad_rows = jnp.where(second[:, None], chosen[:, 1, :], chosen[:, 0, :])
        parts_in.append(
            jnp.dot(acts[positions], basis_in[expert], preferred_element_type=jnp.float32)
        )
        parts_out.append(jnp.dot(grad_rows, basis_out[expert], preferred_element_type=jnp.float32))
        label_rows.append(jnp.where(filled, example_ids[positions], -1))
    part_in = jnp.stack(parts_in)
    part_out = jnp.stack(parts_out)
    labels = jnp.stack(label_rows)
    slice_width = basis_out.shape[2] // lax.axis_size("tensor")
    summed_in, summed_out = lax.psum((part_in, part_out), "tensor")
    rot_in = summed_in.astype(jnp.bfloat16)
    rot_out = lax.dynamic_slice_in_dim(
        summed_out.astype(jnp.bfloat16), lax.axis_index("tensor") * slice_width, slice_width, 2
    )
    owned_count = EX_DEV
    wanted = jnp.arange(lax.axis_size("dp") * owned_count, dtype=jnp.int32)
    onehot = (labels[:, :, None] == wanted[None, None, :]).astype(jnp.bfloat16)
    spread = onehot[:, :, :, None] * rot_out[:, :, None, :]
    owned_sums = lax.psum_scatter(
        jnp.einsum("ecnw,eca->newa", spread, rot_in, preferred_element_type=jnp.float32),
        "dp",
        scatter_dimension=0,
        tiled=True,
    )
    squared = jnp.sum(owned_sums * owned_sums, axis=0)
    totals = lax.psum_scatter(squared, "dp", scatter_dimension=2, tiled=True)
    return totals / expert_counts.astype(jnp.float32)[:, None, None]


def shards(*args):
    width = args[5].shape[2]
    fits = lax.axis_size("tensor") == 4 and lax.axis_size("dp") == 4 and width == 512
    return (fast if fits else general)(*args)


def solution(mesh):
    placed = (
        P(("group", "dp"), "tensor"),
        P(("group", "dp"), None, "tensor"),
        P(("group", "dp"), None),
        P(("group", "dp")),
        P("group"),
        P(None, "tensor", None),
        P(None, "tensor", None),
    )
    return jax.shard_map(
        shards, mesh=mesh, in_specs=placed, out_specs=P("group", "tensor", "dp"), check_vma=False
    )
```

```python
import functools

import jax
import jax.numpy as jnp
from jax import lax
from jax.experimental import pallas as pl
from jax.experimental.pallas import tpu as pltpu
from jax.sharding import PartitionSpec as P

F32 = jnp.float32
BF16 = jnp.bfloat16
CHUNK = 512
VMEM = 20 * 2**20
FAR_FIRST = (2, 3, 1)
LABEL_ROWS = 16


def iota(shape, dim):
    return lax.broadcasted_iota(jnp.int32, shape, dim)


def dot(a, b):
    return jnp.dot(a, b, preferred_element_type=F32)


def fetcher(sems):
    count = iter(range(sems.shape[0]))

    def fetch(src, dst):
        copy = pltpu.make_async_copy(src, dst, sems.at[next(count)])
        copy.start()
        return copy

    return fetch


def rotate_in_kernel(
    acts, routes, ids, basis_in,
    acc, label, pick,
    acts_v, routes_v, ids_v, basis_v, sems,
):
    tokens = acts.shape[0]
    experts, _, width = basis_in.shape
    cap = tokens // 2
    fetch = fetcher(sems)
    first = [fetch(routes, routes_v), fetch(ids, ids_v)]
    acts_in = fetch(acts, acts_v)
    bases = [fetch(basis_in.at[e], basis_v.at[e]) for e in range(experts)]
    for copy in first:
        copy.wait()
    hits = [
        jnp.max((routes_v[...] == e).astype(F32), axis=0, keepdims=True) for e in range(experts)
    ]
    rows = jnp.concatenate(hits + [jnp.zeros((8 - experts, tokens), F32)], axis=0).astype(BF16)
    upto = (iota((tokens, tokens), 0) <= iota((tokens, tokens), 1)).astype(BF16)
    order = dot(rows, upto)
    slots = iota((cap, tokens), 0).astype(F32) + 1.0
    pick_in = jnp.concatenate(
        [((order[e : e + 1] == slots) & (hits[e] > 0.5)).astype(BF16) for e in range(experts)],
        axis=0,
    )
    repeat = (iota((tokens, 2 * tokens), 0) == iota((tokens, 2 * tokens), 1) // 2).astype(BF16)
    wide = dot(
        jnp.concatenate(
            [order[:experts], routes_v[...].astype(F32), jnp.zeros((6 - experts, tokens), F32)],
            axis=0,
        ).astype(BF16),
        repeat,
    )
    odd = iota((1, 2 * tokens), 1) % 2 == 1
    routed_to = jnp.where(odd, wide[experts + 1 : experts + 2], wide[experts : experts + 1])
    slots = iota((cap, 2 * tokens), 0).astype(F32) + 1.0
    for e in range(experts):
        pick[e * cap : (e + 1) * cap, :] = (
            (wide[e : e + 1] == slots) & (routed_to == float(e))
        ).astype(BF16)
    numbers = jnp.broadcast_to(ids_v[...].reshape(1, tokens).astype(F32) + 1.0, (8, tokens)).astype(BF16)
    named = lax.dot_general(numbers, pick_in, (((1,), (1,)), ((), ())), preferred_element_type=F32)
    block = jnp.zeros((LABEL_ROWS, 128), F32)
    row = iota((LABEL_ROWS, 128), 0)
    half = cap // 2
    for at in range(2 * experts):
        mine = named[0:1, at * half : (at + 1) * half]
        mine = jnp.concatenate([mine, jnp.zeros((1, 128 - half), F32)], axis=1)
        block = jnp.where(row == at, mine, block)
    label[...] = block.astype(BF16)

    acts_in.wait()
    chosen = dot(pick_in, acts_v[...]).astype(BF16)
    for e in range(experts):
        bases[e].wait()
        acc[e] = dot(chosen[e * cap : (e + 1) * cap], basis_v[e])


def split_in_kernel(acc, keep, send):
    experts, cap, width = acc.shape
    core = lax.rem(lax.axis_index("tensor"), 2)
    half = cap // 2
    at = 0
    for q in range(width // 128):
        for e in range(experts):
            for ref, which in ((keep, core), (send, 1 - core)):
                ref[at : at + half, :] = acc[
                    e, pl.ds(pl.multiple_of(which * half, 8), half), q * 128 : (q + 1) * 128
                ]
            at += half


def rotate_out_kernel(grads, pick, basis_out, _, acc):
    tokens, _, hidden = grads.shape
    experts = basis_out.shape[0]
    cap = tokens // 2
    for s in range(hidden // CHUNK):
        cols = pl.ds(s * CHUNK, CHUNK)
        chosen = dot(pick[...], grads[:, :, cols].reshape(2 * tokens, CHUNK)).astype(BF16)
        for e in range(experts):
            part = dot(chosen[e * cap : (e + 1) * cap], basis_out[e, cols, :])
            if s == 0:
                acc[e] = part
            else:
                acc[e] += part


def split_out_kernel(acc, *refs):
    *_, keep, send = refs
    experts, cap, width = acc.shape
    core = lax.rem(lax.axis_index("tensor"), 2)
    at = 0
    for x in range(width // 256):
        for e in range(experts):
            for ref, which in ((keep, core), (send, 1 - core)):
                ref[at : at + cap, :] = acc[
                    e, :, pl.ds(pl.multiple_of((2 * x + which) * 128, 128), 128)
                ]
            at += cap


def pair_in_kernel(kept, got, *pays):
    slab = kept.shape[0] // len(pays)
    d = lax.axis_index("dp")
    for k, pay in enumerate(pays):
        rows = pl.ds(pl.multiple_of((d ^ k) * slab, 16), slab)
        pay[...] = (kept[rows, :] + got[rows, :]).astype(BF16)


def pair_out_kernel(kept, got, keep, send):
    outer = keep.shape[0]
    x = lax.div(lax.axis_index("tensor"), 2)
    mine = pl.ds(pl.multiple_of(x * outer, 16), outer)
    keep[...] = kept[mine, :] + got[mine, :]
    other = pl.ds(pl.multiple_of((1 - x) * outer, 16), outer)
    send[...] = (kept[other, :] + got[other, :]).astype(BF16)


def round_kernel(kept, got, label, out):
    outer = kept.shape[0]
    out[:outer, :] = (kept[...] + got[...].astype(F32)).astype(BF16)
    out[outer:, :] = label[...]


def stack_kernel(experts, *refs):
    pieces, outs = refs[: -1 - experts], refs[-experts:]
    half = pieces[0].shape[0] // experts
    for k, piece in enumerate(pieces):
        for e, out in enumerate(outs):
            out[k * half : (k + 1) * half, :] = piece[e * half : (e + 1) * half, :]


def half_blocks(e, experts, which, near, far, outs):
    dp = len(outs)
    half = near.shape[0] // dp
    rows_out, labels = [], []
    for ref in outs:
        rows_out.append(ref[pl.ds(pl.multiple_of((2 * e + which) * half, 16), half), :])
        label = ref[2 * experts * half :, :].astype(F32)[2 * e : 2 * e + 2, :half]
        labels.append(jnp.where(which == 0, label[0:1], label[1:2]))
    rows_in = (near[...].astype(F32) + far[...].astype(F32)).astype(BF16)
    rows_out = jnp.concatenate(rows_out, axis=0).T
    labels = jnp.concatenate(labels, axis=1)
    masked = [
        jnp.where(labels == float(n + 1), rows_out, jnp.zeros_like(rows_out)) for n in range(dp)
    ]
    return dot(jnp.concatenate(masked, axis=0), rows_in)


def first_blocks_kernel(experts, dp, counts, *refs):
    near, far, outs = refs[:experts], refs[experts : 2 * experts], refs[2 * experts : -2]
    total, divisor = refs[-2:]
    core = lax.rem(lax.axis_index("tensor"), 2)
    for e in range(experts):
        divisor[e] = jnp.full(divisor.shape[1:], counts[e].astype(F32), F32)
        total[e] = half_blocks(e, experts, core, near[e], far[e], outs)


def blocks_kernel(experts, dp, first, divisor, *refs):
    near, far, outs = refs[:experts], refs[experts : 2 * experts], refs[2 * experts : -3]
    result, final, sems = refs[-3:]
    core = lax.rem(lax.axis_index("tensor"), 2)
    copies = []
    for e in range(experts):
        total = first[e] + half_blocks(e, experts, 1 - core, near[e], far[e], outs)
        side = total.shape[0] // dp
        squares = total * total
        summed = squares[:side]
        for n in range(1, dp):
            summed = summed + squares[n * side : (n + 1) * side]
        final[e] = summed / divisor[e][:1]
        copies.append(pltpu.make_async_copy(final.at[e], result.at[e], sems.at[e]))
        copies[e].start()
    for copy in copies:
        copy.wait()


def call(kernel, name, out_shape, specs=None, scratch=(), out_specs=None, flops=1):
    vmem = pl.BlockSpec(memory_space=pltpu.VMEM)
    given = {} if out_specs is None else {"out_specs": out_specs}
    return lambda *args: pl.pallas_call(
        kernel,
        out_shape=out_shape,
        in_specs=specs or [vmem] * len(args),
        scratch_shapes=scratch,
        compiler_params=pltpu.CompilerParams(vmem_limit_bytes=VMEM),
        cost_estimate=pl.CostEstimate(flops=flops, bytes_accessed=1, transcendentals=0),
        name=name,
        **given,
    )(*args)


def fast(acts, grads, routes, example_ids, expert_counts, basis_in, basis_out):
    tokens = acts.shape[0]
    experts, features, width = basis_in.shape
    cap = tokens // 2
    dp = lax.axis_size("dp")
    wide = experts * cap
    half = wide * width // 256
    hbm = pl.BlockSpec(memory_space=pltpu.HBM)
    vmem = pl.BlockSpec(memory_space=pltpu.VMEM)
    smem = pl.BlockSpec(memory_space=pltpu.SMEM)

    def pin(x):
        return pltpu.with_memory_space_constraint(x, pltpu.HBM)

    def rows(count, dtype):
        return jax.ShapeDtypeStruct((count, 128), dtype)

    core = [(t, t ^ 1) for t in range(4)]
    across = [(t, t ^ 2) for t in range(4)]

    def spread(pays):
        got = {k: lax.ppermute(pays[k], "dp", [(d, d ^ k) for d in range(dp)]) for k in FAR_FIRST}
        return [pays[0]] + [got[k] for k in range(1, dp)]

    partial = jax.ShapeDtypeStruct((experts, cap, width), F32)
    acc, label, pick = call(
        rotate_in_kernel,
        "rotate_in",
        (partial, rows(LABEL_ROWS, BF16), jax.ShapeDtypeStruct((wide, 2 * tokens), BF16)),
        [hbm] * 4,
        [
            pltpu.VMEM(acts.shape, BF16),
            pltpu.VMEM((2, tokens), jnp.int32),
            pltpu.VMEM((tokens,), jnp.int32),
            pltpu.VMEM(basis_in.shape, BF16),
            pltpu.SemaphoreType.DMA((3 + experts,)),
        ],
    )(pin(acts), pin(routes.T), pin(example_ids), pin(basis_in))
    keep, send = call(
        split_in_kernel, "split_in", (rows(half, F32), rows(half, F32)), flops=8 * 10**9
    )(acc)
    got = lax.ppermute(send, "tensor", core)
    pieces = call(pair_in_kernel, "pair_in", [rows(half // dp, BF16)] * dp)(keep, got)
    arrived = spread(pieces)

    acc = call(rotate_out_kernel, "rotate_out", partial)(grads, pick, basis_out, pieces[0])
    keep, send = call(split_out_kernel, "split_out", (rows(half, F32), rows(half, F32)))(
        acc, *arrived[1:]
    )
    got = lax.ppermute(send, "tensor", core)
    keep, send = call(pair_out_kernel, "pair_out", (rows(half // 2, F32), rows(half // 2, BF16)))(
        keep, got
    )
    got = lax.ppermute(send, "tensor", across)
    out = call(round_kernel, "round_out", rows(half // 2 + LABEL_ROWS, BF16))(keep, got, label)

    near = call(
        functools.partial(stack_kernel, experts), "stack_in", [rows(half // experts, BF16)] * experts
    )(*arrived, out)
    far = [lax.ppermute(x, "tensor", across) for x in near]
    outs = spread([out] * dp)
    first, divisor = call(
        functools.partial(first_blocks_kernel, experts, dp),
        "first_blocks",
        (
            jax.ShapeDtypeStruct((experts, dp * 128, 128), F32),
            jax.ShapeDtypeStruct((experts, 8, 128), F32),
        ),
        [smem] + [vmem] * (2 * experts + dp),
    )(expert_counts, *near, *far, *outs)
    near = [lax.ppermute(x, "tensor", core) for x in near]
    far = [lax.ppermute(x, "tensor", core) for x in far]
    result = jax.ShapeDtypeStruct((experts, 128, 128), F32)
    return call(
        functools.partial(blocks_kernel, experts, dp),
        "blocks",
        result,
        scratch=[pltpu.VMEM(result.shape, F32), pltpu.SemaphoreType.DMA((experts,))],
        out_specs=hbm,
    )(first, divisor, *near, *far, *outs)


EX_DEV = 1


def compact(routes, expert, capacity):
    tok_count = routes.shape[0]
    second_hit = routes[:, 1] == expert
    routed = (routes[:, 0] == expert) | second_hit
    order = jnp.cumsum(routed.astype(jnp.int32)) - 1
    slots = jnp.arange(capacity, dtype=jnp.int32)
    match = routed[None, :] & (order[None, :] == slots[:, None])
    token_index = jnp.arange(tok_count, dtype=jnp.int32)
    positions = jnp.sum(jnp.where(match, token_index[None, :], 0), axis=1)
    filled = jnp.any(match, axis=1)
    return (positions, filled, second_hit[positions])


def general(acts, grads, routes, example_ids, expert_counts, basis_in, basis_out):
    capacity = acts.shape[0] // 2
    experts = basis_in.shape[0]
    parts_in, parts_out, label_rows = ([], [], [])
    for expert in range(experts):
        positions, filled, second = compact(routes, expert, capacity)
        chosen = grads[positions]
        grad_rows = jnp.where(second[:, None], chosen[:, 1, :], chosen[:, 0, :])
        parts_in.append(
            jnp.dot(acts[positions], basis_in[expert], preferred_element_type=jnp.float32)
        )
        parts_out.append(jnp.dot(grad_rows, basis_out[expert], preferred_element_type=jnp.float32))
        label_rows.append(jnp.where(filled, example_ids[positions], -1))
    part_in = jnp.stack(parts_in)
    part_out = jnp.stack(parts_out)
    labels = jnp.stack(label_rows)
    slice_width = basis_out.shape[2] // lax.axis_size("tensor")
    summed_in, summed_out = lax.psum((part_in, part_out), "tensor")
    rot_in = summed_in.astype(jnp.bfloat16)
    rot_out = lax.dynamic_slice_in_dim(
        summed_out.astype(jnp.bfloat16), lax.axis_index("tensor") * slice_width, slice_width, 2
    )
    owned_count = EX_DEV
    wanted = jnp.arange(lax.axis_size("dp") * owned_count, dtype=jnp.int32)
    onehot = (labels[:, :, None] == wanted[None, None, :]).astype(jnp.bfloat16)
    spread = onehot[:, :, :, None] * rot_out[:, :, None, :]
    owned_sums = lax.psum_scatter(
        jnp.einsum("ecnw,eca->newa", spread, rot_in, preferred_element_type=jnp.float32),
        "dp",
        scatter_dimension=0,
        tiled=True,
    )
    squared = jnp.sum(owned_sums * owned_sums, axis=0)
    totals = lax.psum_scatter(squared, "dp", scatter_dimension=2, tiled=True)
    return totals / expert_counts.astype(jnp.float32)[:, None, None]


def shards(*args):
    width = args[5].shape[2]
    fits = lax.axis_size("tensor") == 4 and lax.axis_size("dp") == 4 and width == 512
    return (fast if fits else general)(*args)


def solution(mesh):
    placed = (
        P(("group", "dp"), "tensor"),
        P(("group", "dp"), None, "tensor"),
        P(("group", "dp"), None),
        P(("group", "dp")),
        P("group"),
        P(None, "tensor", None),
        P(None, "tensor", None),
    )
    return jax.shard_map(
        shards, mesh=mesh, in_specs=placed, out_specs=P("group", "tensor", "dp"), check_vma=False
    )
```

```python
import functools

import jax
import jax.numpy as jnp
from jax import lax
from jax.experimental import pallas as pl
from jax.experimental.pallas import tpu as pltpu
from jax.sharding import PartitionSpec as P

F32 = jnp.float32
BF16 = jnp.bfloat16
CHUNK = 512
VMEM = 20 * 2**20
FAR_FIRST = (2, 3, 1)
LABEL_ROWS = 16


def iota(shape, dim):
    return lax.broadcasted_iota(jnp.int32, shape, dim)


def dot(a, b):
    return jnp.dot(a, b, preferred_element_type=F32)


def fetcher(sems):
    count = iter(range(sems.shape[0]))

    def fetch(src, dst):
        copy = pltpu.make_async_copy(src, dst, sems.at[next(count)])
        copy.start()
        return copy

    return fetch


def rotate_in_kernel(
    acts, routes, ids, basis_in,
    acc, label, pick,
    acts_v, routes_v, ids_v, basis_v, sems,
):
    tokens = acts.shape[0]
    experts, _, width = basis_in.shape
    cap = tokens // 2
    fetch = fetcher(sems)
    first = [fetch(routes, routes_v), fetch(ids, ids_v)]
    acts_in = fetch(acts, acts_v)
    bases = [fetch(basis_in.at[e], basis_v.at[e]) for e in range(experts)]
    for copy in first:
        copy.wait()
    hits = [
        jnp.max((routes_v[...] == e).astype(F32), axis=0, keepdims=True) for e in range(experts)
    ]
    rows = jnp.concatenate(hits + [jnp.zeros((8 - experts, tokens), F32)], axis=0).astype(BF16)
    upto = (iota((tokens, tokens), 0) <= iota((tokens, tokens), 1)).astype(BF16)
    order = dot(rows, upto)
    slots = iota((cap, tokens), 0).astype(F32) + 1.0
    pick_in = jnp.concatenate(
        [((order[e : e + 1] == slots) & (hits[e] > 0.5)).astype(BF16) for e in range(experts)],
        axis=0,
    )
    repeat = (iota((tokens, 2 * tokens), 0) == iota((tokens, 2 * tokens), 1) // 2).astype(BF16)
    wide = dot(
        jnp.concatenate(
            [order[:experts], routes_v[...].astype(F32), jnp.zeros((6 - experts, tokens), F32)],
            axis=0,
        ).astype(BF16),
        repeat,
    )
    odd = iota((1, 2 * tokens), 1) % 2 == 1
    routed_to = jnp.where(odd, wide[experts + 1 : experts + 2], wide[experts : experts + 1])
    slots = iota((cap, 2 * tokens), 0).astype(F32) + 1.0
    for e in range(experts):
        pick[e * cap : (e + 1) * cap, :] = (
            (wide[e : e + 1] == slots) & (routed_to == float(e))
        ).astype(BF16)
    numbers = jnp.broadcast_to(ids_v[...].reshape(1, tokens).astype(F32) + 1.0, (8, tokens)).astype(BF16)
    named = lax.dot_general(numbers, pick_in, (((1,), (1,)), ((), ())), preferred_element_type=F32)
    block = jnp.zeros((LABEL_ROWS, 128), F32)
    row = iota((LABEL_ROWS, 128), 0)
    half = cap // 2
    for at in range(2 * experts):
        mine = named[0:1, at * half : (at + 1) * half]
        mine = jnp.concatenate([mine, jnp.zeros((1, 128 - half), F32)], axis=1)
        block = jnp.where(row == at, mine, block)
    label[...] = block.astype(BF16)

    acts_in.wait()
    chosen = dot(pick_in, acts_v[...]).astype(BF16)
    for e in range(experts):
        bases[e].wait()
        acc[e] = dot(chosen[e * cap : (e + 1) * cap], basis_v[e])


def split_in_kernel(acc, keep, send):
    experts, cap, width = acc.shape
    core = lax.rem(lax.axis_index("tensor"), 2)
    half = cap // 2
    at = 0
    for q in range(width // 128):
        for e in range(experts):
            for ref, which in ((keep, core), (send, 1 - core)):
                ref[at : at + half, :] = acc[
                    e, pl.ds(pl.multiple_of(which * half, 8), half), q * 128 : (q + 1) * 128
                ]
            at += half


def rotate_first_kernel(grads, pick, basis_out, acc, rest):
    tokens, _, hidden = grads.shape
    cap = tokens // 2
    for s in range(hidden // CHUNK):
        cols = pl.ds(s * CHUNK, CHUNK)
        chosen = dot(pick[...], grads[:, :, cols].reshape(2 * tokens, CHUNK)).astype(BF16)
        rest[:, cols] = chosen[cap:]
        part = dot(chosen[:cap], basis_out[0, cols, :])
        if s == 0:
            acc[...] = part
        else:
            acc[...] += part


def rotate_rest_kernel(e, rest, basis_out, acc):
    cap = acc.shape[0]
    acc[...] = dot(rest[(e - 1) * cap : e * cap, :], basis_out[e])


def split_out_kernel(acc, keep, send):
    cap, width = acc.shape
    core = lax.rem(lax.axis_index("tensor"), 2)
    for x in range(width // 256):
        for ref, which in ((keep, core), (send, 1 - core)):
            ref[x * cap : (x + 1) * cap, :] = acc[
                :, pl.ds(pl.multiple_of((2 * x + which) * 128, 128), 128)
            ]


def pair_in_kernel(kept, got, *pays):
    slab = kept.shape[0] // len(pays)
    d = lax.axis_index("dp")
    for k, pay in enumerate(pays):
        rows = pl.ds(pl.multiple_of((d ^ k) * slab, 16), slab)
        pay[...] = (kept[rows, :] + got[rows, :]).astype(BF16)


def pair_out_kernel(kept, got, keep, send):
    outer = keep.shape[0]
    x = lax.div(lax.axis_index("tensor"), 2)
    mine = pl.ds(pl.multiple_of(x * outer, 16), outer)
    keep[...] = kept[mine, :] + got[mine, :]
    other = pl.ds(pl.multiple_of((1 - x) * outer, 16), outer)
    send[...] = (kept[other, :] + got[other, :]).astype(BF16)


def round_kernel(kept, got, label, out):
    outer = kept.shape[0]
    out[:outer, :] = (kept[...] + got[...].astype(F32)).astype(BF16)
    out[outer:, :] = label[...]


def stack_kernel(*refs):
    *pieces, out = refs
    slab = pieces[0].shape[0]
    for k, piece in enumerate(pieces):
        out[k * slab : (k + 1) * slab, :] = piece[...]


def sum_kernel(near, far, out):
    out[...] = (near[...].astype(F32) + far[...].astype(F32)).astype(BF16)


def squared_blocks(e, experts, mine, other, outs):
    dp = len(outs)
    half = mine.shape[0] // (dp * experts)
    core = lax.rem(lax.axis_index("tensor"), 2)
    rows_in, rows_out, labels = [], [], []
    for which, ref_in in ((core, mine), (1 - core, other)):
        for k, ref in enumerate(outs):
            at = (k * experts + e) * half
            rows_in.append(ref_in[at : at + half, :])
            rows_out.append(ref[pl.ds(pl.multiple_of(which * half, 16), half), :])
            label = ref[2 * half :, :].astype(F32)[2 * e : 2 * e + 2, :half]
            labels.append(jnp.where(which == 0, label[0:1], label[1:2]))
    rows_in = jnp.concatenate(rows_in, axis=0)
    rows_out = jnp.concatenate(rows_out, axis=0).T
    labels = jnp.concatenate(labels, axis=1)
    masked = [
        jnp.where(labels == float(n + 1), rows_out, jnp.zeros_like(rows_out)) for n in range(dp)
    ]
    blocks = dot(jnp.concatenate(masked, axis=0), rows_in)
    squares = blocks * blocks
    side = squares.shape[0] // dp
    summed = squares[:side]
    for n in range(1, dp):
        summed = summed + squares[n * side : (n + 1) * side]
    return summed


def blocks_kernel(e, counts, *refs):
    *given, result, divisor = refs
    experts = counts.shape[0]
    result[...] = squared_blocks(e, experts, *given[:2], given[2:]) / counts[e].astype(F32)
    divisor[...] = jnp.full(divisor.shape, counts[experts - 1].astype(F32), F32)


def last_blocks_kernel(experts, divisor, *refs):
    earlier, given = refs[: experts - 1], refs[experts - 1 : -3]
    result, final, sems = refs[-3:]
    copies = [pltpu.make_async_copy(x, result.at[e], sems.at[e]) for e, x in enumerate(earlier)]
    for copy in copies:
        copy.start()
    final[...] = squared_blocks(experts - 1, experts, *given[:2], given[2:]) / divisor[:1]
    copies.append(pltpu.make_async_copy(final, result.at[experts - 1], sems.at[experts - 1]))
    copies[-1].start()
    for copy in copies:
        copy.wait()


def call(kernel, name, out_shape, specs=None, scratch=(), out_specs=None, flops=1, after=()):
    vmem = pl.BlockSpec(memory_space=pltpu.VMEM)
    given = {} if out_specs is None else {"out_specs": out_specs}

    def run(*args):
        def body(*refs):
            kernel(*refs[: len(args)], *refs[len(args) + len(after) :])

        return pl.pallas_call(
            body,
            out_shape=out_shape,
            in_specs=(specs or [vmem] * len(args)) + [vmem] * len(after),
            scratch_shapes=scratch,
            compiler_params=pltpu.CompilerParams(vmem_limit_bytes=VMEM),
            cost_estimate=pl.CostEstimate(flops=flops, bytes_accessed=1, transcendentals=0),
            name=name,
            **given,
        )(*args, *after)

    return run


def fast(acts, grads, routes, example_ids, expert_counts, basis_in, basis_out):
    tokens = acts.shape[0]
    experts, features, width = basis_in.shape
    cap = tokens // 2
    dp = lax.axis_size("dp")
    wide = experts * cap
    half = wide * width // 256
    hbm = pl.BlockSpec(memory_space=pltpu.HBM)
    vmem = pl.BlockSpec(memory_space=pltpu.VMEM)
    smem = pl.BlockSpec(memory_space=pltpu.SMEM)

    def pin(x):
        return pltpu.with_memory_space_constraint(x, pltpu.HBM)

    def rows(count, dtype):
        return jax.ShapeDtypeStruct((count, 128), dtype)

    core = [(t, t ^ 1) for t in range(4)]
    across = [(t, t ^ 2) for t in range(4)]

    def spread(pays):
        got = {k: lax.ppermute(pays[k], "dp", [(d, d ^ k) for d in range(dp)]) for k in FAR_FIRST}
        return [pays[0]] + [got[k] for k in range(1, dp)]

    partial = jax.ShapeDtypeStruct((experts, cap, width), F32)
    acc, label, pick = call(
        rotate_in_kernel,
        "rotate_in",
        (partial, rows(LABEL_ROWS, BF16), jax.ShapeDtypeStruct((wide, 2 * tokens), BF16)),
        [hbm] * 4,
        [
            pltpu.VMEM(acts.shape, BF16),
            pltpu.VMEM((2, tokens), jnp.int32),
            pltpu.VMEM((tokens,), jnp.int32),
            pltpu.VMEM(basis_in.shape, BF16),
            pltpu.SemaphoreType.DMA((3 + experts,)),
        ],
    )(pin(acts), pin(routes.T), pin(example_ids), pin(basis_in))
    keep, send = call(
        split_in_kernel, "split_in", (rows(half, F32), rows(half, F32)), flops=8 * 10**9
    )(acc)
    got = lax.ppermute(send, "tensor", core)
    pieces = call(pair_in_kernel, "pair_in", [rows(half // dp, BF16)] * dp)(keep, got)
    arrived = spread(pieces)

    quarter = half // (2 * experts)
    split_shape = (rows(2 * quarter, F32), rows(2 * quarter, F32))
    pair_shape = (rows(quarter, F32), rows(quarter, BF16))
    out_shape = rows(quarter + LABEL_ROWS, BF16)
    rotated, rest = call(
        rotate_first_kernel,
        "rotate_first",
        (
            jax.ShapeDtypeStruct((cap, width), F32),
            jax.ShapeDtypeStruct((wide - cap, grads.shape[2]), BF16),
        ),
        after=pieces[:1],
    )(grads, pick, basis_out)
    near = call(stack_kernel, "stack_in", rows(half, BF16))(*arrived)
    far = lax.ppermute(near, "tensor", across)
    keeps, gots, sends = [], [], []
    for e in range(experts):
        if e > 0:
            rotated = call(
                functools.partial(rotate_rest_kernel, e),
                "rotate_rest",
                jax.ShapeDtypeStruct((cap, width), F32),
                flops=10**9,
            )(rest, basis_out)
        keep, send = call(
            split_out_kernel, "split_out", split_shape, after=sends[-1:] or [near]
        )(rotated)
        got = lax.ppermute(send, "tensor", core)
        keep, send = call(pair_out_kernel, "pair_out", pair_shape)(keep, got)
        keeps.append(keep)
        sends.append(send)
        gots.append(lax.ppermute(send, "tensor", across))
    mine = call(sum_kernel, "sum_in", rows(half, BF16), after=gots[:1])(near, far)
    other = lax.ppermute(mine, "tensor", core)
    outs = []
    for e in range(experts):
        early = [mine, sends[-1]] if e == 0 else [outs[-1][1]]
        out = call(round_kernel, "round_out", out_shape, after=early)(keeps[e], gots[e], label)
        outs.append(spread([out] * dp))

    result = jax.ShapeDtypeStruct((experts, 128, 128), F32)
    done = []
    for e in range(experts - 1):
        block, divisor = call(
            functools.partial(blocks_kernel, e),
            "blocks",
            (rows(128, F32), rows(8, F32)),
            [smem] + [vmem] * (2 + dp),
        )(expert_counts, mine, other, *outs[e])
        done.append(block)
    return call(
        functools.partial(last_blocks_kernel, experts),
        "last_blocks",
        result,
        scratch=[pltpu.VMEM(result.shape[1:], F32), pltpu.SemaphoreType.DMA((experts,))],
        out_specs=hbm,
    )(divisor, *done, mine, other, *outs[-1])


EX_DEV = 1


def compact(routes, expert, capacity):
    tok_count = routes.shape[0]
    second_hit = routes[:, 1] == expert
    routed = (routes[:, 0] == expert) | second_hit
    order = jnp.cumsum(routed.astype(jnp.int32)) - 1
    slots = jnp.arange(capacity, dtype=jnp.int32)
    match = routed[None, :] & (order[None, :] == slots[:, None])
    token_index = jnp.arange(tok_count, dtype=jnp.int32)
    positions = jnp.sum(jnp.where(match, token_index[None, :], 0), axis=1)
    filled = jnp.any(match, axis=1)
    return (positions, filled, second_hit[positions])


def general(acts, grads, routes, example_ids, expert_counts, basis_in, basis_out):
    capacity = acts.shape[0] // 2
    experts = basis_in.shape[0]
    parts_in, parts_out, label_rows = ([], [], [])
    for expert in range(experts):
        positions, filled, second = compact(routes, expert, capacity)
        chosen = grads[positions]
        grad_rows = jnp.where(second[:, None], chosen[:, 1, :], chosen[:, 0, :])
        parts_in.append(
            jnp.dot(acts[positions], basis_in[expert], preferred_element_type=jnp.float32)
        )
        parts_out.append(jnp.dot(grad_rows, basis_out[expert], preferred_element_type=jnp.float32))
        label_rows.append(jnp.where(filled, example_ids[positions], -1))
    part_in = jnp.stack(parts_in)
    part_out = jnp.stack(parts_out)
    labels = jnp.stack(label_rows)
    slice_width = basis_out.shape[2] // lax.axis_size("tensor")
    summed_in, summed_out = lax.psum((part_in, part_out), "tensor")
    rot_in = summed_in.astype(jnp.bfloat16)
    rot_out = lax.dynamic_slice_in_dim(
        summed_out.astype(jnp.bfloat16), lax.axis_index("tensor") * slice_width, slice_width, 2
    )
    owned_count = EX_DEV
    wanted = jnp.arange(lax.axis_size("dp") * owned_count, dtype=jnp.int32)
    onehot = (labels[:, :, None] == wanted[None, None, :]).astype(jnp.bfloat16)
    spread = onehot[:, :, :, None] * rot_out[:, :, None, :]
    owned_sums = lax.psum_scatter(
        jnp.einsum("ecnw,eca->newa", spread, rot_in, preferred_element_type=jnp.float32),
        "dp",
        scatter_dimension=0,
        tiled=True,
    )
    squared = jnp.sum(owned_sums * owned_sums, axis=0)
    totals = lax.psum_scatter(squared, "dp", scatter_dimension=2, tiled=True)
    return totals / expert_counts.astype(jnp.float32)[:, None, None]


def shards(*args):
    width = args[5].shape[2]
    fits = lax.axis_size("tensor") == 4 and lax.axis_size("dp") == 4 and width == 512
    return (fast if fits else general)(*args)


def solution(mesh):
    placed = (
        P(("group", "dp"), "tensor"),
        P(("group", "dp"), None, "tensor"),
        P(("group", "dp"), None),
        P(("group", "dp")),
        P("group"),
        P(None, "tensor", None),
        P(None, "tensor", None),
    )
    return jax.shard_map(
        shards, mesh=mesh, in_specs=placed, out_specs=P("group", "tensor", "dp"), check_vma=False
    )
```

```python
import functools

import jax
import jax.numpy as jnp
from jax import lax
from jax.experimental import pallas as pl
from jax.experimental.pallas import tpu as pltpu
from jax.sharding import PartitionSpec as P

F32 = jnp.float32
BF16 = jnp.bfloat16
CHUNK = 512
VMEM = 20 * 2**20
ARRIVAL = (0, 2, 1, 3)
LABEL_ROWS = 16


def iota(shape, dim):
    return lax.broadcasted_iota(jnp.int32, shape, dim)


def dot(a, b):
    return jnp.dot(a, b, preferred_element_type=F32)


def fetcher(sems):
    count = iter(range(sems.shape[0]))

    def fetch(src, dst):
        copy = pltpu.make_async_copy(src, dst, sems.at[next(count)])
        copy.start()
        return copy

    return fetch


def rotate_in_kernel(
    acts, routes, ids, basis_in,
    acc, label, pick,
    acts_v, routes_v, ids_v, basis_v, sems,
):
    tokens = acts.shape[0]
    experts, _, width = basis_in.shape
    cap = tokens // 2
    fetch = fetcher(sems)
    first = [fetch(routes, routes_v), fetch(ids, ids_v)]
    acts_in = fetch(acts, acts_v)
    bases = [fetch(basis_in.at[e], basis_v.at[e]) for e in range(experts)]
    for copy in first:
        copy.wait()
    hits = [
        jnp.max((routes_v[...] == e).astype(F32), axis=0, keepdims=True) for e in range(experts)
    ]
    rows = jnp.concatenate(hits + [jnp.zeros((8 - experts, tokens), F32)], axis=0).astype(BF16)
    upto = (iota((tokens, tokens), 0) <= iota((tokens, tokens), 1)).astype(BF16)
    order = dot(rows, upto)
    slots = iota((cap, tokens), 0).astype(F32) + 1.0
    pick_in = jnp.concatenate(
        [((order[e : e + 1] == slots) & (hits[e] > 0.5)).astype(BF16) for e in range(experts)],
        axis=0,
    )
    repeat = (iota((tokens, 2 * tokens), 0) == iota((tokens, 2 * tokens), 1) // 2).astype(BF16)
    wide = dot(
        jnp.concatenate(
            [order[:experts], routes_v[...].astype(F32), jnp.zeros((6 - experts, tokens), F32)],
            axis=0,
        ).astype(BF16),
        repeat,
    )
    odd = iota((1, 2 * tokens), 1) % 2 == 1
    routed_to = jnp.where(odd, wide[experts + 1 : experts + 2], wide[experts : experts + 1])
    slots = iota((cap, 2 * tokens), 0).astype(F32) + 1.0
    for e in range(experts):
        pick[e * cap : (e + 1) * cap, :] = (
            (wide[e : e + 1] == slots) & (routed_to == float(e))
        ).astype(BF16)
    numbers = jnp.broadcast_to(ids_v[...].reshape(1, tokens).astype(F32) + 1.0, (8, tokens)).astype(BF16)
    named = lax.dot_general(numbers, pick_in, (((1,), (1,)), ((), ())), preferred_element_type=F32)
    block = jnp.zeros((LABEL_ROWS, 128), F32)
    row = iota((LABEL_ROWS, 128), 0)
    half = cap // 2
    for at in range(2 * experts):
        mine = named[0:1, at * half : (at + 1) * half]
        mine = jnp.concatenate([mine, jnp.zeros((1, 128 - half), F32)], axis=1)
        block = jnp.where(row == at, mine, block)
    label[...] = block.astype(BF16)

    acts_in.wait()
    chosen = dot(pick_in, acts_v[...]).astype(BF16)
    for e in range(experts):
        bases[e].wait()
        acc[e] = dot(chosen[e * cap : (e + 1) * cap], basis_v[e])


def split_in_kernel(acc, keep, send):
    experts, cap, width = acc.shape
    core = lax.rem(lax.axis_index("tensor"), 2)
    half = cap // 2
    at = 0
    for q in range(width // 128):
        for e in range(experts):
            for ref, which in ((keep, core), (send, 1 - core)):
                ref[at : at + half, :] = acc[
                    e, pl.ds(pl.multiple_of(which * half, 8), half), q * 128 : (q + 1) * 128
                ]
            at += half


def rotate_first_kernel(grads, pick, basis_out, acc, rest):
    tokens, _, hidden = grads.shape
    cap = tokens // 2
    for s in range(hidden // CHUNK):
        cols = pl.ds(s * CHUNK, CHUNK)
        chosen = dot(pick[...], grads[:, :, cols].reshape(2 * tokens, CHUNK)).astype(BF16)
        rest[:, cols] = chosen[cap:]
        part = dot(chosen[:cap], basis_out[0, cols, :])
        if s == 0:
            acc[...] = part
        else:
            acc[...] += part


def rotate_rest_kernel(e, rest, basis_out, acc):
    cap = acc.shape[0]
    acc[...] = dot(rest[(e - 1) * cap : e * cap, :], basis_out[e])


def split_out_kernel(acc, keep, send):
    cap, width = acc.shape
    core = lax.rem(lax.axis_index("tensor"), 2)
    for x in range(width // 256):
        for ref, which in ((keep, core), (send, 1 - core)):
            ref[x * cap : (x + 1) * cap, :] = acc[
                :, pl.ds(pl.multiple_of((2 * x + which) * 128, 128), 128)
            ]


def pair_in_kernel(kept, got, label, *pays):
    slab = kept.shape[0] // len(pays)
    d = lax.axis_index("dp")
    for k, pay in enumerate(pays):
        rows = pl.ds(pl.multiple_of((d ^ k) * slab, 16), slab)
        pay[:slab, :] = (kept[rows, :] + got[rows, :]).astype(BF16)
        pay[slab:, :] = label[...]


def pair_out_kernel(kept, got, keep, send):
    outer = keep.shape[0]
    x = lax.div(lax.axis_index("tensor"), 2)
    mine = pl.ds(pl.multiple_of(x * outer, 16), outer)
    keep[...] = kept[mine, :] + got[mine, :]
    other = pl.ds(pl.multiple_of((1 - x) * outer, 16), outer)
    send[...] = (kept[other, :] + got[other, :]).astype(BF16)


def round_kernel(kept, got, out):
    out[...] = (kept[...] + got[...].astype(F32)).astype(BF16)


def pile_kernel(near, far, out):
    out[: near.shape[0], :] = near[...]
    out[near.shape[0] :, :] = far[...]


def stack_kernel(*refs):
    *pieces, out = refs
    slab = pieces[0].shape[0] - LABEL_ROWS
    for k, piece in enumerate(pieces):
        out[k * slab : (k + 1) * slab, :] = piece[:slab, :]


def sum_kernel(near, far, out):
    out[...] = (near[...].astype(F32) + far[...].astype(F32)).astype(BF16)


def mask_kernel(experts, mine, other, *refs):
    pieces, out = refs[:-1], refs[-1]
    dp = len(pieces)
    slab = pieces[0].shape[0] - LABEL_ROWS
    half = slab // experts
    core = lax.rem(lax.axis_index("tensor"), 2)
    for e in range(experts):
        rows, labels = [], []
        for which, ref in ((core, mine), (1 - core, other)):
            for k, piece in enumerate(pieces):
                at = (k * experts + e) * half
                rows.append(ref[at : at + half, :])
                label = piece[slab:, :].astype(F32)[2 * e : 2 * e + 2, :half]
                labels.append(jnp.where(which == 0, label[0:1], label[1:2]))
        rows = jnp.concatenate(rows, axis=0).astype(F32)
        labels = jnp.concatenate(labels, axis=1)
        labels = jnp.broadcast_to(labels, (128, labels.shape[1])).T
        for n in range(dp):
            out[e, :, n * 128 : (n + 1) * 128] = jnp.where(
                labels == float(n + 1), rows, 0.0
            ).astype(BF16)


def squared_blocks(e, masked, *outs):
    cap = masked.shape[1] * 128 // masked.shape[2]
    half = cap // 2
    core = lax.rem(lax.axis_index("tensor"), 2)
    rows = [
        ref[pl.ds(pl.multiple_of(at + which * half, 16), half), :]
        for which in (core, 1 - core)
        for ref in outs
        for at in range(0, ref.shape[0], cap)
    ]
    blocks = dot(jnp.concatenate(rows, axis=0).T, masked[e])
    squares = blocks * blocks
    summed = squares[:, :128]
    for at in range(128, squares.shape[1], 128):
        summed = summed + squares[:, at : at + 128]
    return summed


def blocks_kernel(e, counts, masked, near, far, result, divisor):
    result[...] = squared_blocks(e, masked, near, far) / counts[e].astype(F32)
    divisor[...] = jnp.full(divisor.shape, counts[counts.shape[0] - 1].astype(F32), F32)


def last_blocks_kernel(experts, divisor, masked, near, far, *refs):
    *earlier, result, final, sems = refs
    copies = [pltpu.make_async_copy(x, result.at[e], sems.at[e]) for e, x in enumerate(earlier)]
    for copy in copies:
        copy.start()
    final[...] = squared_blocks(experts - 1, masked, near, far) / divisor[:1]
    copies.append(pltpu.make_async_copy(final, result.at[experts - 1], sems.at[experts - 1]))
    copies[-1].start()
    for copy in copies:
        copy.wait()


def call(kernel, name, out_shape, specs=None, scratch=(), out_specs=None, flops=1, after=()):
    vmem = pl.BlockSpec(memory_space=pltpu.VMEM)
    given = {} if out_specs is None else {"out_specs": out_specs}

    def run(*args):
        def body(*refs):
            kernel(*refs[: len(args)], *refs[len(args) + len(after) :])

        return pl.pallas_call(
            body,
            out_shape=out_shape,
            in_specs=(specs or [vmem] * len(args)) + [vmem] * len(after),
            scratch_shapes=scratch,
            compiler_params=pltpu.CompilerParams(vmem_limit_bytes=VMEM),
            cost_estimate=pl.CostEstimate(flops=flops, bytes_accessed=1, transcendentals=0),
            name=name,
            **given,
        )(*args, *after)

    return run


def fast(acts, grads, routes, example_ids, expert_counts, basis_in, basis_out):
    tokens = acts.shape[0]
    experts, features, width = basis_in.shape
    cap = tokens // 2
    dp = lax.axis_size("dp")
    wide = experts * cap
    half = wide * width // 256
    hbm = pl.BlockSpec(memory_space=pltpu.HBM)
    vmem = pl.BlockSpec(memory_space=pltpu.VMEM)
    smem = pl.BlockSpec(memory_space=pltpu.SMEM)

    def pin(x):
        return pltpu.with_memory_space_constraint(x, pltpu.HBM)

    def rows(count, dtype):
        return jax.ShapeDtypeStruct((count, 128), dtype)

    core = [(t, t ^ 1) for t in range(4)]
    across = [(t, t ^ 2) for t in range(4)]

    def swap(x, k):
        return lax.ppermute(x, "dp", [(d, d ^ k) for d in range(dp)])

    partial = jax.ShapeDtypeStruct((experts, cap, width), F32)
    acc, label, pick = call(
        rotate_in_kernel,
        "rotate_in",
        (partial, rows(LABEL_ROWS, BF16), jax.ShapeDtypeStruct((wide, 2 * tokens), BF16)),
        [hbm] * 4,
        [
            pltpu.VMEM(acts.shape, BF16),
            pltpu.VMEM((2, tokens), jnp.int32),
            pltpu.VMEM((tokens,), jnp.int32),
            pltpu.VMEM(basis_in.shape, BF16),
            pltpu.SemaphoreType.DMA((3 + experts,)),
        ],
    )(pin(acts), pin(routes.T), pin(example_ids), pin(basis_in))
    keep, send = call(
        split_in_kernel, "split_in", (rows(half, F32), rows(half, F32)), flops=8 * 10**9
    )(acc)
    got = lax.ppermute(send, "tensor", core)
    pieces = call(pair_in_kernel, "pair_in", [rows(half // dp + LABEL_ROWS, BF16)] * dp)(
        keep, got, label
    )
    arrived = [pieces[0]] + [swap(pieces[k], k) for k in range(1, dp)]
    arrived = [arrived[k] for k in ARRIVAL]

    quarter = half // (2 * experts)
    split_shape = (rows(2 * quarter, F32), rows(2 * quarter, F32))
    pair_shape = (rows(quarter, F32), rows(quarter, BF16))
    out_shape = rows(quarter + LABEL_ROWS, BF16)
    rotated, rest = call(
        rotate_first_kernel,
        "rotate_first",
        (
            jax.ShapeDtypeStruct((cap, width), F32),
            jax.ShapeDtypeStruct((wide - cap, grads.shape[2]), BF16),
        ),
        after=pieces[:1],
    )(grads, pick, basis_out)
    keeps, gots, sends = [], [], []
    for e in range(experts):
        if e > 0:
            rotated = call(
                functools.partial(rotate_rest_kernel, e),
                "rotate_rest",
                jax.ShapeDtypeStruct((cap, width), F32),
                flops=10**9,
            )(rest, basis_out)
        keep, send = call(
            split_out_kernel, "split_out", split_shape, after=sends[-1:] or arrived[1:]
        )(rotated)
        got = lax.ppermute(send, "tensor", core)
        keep, send = call(pair_out_kernel, "pair_out", pair_shape)(keep, got)
        keeps.append(keep)
        sends.append(send)
        gots.append(lax.ppermute(send, "tensor", across))
    near = call(stack_kernel, "stack_in", rows(half, BF16), after=[gots[0], sends[-1]])(
        *arrived
    )
    far = lax.ppermute(near, "tensor", across)
    outs = []
    for e in range(experts):
        out = call(round_kernel, "round_out", rows(quarter, BF16), after=sends[-1:])(
            keeps[e], gots[e]
        )
        pair = call(pile_kernel, "pile_out", rows(2 * quarter, BF16))(out, swap(out, 2))
        outs.append((pair, swap(pair, 1)))
    mine = call(sum_kernel, "sum_in", rows(half, BF16), after=outs[0][:1])(near, far)
    other = lax.ppermute(mine, "tensor", core)
    masked = call(
        functools.partial(mask_kernel, experts),
        "mask_in",
        jax.ShapeDtypeStruct((experts, dp * cap, dp * 128), BF16),
    )(mine, other, *arrived)

    result = jax.ShapeDtypeStruct((experts, 128, 128), F32)
    done = []
    for e in range(experts - 1):
        block, divisor = call(
            functools.partial(blocks_kernel, e),
            "blocks",
            (rows(128, F32), rows(8, F32)),
            [smem] + [vmem] * 3,
        )(expert_counts, masked, *outs[e])
        done.append(block)
    return call(
        functools.partial(last_blocks_kernel, experts),
        "last_blocks",
        result,
        scratch=[pltpu.VMEM(result.shape[1:], F32), pltpu.SemaphoreType.DMA((experts,))],
        out_specs=hbm,
    )(divisor, masked, *outs[-1], *done)


EX_DEV = 1


def compact(routes, expert, capacity):
    tok_count = routes.shape[0]
    second_hit = routes[:, 1] == expert
    routed = (routes[:, 0] == expert) | second_hit
    order = jnp.cumsum(routed.astype(jnp.int32)) - 1
    slots = jnp.arange(capacity, dtype=jnp.int32)
    match = routed[None, :] & (order[None, :] == slots[:, None])
    token_index = jnp.arange(tok_count, dtype=jnp.int32)
    positions = jnp.sum(jnp.where(match, token_index[None, :], 0), axis=1)
    filled = jnp.any(match, axis=1)
    return (positions, filled, second_hit[positions])


def general(acts, grads, routes, example_ids, expert_counts, basis_in, basis_out):
    capacity = acts.shape[0] // 2
    experts = basis_in.shape[0]
    parts_in, parts_out, label_rows = ([], [], [])
    for expert in range(experts):
        positions, filled, second = compact(routes, expert, capacity)
        chosen = grads[positions]
        grad_rows = jnp.where(second[:, None], chosen[:, 1, :], chosen[:, 0, :])
        parts_in.append(
            jnp.dot(acts[positions], basis_in[expert], preferred_element_type=jnp.float32)
        )
        parts_out.append(jnp.dot(grad_rows, basis_out[expert], preferred_element_type=jnp.float32))
        label_rows.append(jnp.where(filled, example_ids[positions], -1))
    part_in = jnp.stack(parts_in)
    part_out = jnp.stack(parts_out)
    labels = jnp.stack(label_rows)
    slice_width = basis_out.shape[2] // lax.axis_size("tensor")
    summed_in, summed_out = lax.psum((part_in, part_out), "tensor")
    rot_in = summed_in.astype(jnp.bfloat16)
    rot_out = lax.dynamic_slice_in_dim(
        summed_out.astype(jnp.bfloat16), lax.axis_index("tensor") * slice_width, slice_width, 2
    )
    owned_count = EX_DEV
    wanted = jnp.arange(lax.axis_size("dp") * owned_count, dtype=jnp.int32)
    onehot = (labels[:, :, None] == wanted[None, None, :]).astype(jnp.bfloat16)
    spread = onehot[:, :, :, None] * rot_out[:, :, None, :]
    owned_sums = lax.psum_scatter(
        jnp.einsum("ecnw,eca->newa", spread, rot_in, preferred_element_type=jnp.float32),
        "dp",
        scatter_dimension=0,
        tiled=True,
    )
    squared = jnp.sum(owned_sums * owned_sums, axis=0)
    totals = lax.psum_scatter(squared, "dp", scatter_dimension=2, tiled=True)
    return totals / expert_counts.astype(jnp.float32)[:, None, None]


def shards(*args):
    width = args[5].shape[2]
    fits = lax.axis_size("tensor") == 4 and lax.axis_size("dp") == 4 and width == 512
    return (fast if fits else general)(*args)


def solution(mesh):
    placed = (
        P(("group", "dp"), "tensor"),
        P(("group", "dp"), None, "tensor"),
        P(("group", "dp"), None),
        P(("group", "dp")),
        P("group"),
        P(None, "tensor", None),
        P(None, "tensor", None),
    )
    return jax.shard_map(
        shards, mesh=mesh, in_specs=placed, out_specs=P("group", "tensor", "dp"), check_vma=False
    )
```

```python
import functools

import jax
import jax.numpy as jnp
from jax import lax
from jax.experimental import pallas as pl
from jax.experimental.pallas import tpu as pltpu
from jax.sharding import PartitionSpec as P

F32 = jnp.float32
BF16 = jnp.bfloat16
CHUNK = 1024
EARLY = 1024
PARTS = 3
VMEM = 20 * 2**20
ARRIVAL = (0, 1, 3, 2)
LABEL_ROWS = 16


def iota(shape, dim):
    return lax.broadcasted_iota(jnp.int32, shape, dim)


def dot(a, b):
    return jnp.dot(a, b, preferred_element_type=F32)


def fetcher(sems):
    count = iter(range(sems.shape[0]))

    def fetch(src, dst):
        copy = pltpu.make_async_copy(src, dst, sems.at[next(count)])
        copy.start()
        return copy

    return fetch


def rotate_in_kernel(
    acts, routes, ids, basis_in, grads,
    acc, label, pick, early,
    acts_v, routes_v, ids_v, basis_v, sems,
):
    tokens, features = acts.shape
    experts = basis_in.shape[0]
    cap = tokens // 2
    parts = [pl.ds(at, features // PARTS) for at in range(0, features, features // PARTS)]
    fetch = fetcher(sems)
    first = [fetch(routes, routes_v), fetch(ids, ids_v)]
    acts_in = [fetch(acts.at[:, part], acts_v.at[:, part]) for part in parts]
    bases = [fetch(basis_in.at[:, part, :], basis_v.at[:, part, :]) for part in parts]
    grads_in = fetch(grads.at[:, :, pl.ds(0, early.shape[2])], early)
    for copy in first:
        copy.wait()
    hits = [
        jnp.max((routes_v[...] == e).astype(F32), axis=0, keepdims=True) for e in range(experts)
    ]
    rows = jnp.concatenate(hits + [jnp.zeros((8 - experts, tokens), F32)], axis=0).astype(BF16)
    upto = (iota((tokens, tokens), 0) <= iota((tokens, tokens), 1)).astype(BF16)
    order = dot(rows, upto)
    slots = iota((cap, tokens), 0).astype(F32) + 1.0
    pick_in = jnp.concatenate(
        [((order[e : e + 1] == slots) & (hits[e] > 0.5)).astype(BF16) for e in range(experts)],
        axis=0,
    )
    repeat = (iota((tokens, 2 * tokens), 0) == iota((tokens, 2 * tokens), 1) // 2).astype(BF16)
    wide = dot(
        jnp.concatenate(
            [order[:experts], routes_v[...].astype(F32), jnp.zeros((6 - experts, tokens), F32)],
            axis=0,
        ).astype(BF16),
        repeat,
    )
    odd = iota((1, 2 * tokens), 1) % 2 == 1
    routed_to = jnp.where(odd, wide[experts + 1 : experts + 2], wide[experts : experts + 1])
    slots = iota((cap, 2 * tokens), 0).astype(F32) + 1.0
    for e in range(experts):
        pick[e * cap : (e + 1) * cap, :] = (
            (wide[e : e + 1] == slots) & (routed_to == float(e))
        ).astype(BF16)
    numbers = jnp.broadcast_to(ids_v[...].reshape(1, tokens).astype(F32) + 1.0, (8, tokens)).astype(BF16)
    named = lax.dot_general(numbers, pick_in, (((1,), (1,)), ((), ())), preferred_element_type=F32)
    block = jnp.zeros((LABEL_ROWS, 128), F32)
    row = iota((LABEL_ROWS, 128), 0)
    half = cap // 2
    for at in range(2 * experts):
        mine = named[0:1, at * half : (at + 1) * half]
        mine = jnp.concatenate([mine, jnp.zeros((1, 128 - half), F32)], axis=1)
        block = jnp.where(row == at, mine, block)
    label[...] = block.astype(BF16)

    chosen = []
    for part, copy in zip(parts, acts_in):
        copy.wait()
        chosen.append(dot(pick_in, acts_v[:, part]).astype(BF16))
    for n, part in enumerate(parts):
        bases[n].wait()
        for e in range(experts):
            more = dot(chosen[n][e * cap : (e + 1) * cap], basis_v[e, part, :])
            acc[e] = more if n == 0 else acc[e] + more
    grads_in.wait()


def split_in_kernel(acc, keep, send):
    experts, cap, width = acc.shape
    core = lax.rem(lax.axis_index("tensor"), 2)
    half = cap // 2
    at = 0
    for q in range(width // 128):
        for e in range(experts):
            for ref, which in ((keep, core), (send, 1 - core)):
                ref[at : at + half, :] = acc[
                    e, pl.ds(pl.multiple_of(which * half, 8), half), q * 128 : (q + 1) * 128
                ]
            at += half


def choose(pick, grads, cols):
    rows = grads[:, :, cols]
    return dot(pick[...], rows.reshape(rows.shape[0] * 2, rows.shape[2])).astype(BF16)


def choose_kernel(grads, pick, out):
    out[...] = choose(pick, grads, slice(None))


def rotate_first_kernel(grads, pick, basis_out, early, acc, rest):
    cap, width = acc.shape
    done = early.shape[1]
    rest[:, :done] = early[cap:, :]
    acc[...] = dot(early[:cap, :], basis_out[0, :done, :])
    for at in range(done, grads.shape[2], CHUNK):
        cols = pl.ds(at, CHUNK)
        chosen = choose(pick, grads, cols)
        rest[:, cols] = chosen[cap:]
        acc[...] += dot(chosen[:cap], basis_out[0, cols, :])


def rotate_rest_kernel(e, rest, basis_out, acc):
    cap = acc.shape[0]
    acc[...] = dot(rest[(e - 1) * cap : e * cap, :], basis_out[e])


def split_out_kernel(acc, keep, send):
    cap, width = acc.shape
    core = lax.rem(lax.axis_index("tensor"), 2)
    for x in range(width // 256):
        for ref, which in ((keep, core), (send, 1 - core)):
            ref[x * cap : (x + 1) * cap, :] = acc[
                :, pl.ds(pl.multiple_of((2 * x + which) * 128, 128), 128)
            ]


def pair_in_kernel(kept, got, label, *pays):
    slab = kept.shape[0] // len(pays)
    d = lax.axis_index("dp")
    for k, pay in enumerate(pays):
        rows = pl.ds(pl.multiple_of((d ^ k) * slab, 16), slab)
        pay[:slab, :] = (kept[rows, :] + got[rows, :]).astype(BF16)
        pay[slab:, :] = label[...]


def pair_out_kernel(kept, got, keep, send):
    outer = keep.shape[0]
    x = lax.div(lax.axis_index("tensor"), 2)
    mine = pl.ds(pl.multiple_of(x * outer, 16), outer)
    keep[...] = kept[mine, :] + got[mine, :]
    other = pl.ds(pl.multiple_of((1 - x) * outer, 16), outer)
    send[...] = (kept[other, :] + got[other, :]).astype(BF16)


def round_kernel(*refs):
    *given, out = refs
    cap = given[0].shape[0]
    for e in range(len(given) // 2):
        kept, got = given[2 * e : 2 * e + 2]
        out[e * cap : (e + 1) * cap, :] = (kept[...] + got[...].astype(F32)).astype(BF16)


def stack_kernel(experts, *refs):
    pieces, outs = refs[:-experts], refs[-experts:]
    half = (pieces[0].shape[0] - LABEL_ROWS) // experts
    for k, piece in enumerate(pieces):
        for e, out in enumerate(outs):
            out[k * half : (k + 1) * half, :] = piece[e * half : (e + 1) * half, :]


def sum_kernel(near, far, *outs):
    piece = outs[0].shape[0]
    for n, out in enumerate(outs):
        at = pl.ds(n * piece, piece)
        out[...] = (near[at, :].astype(F32) + far[at, :].astype(F32)).astype(BF16)


def mask(e, which, rows, pieces):
    dp = len(pieces)
    rows = jnp.concatenate([row[...] for row in rows], axis=0).astype(F32)
    half = rows.shape[0] // dp
    labels = []
    for piece in pieces:
        label = piece[-LABEL_ROWS:, :].astype(F32)[2 * e : 2 * e + 2, :half]
        labels.append(jnp.where(which == 0, label[0:1], label[1:2]))
    labels = jnp.concatenate(labels, axis=1)
    labels = jnp.broadcast_to(labels, (128, labels.shape[1])).T
    return jnp.concatenate(
        [jnp.where(labels == float(n + 1), rows, 0.0).astype(BF16) for n in range(dp)], axis=1
    )


def mask_kernel(experts, *refs):
    mine, pieces, out = refs[: 2 * experts], refs[2 * experts : -1], refs[-1]
    core = lax.rem(lax.axis_index("tensor"), 2)
    for e in range(experts):
        out[e] = mask(e, core, mine[2 * e : 2 * e + 2], pieces)


def gather_kernel(*refs):
    *given, out = refs
    experts = out.shape[0]
    cap = given[0].shape[0] // experts
    half = cap // 2
    core = lax.rem(lax.axis_index("tensor"), 2)
    for e in range(experts):
        rows = [
            ref[pl.ds(pl.multiple_of(e * cap + which * half, 16), half), :]
            for which in (core, 1 - core)
            for ref in given
        ]
        out[e] = jnp.concatenate(rows, axis=0).T


def blocks_kernel(counts, rows_out, masked, *refs):
    experts, half = masked.shape[:2]
    other, pieces = refs[: 2 * experts], refs[2 * experts : -3]
    result, final, sems = refs[-3:]
    core = lax.rem(lax.axis_index("tensor"), 2)
    copies = []
    for e in range(experts):
        blocks = dot(rows_out[e, :, :half], masked[e])
        blocks += dot(rows_out[e, :, half:], mask(e, 1 - core, other[2 * e : 2 * e + 2], pieces))
        squares = blocks * blocks
        summed = squares[:, :128]
        for at in range(128, squares.shape[1], 128):
            summed = summed + squares[:, at : at + 128]
        final[e] = summed / counts[e].astype(F32)
        copies.append(pltpu.make_async_copy(final.at[e], result.at[e], sems.at[e]))
        copies[-1].start()
    for copy in copies:
        copy.wait()


def call(kernel, name, out_shape, specs=None, scratch=(), out_specs=None, flops=1, after=()):
    vmem = pl.BlockSpec(memory_space=pltpu.VMEM)
    given = {} if out_specs is None else {"out_specs": out_specs}

    def run(*args):
        def body(*refs):
            kernel(*refs[: len(args)], *refs[len(args) + len(after) :])

        return pl.pallas_call(
            body,
            out_shape=out_shape,
            in_specs=(specs or [vmem] * len(args)) + [vmem] * len(after),
            scratch_shapes=scratch,
            compiler_params=pltpu.CompilerParams(vmem_limit_bytes=VMEM),
            cost_estimate=pl.CostEstimate(flops=flops, bytes_accessed=1, transcendentals=0),
            name=name,
            **given,
        )(*args, *after)

    return run


def fast(acts, grads, routes, example_ids, expert_counts, basis_in, basis_out):
    tokens = acts.shape[0]
    experts, features, width = basis_in.shape
    cap = tokens // 2
    dp = lax.axis_size("dp")
    wide = experts * cap
    half = wide * width // 256
    hbm = pl.BlockSpec(memory_space=pltpu.HBM)
    vmem = pl.BlockSpec(memory_space=pltpu.VMEM)
    smem = pl.BlockSpec(memory_space=pltpu.SMEM)

    def pin(x):
        return pltpu.with_memory_space_constraint(x, pltpu.HBM)

    def rows(count, dtype):
        return jax.ShapeDtypeStruct((count, 128), dtype)

    core = [(t, t ^ 1) for t in range(4)]
    across = [(t, t ^ 2) for t in range(4)]

    def swap(x, k):
        return lax.ppermute(x, "dp", [(d, d ^ k) for d in range(dp)])

    partial = jax.ShapeDtypeStruct((experts, cap, width), F32)
    acc, label, pick, early = call(
        rotate_in_kernel,
        "rotate_in",
        (
            partial,
            rows(LABEL_ROWS, BF16),
            jax.ShapeDtypeStruct((wide, 2 * tokens), BF16),
            jax.ShapeDtypeStruct((tokens, 2, EARLY), BF16),
        ),
        [hbm] * 5,
        [
            pltpu.VMEM(acts.shape, BF16),
            pltpu.VMEM((2, tokens), jnp.int32),
            pltpu.VMEM((tokens,), jnp.int32),
            pltpu.VMEM(basis_in.shape, BF16),
            pltpu.SemaphoreType.DMA((3 + 2 * PARTS,)),
        ],
    )(pin(acts), pin(routes.T), pin(example_ids), pin(basis_in), pin(grads))
    keep, send = call(
        split_in_kernel, "split_in", (rows(half, F32), rows(half, F32)), flops=8 * 10**9
    )(acc)
    got = lax.ppermute(send, "tensor", core)
    early = call(choose_kernel, "choose", jax.ShapeDtypeStruct((wide, EARLY), BF16))(early, pick)
    pieces = call(pair_in_kernel, "pair_in", [rows(half // dp + LABEL_ROWS, BF16)] * dp, after=[early])(
        keep, got, label
    )
    arrived = [pieces[0]] + [swap(pieces[k], k) for k in range(1, dp)]
    arrived = [arrived[k] for k in ARRIVAL]

    quarter = half // (2 * experts)
    split_shape = (rows(2 * quarter, F32), rows(2 * quarter, F32))
    pair_shape = (rows(quarter, F32), rows(quarter, BF16))
    out_shape = rows(quarter + LABEL_ROWS, BF16)
    rotated, rest = call(
        rotate_first_kernel,
        "rotate_first",
        (
            jax.ShapeDtypeStruct((cap, width), F32),
            jax.ShapeDtypeStruct((wide - cap, grads.shape[2]), BF16),
        ),
        after=pieces[:1],
    )(grads, pick, basis_out, early)
    keeps, gots, sends = [], [], []
    for e in range(experts):
        if e > 0:
            rotated = call(
                functools.partial(rotate_rest_kernel, e),
                "rotate_rest",
                jax.ShapeDtypeStruct((cap, width), F32),
                flops=10**9,
            )(rest, basis_out)
        keep, send = call(
            split_out_kernel, "split_out", split_shape, after=sends[-1:] or arrived[1:]
        )(rotated)
        got = lax.ppermute(send, "tensor", core)
        keep, send = call(pair_out_kernel, "pair_out", pair_shape)(keep, got)
        keeps.append(keep)
        sends.append(send)
        gots.append(lax.ppermute(send, "tensor", across))
    given = [x for e in range(experts) for x in (keeps[e], gots[e])]
    out = call(round_kernel, "round_out", rows(wide, BF16))(*given)
    outs = [out] + [swap(out, k) for k in ARRIVAL[1:]]
    near = call(
        functools.partial(stack_kernel, experts),
        "stack_in",
        [rows(half // experts, BF16)] * experts,
        after=sends[-1:],
    )(*arrived)
    far = [lax.ppermute(x, "tensor", across) for x in near]
    sums = [rows(half // (2 * experts), BF16)] * 2
    mine = [x for pair in zip(near, far) for x in call(sum_kernel, "sum_in", sums)(*pair)]
    other = [lax.ppermute(x, "tensor", core) for x in mine]
    masked = call(
        functools.partial(mask_kernel, experts),
        "mask_in",
        jax.ShapeDtypeStruct((experts, wide * dp // (2 * experts), dp * 128), BF16),
    )(*mine, *arrived)
    rows_out = call(
        gather_kernel, "gather_out", jax.ShapeDtypeStruct((experts, 128, dp * cap), BF16)
    )(*outs)
    result = jax.ShapeDtypeStruct((experts, 128, 128), F32)
    return call(
        blocks_kernel,
        "blocks",
        result,
        [smem] + [vmem] * (2 + 2 * experts + dp),
        scratch=[pltpu.VMEM(result.shape, F32), pltpu.SemaphoreType.DMA((experts,))],
        out_specs=hbm,
    )(expert_counts, rows_out, masked, *other, *arrived)


EX_DEV = 1


def compact(routes, expert, capacity):
    tok_count = routes.shape[0]
    second_hit = routes[:, 1] == expert
    routed = (routes[:, 0] == expert) | second_hit
    order = jnp.cumsum(routed.astype(jnp.int32)) - 1
    slots = jnp.arange(capacity, dtype=jnp.int32)
    match = routed[None, :] & (order[None, :] == slots[:, None])
    token_index = jnp.arange(tok_count, dtype=jnp.int32)
    positions = jnp.sum(jnp.where(match, token_index[None, :], 0), axis=1)
    filled = jnp.any(match, axis=1)
    return (positions, filled, second_hit[positions])


def general(acts, grads, routes, example_ids, expert_counts, basis_in, basis_out):
    capacity = acts.shape[0] // 2
    experts = basis_in.shape[0]
    parts_in, parts_out, label_rows = ([], [], [])
    for expert in range(experts):
        positions, filled, second = compact(routes, expert, capacity)
        chosen = grads[positions]
        grad_rows = jnp.where(second[:, None], chosen[:, 1, :], chosen[:, 0, :])
        parts_in.append(
            jnp.dot(acts[positions], basis_in[expert], preferred_element_type=jnp.float32)
        )
        parts_out.append(jnp.dot(grad_rows, basis_out[expert], preferred_element_type=jnp.float32))
        label_rows.append(jnp.where(filled, example_ids[positions], -1))
    part_in = jnp.stack(parts_in)
    part_out = jnp.stack(parts_out)
    labels = jnp.stack(label_rows)
    slice_width = basis_out.shape[2] // lax.axis_size("tensor")
    summed_in, summed_out = lax.psum((part_in, part_out), "tensor")
    rot_in = summed_in.astype(jnp.bfloat16)
    rot_out = lax.dynamic_slice_in_dim(
        summed_out.astype(jnp.bfloat16), lax.axis_index("tensor") * slice_width, slice_width, 2
    )
    owned_count = EX_DEV
    wanted = jnp.arange(lax.axis_size("dp") * owned_count, dtype=jnp.int32)
    onehot = (labels[:, :, None] == wanted[None, None, :]).astype(jnp.bfloat16)
    spread = onehot[:, :, :, None] * rot_out[:, :, None, :]
    owned_sums = lax.psum_scatter(
        jnp.einsum("ecnw,eca->newa", spread, rot_in, preferred_element_type=jnp.float32),
        "dp",
        scatter_dimension=0,
        tiled=True,
    )
    squared = jnp.sum(owned_sums * owned_sums, axis=0)
    totals = lax.psum_scatter(squared, "dp", scatter_dimension=2, tiled=True)
    return totals / expert_counts.astype(jnp.float32)[:, None, None]


def shards(*args):
    width = args[5].shape[2]
    fits = lax.axis_size("tensor") == 4 and lax.axis_size("dp") == 4 and width == 512
    return (fast if fits else general)(*args)


def solution(mesh):
    placed = (
        P(("group", "dp"), "tensor"),
        P(("group", "dp"), None, "tensor"),
        P(("group", "dp"), None),
        P(("group", "dp")),
        P("group"),
        P(None, "tensor", None),
        P(None, "tensor", None),
    )
    return jax.shard_map(
        shards, mesh=mesh, in_specs=placed, out_specs=P("group", "tensor", "dp"), check_vma=False
    )
```

```python
import functools

import jax
import jax.numpy as jnp
from jax import lax
from jax.experimental import pallas as pl
from jax.experimental.pallas import tpu as pltpu
from jax.sharding import PartitionSpec as P

F32 = jnp.float32
BF16 = jnp.bfloat16
CHUNK = 1024
EARLY = 1024
PARTS = 3
VMEM = 20 * 2**20
LABEL_ROWS = 16


def iota(shape, dim):
    return lax.broadcasted_iota(jnp.int32, shape, dim)


def dot(a, b):
    return jnp.dot(a, b, preferred_element_type=F32)


def fetcher(sems):
    count = iter(range(sems.shape[0]))

    def fetch(src, dst):
        copy = pltpu.make_async_copy(src, dst, sems.at[next(count)])
        copy.start()
        return copy

    return fetch


def rotate_in_kernel(
    acts, routes, ids, basis_in, grads,
    acc, label, pick, early,
    acts_v, routes_v, ids_v, basis_v, sems,
):
    tokens, features = acts.shape
    experts = basis_in.shape[0]
    cap = tokens // 2
    parts = [pl.ds(at, features // PARTS) for at in range(0, features, features // PARTS)]
    fetch = fetcher(sems)
    first = [fetch(routes, routes_v), fetch(ids, ids_v)]
    acts_in = [fetch(acts.at[:, part], acts_v.at[:, part]) for part in parts]
    bases = [fetch(basis_in.at[:, part, :], basis_v.at[:, part, :]) for part in parts]
    grads_in = fetch(grads.at[:, :, pl.ds(0, early.shape[2])], early)
    for copy in first:
        copy.wait()
    hits = [
        jnp.max((routes_v[...] == e).astype(F32), axis=0, keepdims=True) for e in range(experts)
    ]
    rows = jnp.concatenate(hits + [jnp.zeros((8 - experts, tokens), F32)], axis=0).astype(BF16)
    upto = (iota((tokens, tokens), 0) <= iota((tokens, tokens), 1)).astype(BF16)
    order = dot(rows, upto)
    slots = iota((cap, tokens), 0).astype(F32) + 1.0
    pick_in = jnp.concatenate(
        [((order[e : e + 1] == slots) & (hits[e] > 0.5)).astype(BF16) for e in range(experts)],
        axis=0,
    )
    repeat = (iota((tokens, 2 * tokens), 0) == iota((tokens, 2 * tokens), 1) // 2).astype(BF16)
    wide = dot(
        jnp.concatenate(
            [order[:experts], routes_v[...].astype(F32), jnp.zeros((6 - experts, tokens), F32)],
            axis=0,
        ).astype(BF16),
        repeat,
    )
    odd = iota((1, 2 * tokens), 1) % 2 == 1
    routed_to = jnp.where(odd, wide[experts + 1 : experts + 2], wide[experts : experts + 1])
    slots = iota((cap, 2 * tokens), 0).astype(F32) + 1.0
    for e in range(experts):
        pick[e * cap : (e + 1) * cap, :] = (
            (wide[e : e + 1] == slots) & (routed_to == float(e))
        ).astype(BF16)
    numbers = jnp.broadcast_to(ids_v[...].reshape(1, tokens).astype(F32) + 1.0, (8, tokens)).astype(BF16)
    named = lax.dot_general(numbers, pick_in, (((1,), (1,)), ((), ())), preferred_element_type=F32)
    block = jnp.zeros((LABEL_ROWS, 128), F32)
    row = iota((LABEL_ROWS, 128), 0)
    half = cap // 2
    for at in range(2 * experts):
        mine = named[0:1, at * half : (at + 1) * half]
        mine = jnp.concatenate([mine, jnp.zeros((1, 128 - half), F32)], axis=1)
        block = jnp.where(row == at, mine, block)
    label[...] = block.astype(BF16)

    chosen = []
    for part, copy in zip(parts, acts_in):
        copy.wait()
        chosen.append(dot(pick_in, acts_v[:, part]).astype(BF16))
    for n, part in enumerate(parts):
        bases[n].wait()
        for e in range(experts):
            more = dot(chosen[n][e * cap : (e + 1) * cap], basis_v[e, part, :])
            acc[e] = more if n == 0 else acc[e] + more
    grads_in.wait()


def split_in_kernel(acc, keep, send):
    experts, cap, width = acc.shape
    core = lax.rem(lax.axis_index("tensor"), 2)
    half = cap // 2
    at = 0
    for q in range(width // 128):
        for e in range(experts):
            for ref, which in ((keep, core), (send, 1 - core)):
                ref[at : at + half, :] = acc[
                    e, pl.ds(pl.multiple_of(which * half, 8), half), q * 128 : (q + 1) * 128
                ]
            at += half


def choose(pick, grads, cols):
    rows = grads[:, :, cols]
    return dot(pick[...], rows.reshape(rows.shape[0] * 2, rows.shape[2])).astype(BF16)


def choose_kernel(grads, pick, out):
    out[...] = choose(pick, grads, slice(None))


def rotate_out_kernel(grads, pick, basis_out, early, acc):
    experts, cap, _ = acc.shape
    done = early.shape[1]
    for e in range(experts):
        acc[e] = dot(early[e * cap : (e + 1) * cap, :], basis_out[e, :done, :])
    for at in range(done, grads.shape[2], CHUNK):
        cols = pl.ds(at, CHUNK)
        chosen = choose(pick, grads, cols)
        for e in range(experts):
            acc[e] += dot(chosen[e * cap : (e + 1) * cap], basis_out[e, cols, :])


def split_out_kernel(acc, keep, send):
    experts, cap, width = acc.shape
    core = lax.rem(lax.axis_index("tensor"), 2)
    at = 0
    for x in range(width // 256):
        for e in range(experts):
            for ref, which in ((keep, core), (send, 1 - core)):
                ref[at : at + cap, :] = acc[
                    e, :, pl.ds(pl.multiple_of((2 * x + which) * 128, 128), 128)
                ]
            at += cap


def fill(ref, start):
    if start < ref.shape[0]:
        ref[start:, :] = jnp.zeros((ref.shape[0] - start, ref.shape[1]), ref.dtype)


def pair_in_kernel(kept, got, label, *pays):
    slab = kept.shape[0] // len(pays)
    d = lax.axis_index("dp")
    for k, pay in enumerate(pays):
        rows = pl.ds(pl.multiple_of((d ^ k) * slab, 16), slab)
        pay[:slab, :] = (kept[rows, :] + got[rows, :]).astype(BF16)
        pay[slab : slab + LABEL_ROWS, :] = label[...]
        fill(pay, slab + LABEL_ROWS)


def pair_out_kernel(kept, got, keep, send):
    outer = keep.shape[0]
    x = lax.div(lax.axis_index("tensor"), 2)
    mine = pl.ds(pl.multiple_of(x * outer, 16), outer)
    keep[...] = kept[mine, :] + got[mine, :]
    other = pl.ds(pl.multiple_of((1 - x) * outer, 16), outer)
    send[...] = (kept[other, :] + got[other, :]).astype(BF16)


def round_kernel(kept, got, out, *pays):
    rows = (kept[...] + got[...].astype(F32)).astype(BF16)
    cap = rows.shape[0] // 2
    out[...] = rows
    for pay, e in zip(pays, (1, 0, 0)):
        pay[:cap, :] = rows[e * cap : (e + 1) * cap]
        fill(pay, cap)


def stack_kernel(slab, *refs):
    *pieces, out = refs
    for k, piece in enumerate(pieces):
        out[k * slab : (k + 1) * slab, :] = piece[:slab, :]


def sum_kernel(near, far, out):
    out[...] = (near[...].astype(F32) + far[...].astype(F32)).astype(BF16)


def mask_kernel(mine, other, *refs):
    *pieces, out = refs
    experts, dp = out.shape[0], len(pieces)
    half = mine.shape[0] // (dp * experts)
    slab = experts * half
    core = lax.rem(lax.axis_index("tensor"), 2)
    for e in range(experts):
        rows, labels = [], []
        for which, ref in ((core, mine), (1 - core, other)):
            for k, piece in enumerate(pieces):
                at = (k * experts + e) * half
                rows.append(ref[at : at + half, :])
                label = piece[slab : slab + LABEL_ROWS, :].astype(F32)
                label = label[2 * e : 2 * e + 2, :half]
                labels.append(jnp.where(which == 0, label[0:1], label[1:2]))
        rows = jnp.concatenate(rows, axis=0).astype(F32)
        labels = jnp.concatenate(labels, axis=1)
        labels = jnp.broadcast_to(labels, (128, labels.shape[1])).T
        for n in range(dp):
            out[e, :, n * 128 : (n + 1) * 128] = jnp.where(
                labels == float(n + 1), rows, 0.0
            ).astype(BF16)


def blocks_kernel(counts, masked, own, near, *refs):
    *far, result, final, sems = refs
    experts = masked.shape[0]
    cap = own.shape[0] // experts
    half = cap // 2
    core = lax.rem(lax.axis_index("tensor"), 2)
    copies = []
    for e in range(experts):
        sources = [(own, e * cap), (near, e * cap)] + [(x, 0) for x in far[2 * e : 2 * e + 2]]
        rows = [
            ref[pl.ds(pl.multiple_of(at + which * half, 16), half), :]
            for which in (core, 1 - core)
            for ref, at in sources
        ]
        blocks = dot(jnp.concatenate(rows, axis=0).T, masked[e])
        squares = blocks * blocks
        summed = squares[:, :128]
        for at in range(128, squares.shape[1], 128):
            summed = summed + squares[:, at : at + 128]
        final[e] = summed / counts[e].astype(F32)
        copies.append(pltpu.make_async_copy(final.at[e], result.at[e], sems.at[e]))
        copies[-1].start()
    for copy in copies:
        copy.wait()


def call(kernel, name, out_shape, specs=None, scratch=(), out_specs=None, flops=1, after=()):
    vmem = pl.BlockSpec(memory_space=pltpu.VMEM)
    given = {} if out_specs is None else {"out_specs": out_specs}

    def run(*args):
        def body(*refs):
            kernel(*refs[: len(args)], *refs[len(args) + len(after) :])

        return pl.pallas_call(
            body,
            out_shape=out_shape,
            in_specs=(specs or [vmem] * len(args)) + [vmem] * len(after),
            scratch_shapes=scratch,
            compiler_params=pltpu.CompilerParams(vmem_limit_bytes=VMEM),
            cost_estimate=pl.CostEstimate(flops=flops, bytes_accessed=1, transcendentals=0),
            name=name,
            **given,
        )(*args, *after)

    return run


def fast(acts, grads, routes, example_ids, expert_counts, basis_in, basis_out):
    tokens = acts.shape[0]
    experts, features, width = basis_in.shape
    cap = tokens // 2
    dp = lax.axis_size("dp")
    wide = experts * cap
    half = wide * width // 256
    hbm = pl.BlockSpec(memory_space=pltpu.HBM)
    vmem = pl.BlockSpec(memory_space=pltpu.VMEM)
    smem = pl.BlockSpec(memory_space=pltpu.SMEM)

    def pin(x):
        return pltpu.with_memory_space_constraint(x, pltpu.HBM)

    def rows(count, dtype):
        return jax.ShapeDtypeStruct((count, 128), dtype)

    core = [(t, t ^ 1) for t in range(4)]
    across = [(t, t ^ 2) for t in range(4)]

    def swap(x, k):
        return lax.ppermute(x, "dp", [(d, d ^ k) for d in range(dp)])

    partial = jax.ShapeDtypeStruct((experts, cap, width), F32)
    acc, label, pick, early = call(
        rotate_in_kernel,
        "rotate_in",
        (
            partial,
            rows(LABEL_ROWS, BF16),
            jax.ShapeDtypeStruct((wide, 2 * tokens), BF16),
            jax.ShapeDtypeStruct((tokens, 2, EARLY), BF16),
        ),
        [hbm] * 5,
        [
            pltpu.VMEM(acts.shape, BF16),
            pltpu.VMEM((2, tokens), jnp.int32),
            pltpu.VMEM((tokens,), jnp.int32),
            pltpu.VMEM(basis_in.shape, BF16),
            pltpu.SemaphoreType.DMA((3 + 2 * PARTS,)),
        ],
    )(pin(acts), pin(routes.T), pin(example_ids), pin(basis_in), pin(grads))
    keep, send = call(
        split_in_kernel, "split_in", (rows(half, F32), rows(half, F32)), flops=8 * 10**9
    )(acc)
    got = lax.ppermute(send, "tensor", core)
    early = call(choose_kernel, "choose", jax.ShapeDtypeStruct((wide, EARLY), BF16))(early, pick)
    slab = half // dp
    pieces = call(
        pair_in_kernel,
        "pair_in",
        [rows(slab + LABEL_ROWS + extra, BF16) for extra in (0, 0, 32, 16)],
        after=[early],
    )(keep, got, label)
    arrived = [pieces[0]] + [swap(pieces[k], k) for k in range(1, dp)]

    acc = call(rotate_out_kernel, "rotate_out", partial, after=[pieces[0]])(
        grads, pick, basis_out, early
    )
    keep, send = call(
        split_out_kernel, "split_out", (rows(half, F32), rows(half, F32)), after=arrived[1:]
    )(acc)
    got = lax.ppermute(send, "tensor", core)
    near = call(functools.partial(stack_kernel, slab), "stack_in", rows(half, BF16))(*arrived)
    far = lax.ppermute(near, "tensor", across)
    keep, send = call(pair_out_kernel, "pair_out", (rows(wide, F32), rows(wide, BF16)))(keep, got)
    got = lax.ppermute(send, "tensor", across)
    mine = call(sum_kernel, "sum_in", rows(half, BF16))(near, far)
    other = lax.ppermute(mine, "tensor", core)
    out, second, first2, first3 = call(
        round_kernel,
        "round_out",
        [rows(wide, BF16)] + [rows(cap + extra, BF16) for extra in (16, 48, 32)],
    )(keep, got)
    second2 = swap(second, 2)
    outs = [out, swap(out, 1), swap(first2, 2), swap(first3, 3), second2, swap(second2, 1)]
    masked = call(
        mask_kernel, "mask_in", jax.ShapeDtypeStruct((experts, dp * cap, dp * 128), BF16)
    )(mine, other, *arrived)
    result = jax.ShapeDtypeStruct((experts, 128, 128), F32)
    return call(
        blocks_kernel,
        "blocks",
        result,
        [smem] + [vmem] * (1 + len(outs)),
        scratch=[pltpu.VMEM(result.shape, F32), pltpu.SemaphoreType.DMA((experts,))],
        out_specs=hbm,
    )(expert_counts, masked, *outs)


EX_DEV = 1


def compact(routes, expert, capacity):
    tok_count = routes.shape[0]
    second_hit = routes[:, 1] == expert
    routed = (routes[:, 0] == expert) | second_hit
    order = jnp.cumsum(routed.astype(jnp.int32)) - 1
    slots = jnp.arange(capacity, dtype=jnp.int32)
    match = routed[None, :] & (order[None, :] == slots[:, None])
    token_index = jnp.arange(tok_count, dtype=jnp.int32)
    positions = jnp.sum(jnp.where(match, token_index[None, :], 0), axis=1)
    filled = jnp.any(match, axis=1)
    return (positions, filled, second_hit[positions])


def general(acts, grads, routes, example_ids, expert_counts, basis_in, basis_out):
    capacity = acts.shape[0] // 2
    experts = basis_in.shape[0]
    parts_in, parts_out, label_rows = ([], [], [])
    for expert in range(experts):
        positions, filled, second = compact(routes, expert, capacity)
        chosen = grads[positions]
        grad_rows = jnp.where(second[:, None], chosen[:, 1, :], chosen[:, 0, :])
        parts_in.append(
            jnp.dot(acts[positions], basis_in[expert], preferred_element_type=jnp.float32)
        )
        parts_out.append(jnp.dot(grad_rows, basis_out[expert], preferred_element_type=jnp.float32))
        label_rows.append(jnp.where(filled, example_ids[positions], -1))
    part_in = jnp.stack(parts_in)
    part_out = jnp.stack(parts_out)
    labels = jnp.stack(label_rows)
    slice_width = basis_out.shape[2] // lax.axis_size("tensor")
    summed_in, summed_out = lax.psum((part_in, part_out), "tensor")
    rot_in = summed_in.astype(jnp.bfloat16)
    rot_out = lax.dynamic_slice_in_dim(
        summed_out.astype(jnp.bfloat16), lax.axis_index("tensor") * slice_width, slice_width, 2
    )
    owned_count = EX_DEV
    wanted = jnp.arange(lax.axis_size("dp") * owned_count, dtype=jnp.int32)
    onehot = (labels[:, :, None] == wanted[None, None, :]).astype(jnp.bfloat16)
    spread = onehot[:, :, :, None] * rot_out[:, :, None, :]
    owned_sums = lax.psum_scatter(
        jnp.einsum("ecnw,eca->newa", spread, rot_in, preferred_element_type=jnp.float32),
        "dp",
        scatter_dimension=0,
        tiled=True,
    )
    squared = jnp.sum(owned_sums * owned_sums, axis=0)
    totals = lax.psum_scatter(squared, "dp", scatter_dimension=2, tiled=True)
    return totals / expert_counts.astype(jnp.float32)[:, None, None]


def shards(*args):
    experts, _, width = args[5].shape
    sizes = (lax.axis_size("dp"), lax.axis_size("tensor"), experts, width)
    fits = sizes == (4, 4, 2, 512) and args[0].shape[0] == 384
    return (fast if fits else general)(*args)


def solution(mesh):
    placed = (
        P(("group", "dp"), "tensor"),
        P(("group", "dp"), None, "tensor"),
        P(("group", "dp"), None),
        P(("group", "dp")),
        P("group"),
        P(None, "tensor", None),
        P(None, "tensor", None),
    )
    return jax.shard_map(
        shards, mesh=mesh, in_specs=placed, out_specs=P("group", "tensor", "dp"), check_vma=False
    )
```

```python
import functools

import jax
import jax.numpy as jnp
from jax import lax
from jax.experimental import pallas as pl
from jax.experimental.pallas import tpu as pltpu
from jax.sharding import PartitionSpec as P

F32 = jnp.float32
BF16 = jnp.bfloat16
CHUNK = 1024
PARTS = 3
VMEM = 20 * 2**20
LABEL_ROWS = 16


def iota(shape, dim):
    return lax.broadcasted_iota(jnp.int32, shape, dim)


def dot(a, b):
    return jnp.dot(a, b, preferred_element_type=F32)


def fetcher(sems):
    count = iter(range(sems.shape[0]))

    def fetch(src, dst):
        copy = pltpu.make_async_copy(src, dst, sems.at[next(count)])
        copy.start()
        return copy

    return fetch


def rotate_in_kernel(
    acts, routes, ids, basis_in,
    acc, label, pick,
    acts_v, routes_v, ids_v, basis_v, sems,
):
    tokens, features = acts.shape
    experts = basis_in.shape[0]
    cap = tokens // 2
    parts = [pl.ds(at, features // PARTS) for at in range(0, features, features // PARTS)]
    fetch = fetcher(sems)
    first = [fetch(routes, routes_v), fetch(ids, ids_v)]
    acts_in = [fetch(acts.at[:, part], acts_v.at[:, part]) for part in parts]
    bases = [fetch(basis_in.at[:, part, :], basis_v.at[:, part, :]) for part in parts]
    for copy in first:
        copy.wait()
    hits = [
        jnp.max((routes_v[...] == e).astype(F32), axis=0, keepdims=True) for e in range(experts)
    ]
    rows = jnp.concatenate(hits + [jnp.zeros((8 - experts, tokens), F32)], axis=0).astype(BF16)
    upto = (iota((tokens, tokens), 0) <= iota((tokens, tokens), 1)).astype(BF16)
    order = dot(rows, upto)
    slots = iota((cap, tokens), 0).astype(F32) + 1.0
    pick_in = jnp.concatenate(
        [((order[e : e + 1] == slots) & (hits[e] > 0.5)).astype(BF16) for e in range(experts)],
        axis=0,
    )
    repeat = (iota((tokens, 2 * tokens), 0) == iota((tokens, 2 * tokens), 1) // 2).astype(BF16)
    wide = dot(
        jnp.concatenate(
            [order[:experts], routes_v[...].astype(F32), jnp.zeros((6 - experts, tokens), F32)],
            axis=0,
        ).astype(BF16),
        repeat,
    )
    odd = iota((1, 2 * tokens), 1) % 2 == 1
    routed_to = jnp.where(odd, wide[experts + 1 : experts + 2], wide[experts : experts + 1])
    slots = iota((cap, 2 * tokens), 0).astype(F32) + 1.0
    for e in range(experts):
        pick[e * cap : (e + 1) * cap, :] = (
            (wide[e : e + 1] == slots) & (routed_to == float(e))
        ).astype(BF16)
    numbers = jnp.broadcast_to(ids_v[...].reshape(1, tokens).astype(F32) + 1.0, (8, tokens)).astype(BF16)
    named = lax.dot_general(numbers, pick_in, (((1,), (1,)), ((), ())), preferred_element_type=F32)
    block = jnp.zeros((LABEL_ROWS, 128), F32)
    row = iota((LABEL_ROWS, 128), 0)
    half = cap // 2
    for at in range(2 * experts):
        mine = named[0:1, at * half : (at + 1) * half]
        mine = jnp.concatenate([mine, jnp.zeros((1, 128 - half), F32)], axis=1)
        block = jnp.where(row == at, mine, block)
    label[...] = block.astype(BF16)

    chosen = []
    for part, copy in zip(parts, acts_in):
        copy.wait()
        chosen.append(dot(pick_in, acts_v[:, part]).astype(BF16))
    for n, part in enumerate(parts):
        bases[n].wait()
        for e in range(experts):
            more = dot(chosen[n][e * cap : (e + 1) * cap], basis_v[e, part, :])
            acc[e] = more if n == 0 else acc[e] + more


def split_in_kernel(acc, keep, send):
    experts, cap, width = acc.shape
    core = lax.rem(lax.axis_index("tensor"), 2)
    half = cap // 2
    at = 0
    for q in range(width // 128):
        for e in range(experts):
            for ref, which in ((keep, core), (send, 1 - core)):
                ref[at : at + half, :] = acc[
                    e, pl.ds(pl.multiple_of(which * half, 8), half), q * 128 : (q + 1) * 128
                ]
            at += half


def rotate_out_kernel(grads, pick, basis_out, acc):
    tokens, _, hidden = grads.shape
    experts, cap, _ = acc.shape
    for at in range(0, hidden, CHUNK):
        cols = pl.ds(at, CHUNK)
        chosen = dot(pick[...], grads[:, :, cols].reshape(2 * tokens, CHUNK)).astype(BF16)
        for e in range(experts):
            part = dot(chosen[e * cap : (e + 1) * cap], basis_out[e, cols, :])
            acc[e] = part if at == 0 else acc[e] + part


def split_out_kernel(acc, keep, send):
    experts, cap, width = acc.shape
    core = lax.rem(lax.axis_index("tensor"), 2)
    at = 0
    for x in range(width // 256):
        for e in range(experts):
            for ref, which in ((keep, core), (send, 1 - core)):
                ref[at : at + cap, :] = acc[
                    e, :, pl.ds(pl.multiple_of((2 * x + which) * 128, 128), 128)
                ]
            at += cap


def fill(ref, start):
    if start < ref.shape[0]:
        ref[start:, :] = jnp.zeros((ref.shape[0] - start, ref.shape[1]), ref.dtype)


def pair_in_kernel(kept, got, label, *pays):
    slab = kept.shape[0] // len(pays)
    d = lax.axis_index("dp")
    for k, pay in enumerate(pays):
        rows = pl.ds(pl.multiple_of((d ^ k) * slab, 16), slab)
        pay[:slab, :] = (kept[rows, :] + got[rows, :]).astype(BF16)
        pay[slab : slab + LABEL_ROWS, :] = label[...]
        fill(pay, slab + LABEL_ROWS)


def pair_out_kernel(kept, got, keep, send):
    outer = keep.shape[0]
    x = lax.div(lax.axis_index("tensor"), 2)
    mine = pl.ds(pl.multiple_of(x * outer, 16), outer)
    keep[...] = kept[mine, :] + got[mine, :]
    other = pl.ds(pl.multiple_of((1 - x) * outer, 16), outer)
    send[...] = (kept[other, :] + got[other, :]).astype(BF16)


def round_kernel(kept, got, *pays):
    outer = kept.shape[0]
    rows = (kept[...] + got[...].astype(F32)).astype(BF16)
    for pay in pays:
        pay[:outer, :] = rows
        fill(pay, outer)


def stack_kernel(slab, *refs):
    *pieces, out = refs
    for k, piece in enumerate(pieces):
        out[k * slab : (k + 1) * slab, :] = piece[:slab, :]


def sum_kernel(near, far, *outs):
    piece = outs[0].shape[0]
    for n, out in enumerate(outs):
        rows = pl.ds(n * piece, piece)
        out[...] = (near[rows, :].astype(F32) + far[rows, :].astype(F32)).astype(BF16)


def mask_kernel(counts, *refs):
    mine, other, pieces = refs[:2], refs[2:4], refs[4:-2]
    out, divisor = refs[-2:]
    experts, dp = out.shape[0], len(pieces)
    half = 2 * mine[0].shape[0] // (dp * experts)
    slab = experts * half
    core = lax.rem(lax.axis_index("tensor"), 2)
    for e in range(experts):
        divisor[e] = jnp.full(divisor.shape[1:], counts[e].astype(F32), F32)
        rows, labels = [], []
        for which, refs in ((core, mine), (1 - core, other)):
            for k, piece in enumerate(pieces):
                at = (k % (dp // 2) * experts + e) * half
                rows.append(refs[k // (dp // 2)][at : at + half, :])
                label = piece[slab : slab + LABEL_ROWS, :].astype(F32)
                label = label[2 * e : 2 * e + 2, :half]
                labels.append(jnp.where(which == 0, label[0:1], label[1:2]))
        rows = jnp.concatenate(rows, axis=0).astype(F32)
        labels = jnp.concatenate(labels, axis=1)
        labels = jnp.broadcast_to(labels, (128, labels.shape[1])).T
        for n in range(dp):
            out[e, :, n * 128 : (n + 1) * 128] = jnp.where(
                labels == float(n + 1), rows, 0.0
            ).astype(BF16)


def blocks_kernel(divisor, masked, *refs):
    *outs, result, final, sems = refs
    experts, slots, _ = masked.shape
    half = slots // (2 * len(outs))
    core = lax.rem(lax.axis_index("tensor"), 2)
    copies = []
    for e in range(experts):
        rows = [
            ref[pl.ds(pl.multiple_of((2 * e + which) * half, 16), half), :]
            for which in (core, 1 - core)
            for ref in outs
        ]
        blocks = dot(jnp.concatenate(rows, axis=0).T, masked[e])
        squares = blocks * blocks
        summed = squares[:, :128]
        for at in range(128, squares.shape[1], 128):
            summed = summed + squares[:, at : at + 128]
        final[e] = summed / divisor[e][:1]
        copies.append(pltpu.make_async_copy(final.at[e], result.at[e], sems.at[e]))
        copies[-1].start()
    for copy in copies:
        copy.wait()


def call(kernel, name, out_shape, specs=None, scratch=(), out_specs=None, flops=1, after=()):
    vmem = pl.BlockSpec(memory_space=pltpu.VMEM)
    given = {} if out_specs is None else {"out_specs": out_specs}

    def run(*args):
        def body(*refs):
            kernel(*refs[: len(args)], *refs[len(args) + len(after) :])

        return pl.pallas_call(
            body,
            out_shape=out_shape,
            in_specs=(specs or [vmem] * len(args)) + [vmem] * len(after),
            scratch_shapes=scratch,
            compiler_params=pltpu.CompilerParams(vmem_limit_bytes=VMEM),
            cost_estimate=pl.CostEstimate(flops=flops, bytes_accessed=1, transcendentals=0),
            name=name,
            **given,
        )(*args, *after)

    return run


def fast(acts, grads, routes, example_ids, expert_counts, basis_in, basis_out):
    tokens = acts.shape[0]
    experts, features, width = basis_in.shape
    cap = tokens // 2
    dp = lax.axis_size("dp")
    wide = experts * cap
    half = wide * width // 256
    hbm = pl.BlockSpec(memory_space=pltpu.HBM)
    vmem = pl.BlockSpec(memory_space=pltpu.VMEM)
    smem = pl.BlockSpec(memory_space=pltpu.SMEM)

    def pin(x):
        return pltpu.with_memory_space_constraint(x, pltpu.HBM)

    def rows(count, dtype):
        return jax.ShapeDtypeStruct((count, 128), dtype)

    core = [(t, t ^ 1) for t in range(4)]
    across = [(t, t ^ 2) for t in range(4)]

    def swap(x, k):
        return lax.ppermute(x, "dp", [(d, d ^ k) for d in range(dp)])

    partial = jax.ShapeDtypeStruct((experts, cap, width), F32)
    acc, label, pick = call(
        rotate_in_kernel,
        "rotate_in",
        (
            partial,
            rows(LABEL_ROWS, BF16),
            jax.ShapeDtypeStruct((wide, 2 * tokens), BF16),
        ),
        [hbm] * 4,
        [
            pltpu.VMEM(acts.shape, BF16),
            pltpu.VMEM((2, tokens), jnp.int32),
            pltpu.VMEM((tokens,), jnp.int32),
            pltpu.VMEM(basis_in.shape, BF16),
            pltpu.SemaphoreType.DMA((3 + 2 * PARTS,)),
        ],
    )(pin(acts), pin(routes.T), pin(example_ids), pin(basis_in))
    keep, send = call(
        split_in_kernel, "split_in", (rows(half, F32), rows(half, F32)), flops=8 * 10**9
    )(acc)
    got = lax.ppermute(send, "tensor", core)
    slab = half // dp
    pieces = call(
        pair_in_kernel,
        "pair_in",
        [rows(slab + LABEL_ROWS + extra, BF16) for extra in (0, 0, 32, 16)],
    )(keep, got, label)
    arrived = [pieces[0]] + [swap(pieces[k], k) for k in range(1, dp)]

    acc = call(rotate_out_kernel, "rotate_out", partial, after=[pieces[0]])(
        grads, pick, basis_out
    )
    keep, send = call(
        split_out_kernel, "split_out", (rows(half, F32), rows(half, F32)), after=arrived[1:]
    )(acc)
    got = lax.ppermute(send, "tensor", core)
    keep, send = call(pair_out_kernel, "pair_out", (rows(wide, F32), rows(wide, BF16)))(keep, got)
    got = lax.ppermute(send, "tensor", across)
    outs = call(
        round_kernel, "round_out", [rows(wide + extra, BF16) for extra in (0, 16, 48, 32)]
    )(keep, got)
    outs = [outs[0]] + [swap(outs[k], k) for k in range(1, dp)]

    near = call(
        functools.partial(stack_kernel, slab), "stack_in", rows(half, BF16), after=[got]
    )(*arrived)
    far = lax.ppermute(near, "tensor", across)
    mine = call(sum_kernel, "sum_in", [rows(half // 2, BF16)] * 2)(near, far)
    other = [lax.ppermute(x, "tensor", core) for x in mine]
    masked, divisor = call(
        mask_kernel,
        "mask_in",
        (
            jax.ShapeDtypeStruct((experts, dp * cap, dp * 128), BF16),
            jax.ShapeDtypeStruct((experts, 8, 128), F32),
        ),
        [smem] + [vmem] * (4 + dp),
    )(expert_counts, *mine, *other, *arrived)
    result = jax.ShapeDtypeStruct((experts, 128, 128), F32)
    return call(
        blocks_kernel,
        "blocks",
        result,
        scratch=[pltpu.VMEM(result.shape, F32), pltpu.SemaphoreType.DMA((experts,))],
        out_specs=hbm,
    )(divisor, masked, *outs)


EX_DEV = 1


def compact(routes, expert, capacity):
    tok_count = routes.shape[0]
    second_hit = routes[:, 1] == expert
    routed = (routes[:, 0] == expert) | second_hit
    order = jnp.cumsum(routed.astype(jnp.int32)) - 1
    slots = jnp.arange(capacity, dtype=jnp.int32)
    match = routed[None, :] & (order[None, :] == slots[:, None])
    token_index = jnp.arange(tok_count, dtype=jnp.int32)
    positions = jnp.sum(jnp.where(match, token_index[None, :], 0), axis=1)
    filled = jnp.any(match, axis=1)
    return (positions, filled, second_hit[positions])


def general(acts, grads, routes, example_ids, expert_counts, basis_in, basis_out):
    capacity = acts.shape[0] // 2
    experts = basis_in.shape[0]
    parts_in, parts_out, label_rows = ([], [], [])
    for expert in range(experts):
        positions, filled, second = compact(routes, expert, capacity)
        chosen = grads[positions]
        grad_rows = jnp.where(second[:, None], chosen[:, 1, :], chosen[:, 0, :])
        parts_in.append(
            jnp.dot(acts[positions], basis_in[expert], preferred_element_type=jnp.float32)
        )
        parts_out.append(jnp.dot(grad_rows, basis_out[expert], preferred_element_type=jnp.float32))
        label_rows.append(jnp.where(filled, example_ids[positions], -1))
    part_in = jnp.stack(parts_in)
    part_out = jnp.stack(parts_out)
    labels = jnp.stack(label_rows)
    slice_width = basis_out.shape[2] // lax.axis_size("tensor")
    summed_in, summed_out = lax.psum((part_in, part_out), "tensor")
    rot_in = summed_in.astype(jnp.bfloat16)
    rot_out = lax.dynamic_slice_in_dim(
        summed_out.astype(jnp.bfloat16), lax.axis_index("tensor") * slice_width, slice_width, 2
    )
    owned_count = EX_DEV
    wanted = jnp.arange(lax.axis_size("dp") * owned_count, dtype=jnp.int32)
    onehot = (labels[:, :, None] == wanted[None, None, :]).astype(jnp.bfloat16)
    spread = onehot[:, :, :, None] * rot_out[:, :, None, :]
    owned_sums = lax.psum_scatter(
        jnp.einsum("ecnw,eca->newa", spread, rot_in, preferred_element_type=jnp.float32),
        "dp",
        scatter_dimension=0,
        tiled=True,
    )
    squared = jnp.sum(owned_sums * owned_sums, axis=0)
    totals = lax.psum_scatter(squared, "dp", scatter_dimension=2, tiled=True)
    return totals / expert_counts.astype(jnp.float32)[:, None, None]


def shards(*args):
    experts, _, width = args[5].shape
    sizes = (lax.axis_size("dp"), lax.axis_size("tensor"), experts, width)
    fits = sizes == (4, 4, 2, 512) and args[0].shape[0] == 384
    return (fast if fits else general)(*args)


def solution(mesh):
    placed = (
        P(("group", "dp"), "tensor"),
        P(("group", "dp"), None, "tensor"),
        P(("group", "dp"), None),
        P(("group", "dp")),
        P("group"),
        P(None, "tensor", None),
        P(None, "tensor", None),
    )
    return jax.shard_map(
        shards, mesh=mesh, in_specs=placed, out_specs=P("group", "tensor", "dp"), check_vma=False
    )
```

```python
import functools

import jax
import jax.numpy as jnp
from jax import lax
from jax.experimental import pallas as pl
from jax.experimental.pallas import tpu as pltpu
from jax.sharding import PartitionSpec as P

F32 = jnp.float32
BF16 = jnp.bfloat16
CHUNK = 1024
VMEM = 20 * 2**20
FAR_FIRST = (2, 3, 1)
LABEL_ROWS = 16


def iota(shape, dim):
    return lax.broadcasted_iota(jnp.int32, shape, dim)


def dot(a, b):
    return jnp.dot(a, b, preferred_element_type=F32)


def fetcher(sems):
    count = iter(range(sems.shape[0]))

    def fetch(src, dst):
        copy = pltpu.make_async_copy(src, dst, sems.at[next(count)])
        copy.start()
        return copy

    return fetch


def rotate_in_kernel(
    acts, routes, ids, basis_in,
    acc, label, pick,
    acts_v, routes_v, ids_v, basis_v, sems,
):
    tokens = acts.shape[0]
    experts = basis_in.shape[0]
    cap = tokens // 2
    fetch = fetcher(sems)
    first = [fetch(routes, routes_v), fetch(ids, ids_v)]
    acts_in = fetch(acts, acts_v)
    bases = [fetch(basis_in.at[e], basis_v.at[e]) for e in range(experts)]
    for copy in first:
        copy.wait()
    hits = [
        jnp.max((routes_v[...] == e).astype(F32), axis=0, keepdims=True) for e in range(experts)
    ]
    rows = jnp.concatenate(hits + [jnp.zeros((8 - experts, tokens), F32)], axis=0).astype(BF16)
    upto = (iota((tokens, tokens), 0) <= iota((tokens, tokens), 1)).astype(BF16)
    order = dot(rows, upto)
    slots = iota((cap, tokens), 0).astype(F32) + 1.0
    pick_in = jnp.concatenate(
        [((order[e : e + 1] == slots) & (hits[e] > 0.5)).astype(BF16) for e in range(experts)],
        axis=0,
    )
    repeat = (iota((tokens, 2 * tokens), 0) == iota((tokens, 2 * tokens), 1) // 2).astype(BF16)
    wide = dot(
        jnp.concatenate(
            [order[:experts], routes_v[...].astype(F32), jnp.zeros((6 - experts, tokens), F32)],
            axis=0,
        ).astype(BF16),
        repeat,
    )
    odd = iota((1, 2 * tokens), 1) % 2 == 1
    routed_to = jnp.where(odd, wide[experts + 1 : experts + 2], wide[experts : experts + 1])
    slots = iota((cap, 2 * tokens), 0).astype(F32) + 1.0
    for e in range(experts):
        pick[e * cap : (e + 1) * cap, :] = (
            (wide[e : e + 1] == slots) & (routed_to == float(e))
        ).astype(BF16)
    numbers = jnp.broadcast_to(ids_v[...].reshape(1, tokens).astype(F32) + 1.0, (8, tokens)).astype(BF16)
    named = lax.dot_general(numbers, pick_in, (((1,), (1,)), ((), ())), preferred_element_type=F32)
    block = jnp.zeros((LABEL_ROWS, 128), F32)
    row = iota((LABEL_ROWS, 128), 0)
    half = cap // 2
    for at in range(2 * experts):
        mine = named[0:1, at * half : (at + 1) * half]
        mine = jnp.concatenate([mine, jnp.zeros((1, 128 - half), F32)], axis=1)
        block = jnp.where(row == at, mine, block)
    label[...] = block.astype(BF16)

    acts_in.wait()
    chosen = dot(pick_in, acts_v[...]).astype(BF16)
    for e in range(experts):
        bases[e].wait()
        acc[e] = dot(chosen[e * cap : (e + 1) * cap], basis_v[e])


def split_in_kernel(acc, keep, send):
    experts, cap, width = acc.shape
    core = lax.rem(lax.axis_index("tensor"), 2)
    half = cap // 2
    at = 0
    for q in range(width // 128):
        for e in range(experts):
            for ref, which in ((keep, core), (send, 1 - core)):
                ref[at : at + half, :] = acc[
                    e, pl.ds(pl.multiple_of(which * half, 8), half), q * 128 : (q + 1) * 128
                ]
            at += half


def rotate_out_kernel(grads, pick, basis_out, acc):
    tokens, _, hidden = grads.shape
    experts, cap, _ = acc.shape
    for at in range(0, hidden, CHUNK):
        cols = pl.ds(at, CHUNK)
        chosen = dot(pick[...], grads[:, :, cols].reshape(2 * tokens, CHUNK)).astype(BF16)
        for e in range(experts):
            part = dot(chosen[e * cap : (e + 1) * cap], basis_out[e, cols, :])
            acc[e] = part if at == 0 else acc[e] + part


def split_out_kernel(acc, keep, send):
    experts, cap, width = acc.shape
    core = lax.rem(lax.axis_index("tensor"), 2)
    at = 0
    for x in range(width // 256):
        for e in range(experts):
            for ref, which in ((keep, core), (send, 1 - core)):
                ref[at : at + cap, :] = acc[
                    e, :, pl.ds(pl.multiple_of((2 * x + which) * 128, 128), 128)
                ]
            at += cap


def pair_in_kernel(kept, got, label, *pays):
    slab = kept.shape[0] // len(pays)
    d = lax.axis_index("dp")
    for k, pay in enumerate(pays):
        rows = pl.ds(pl.multiple_of((d ^ k) * slab, 16), slab)
        pay[:slab, :] = (kept[rows, :] + got[rows, :]).astype(BF16)
        pay[slab:, :] = label[...]


def pair_out_kernel(kept, got, keep, send):
    outer = keep.shape[0]
    x = lax.div(lax.axis_index("tensor"), 2)
    mine = pl.ds(pl.multiple_of(x * outer, 16), outer)
    keep[...] = kept[mine, :] + got[mine, :]
    other = pl.ds(pl.multiple_of((1 - x) * outer, 16), outer)
    send[...] = (kept[other, :] + got[other, :]).astype(BF16)


def round_kernel(kept, got, out):
    outer = kept.shape[0]
    out[:outer, :] = (kept[...] + got[...].astype(F32)).astype(BF16)
    out[outer:, :] = jnp.zeros((out.shape[0] - outer, 128), BF16)


def stack_kernel(slab, *refs):
    *pieces, out = refs
    for k, piece in enumerate(pieces):
        out[k * slab : (k + 1) * slab, :] = piece[:slab, :]


def sum_kernel(near, far, *outs):
    piece = outs[0].shape[0]
    for n, out in enumerate(outs):
        rows = pl.ds(n * piece, piece)
        out[...] = (near[rows, :].astype(F32) + far[rows, :].astype(F32)).astype(BF16)


def mask_kernel(counts, *refs):
    mine, other, pieces = refs[:2], refs[2:4], refs[4:-2]
    out, divisor = refs[-2:]
    experts, dp = out.shape[0], len(pieces)
    slab = 2 * mine[0].shape[0] // dp
    half = slab // experts
    core = lax.rem(lax.axis_index("tensor"), 2)
    for e in range(experts):
        divisor[e] = jnp.full(divisor.shape[1:], counts[e].astype(F32), F32)
        rows, labels = [], []
        for which, parts in ((core, mine), (1 - core, other)):
            for k, piece in enumerate(pieces):
                at = k % (dp // 2) * slab + e * half
                rows.append(parts[k // (dp // 2)][at : at + half, :])
                label = piece[slab:, :].astype(F32)[2 * e : 2 * e + 2, :half]
                labels.append(jnp.where(which == 0, label[0:1], label[1:2]))
        rows = jnp.concatenate(rows, axis=0).astype(F32)
        labels = jnp.concatenate(labels, axis=1)
        labels = jnp.broadcast_to(labels, (128, labels.shape[1])).T
        for n in range(dp):
            out[e, :, n * 128 : (n + 1) * 128] = jnp.where(
                labels == float(n + 1), rows, 0.0
            ).astype(BF16)


def blocks_kernel(divisor, masked, *refs):
    *outs, result, final, sems = refs
    experts, slots, _ = masked.shape
    half = slots // (2 * len(outs))
    core = lax.rem(lax.axis_index("tensor"), 2)
    copies = []
    for e in range(experts):
        rows = [
            ref[pl.ds(pl.multiple_of((2 * e + which) * half, 16), half), :]
            for which in (core, 1 - core)
            for ref in outs
        ]
        blocks = dot(jnp.concatenate(rows, axis=0).T, masked[e])
        squares = blocks * blocks
        summed = squares[:, :128]
        for at in range(128, squares.shape[1], 128):
            summed = summed + squares[:, at : at + 128]
        final[e] = summed / divisor[e][:1]
        copies.append(pltpu.make_async_copy(final.at[e], result.at[e], sems.at[e]))
        copies[-1].start()
    for copy in copies:
        copy.wait()


def call(kernel, name, out_shape, specs=None, scratch=(), out_specs=None, flops=1, after=()):
    vmem = pl.BlockSpec(memory_space=pltpu.VMEM)
    given = {} if out_specs is None else {"out_specs": out_specs}

    def run(*args):
        def body(*refs):
            kernel(*refs[: len(args)], *refs[len(args) + len(after) :])

        return pl.pallas_call(
            body,
            out_shape=out_shape,
            in_specs=(specs or [vmem] * len(args)) + [vmem] * len(after),
            scratch_shapes=scratch,
            compiler_params=pltpu.CompilerParams(vmem_limit_bytes=VMEM),
            cost_estimate=pl.CostEstimate(flops=flops, bytes_accessed=1, transcendentals=0),
            name=name,
            **given,
        )(*args, *after)

    return run


def fast(acts, grads, routes, example_ids, expert_counts, basis_in, basis_out):
    tokens = acts.shape[0]
    experts, features, width = basis_in.shape
    cap = tokens // 2
    dp = lax.axis_size("dp")
    wide = experts * cap
    half = wide * width // 256
    hbm = pl.BlockSpec(memory_space=pltpu.HBM)
    vmem = pl.BlockSpec(memory_space=pltpu.VMEM)
    smem = pl.BlockSpec(memory_space=pltpu.SMEM)

    def pin(x):
        return pltpu.with_memory_space_constraint(x, pltpu.HBM)

    def rows(count, dtype):
        return jax.ShapeDtypeStruct((count, 128), dtype)

    core = [(t, t ^ 1) for t in range(4)]
    across = [(t, t ^ 2) for t in range(4)]

    def swap(x, k):
        return lax.ppermute(x, "dp", [(d, d ^ k) for d in range(dp)])

    partial = jax.ShapeDtypeStruct((experts, cap, width), F32)
    acc, label, pick = call(
        rotate_in_kernel,
        "rotate_in",
        (
            partial,
            rows(LABEL_ROWS, BF16),
            jax.ShapeDtypeStruct((wide, 2 * tokens), BF16),
        ),
        [hbm] * 4,
        [
            pltpu.VMEM(acts.shape, BF16),
            pltpu.VMEM((2, tokens), jnp.int32),
            pltpu.VMEM((tokens,), jnp.int32),
            pltpu.VMEM(basis_in.shape, BF16),
            pltpu.SemaphoreType.DMA((3 + experts,)),
        ],
    )(pin(acts), pin(routes.T), pin(example_ids), pin(basis_in))
    keep, send = call(
        split_in_kernel, "split_in", (rows(half, F32), rows(half, F32)), flops=8 * 10**9
    )(acc)
    got = lax.ppermute(send, "tensor", core)
    slab = half // dp
    pieces = call(pair_in_kernel, "pair_in", [rows(slab + LABEL_ROWS, BF16)] * dp)(
        keep, got, label
    )
    arrived = [pieces[0]] + [swap(pieces[k], k) for k in FAR_FIRST]

    acc = call(rotate_out_kernel, "rotate_out", partial, after=[pieces[0]])(
        grads, pick, basis_out
    )
    keep, send = call(
        split_out_kernel, "split_out", (rows(half, F32), rows(half, F32)), after=arrived[1:]
    )(acc)
    got = lax.ppermute(send, "tensor", core)
    keep, send = call(pair_out_kernel, "pair_out", (rows(wide, F32), rows(wide, BF16)))(keep, got)
    got = lax.ppermute(send, "tensor", across)
    out = call(round_kernel, "round_out", rows(wide + 16, BF16))(keep, got)
    outs = [out] + [swap(out, k) for k in FAR_FIRST]

    near = call(
        functools.partial(stack_kernel, slab), "stack_in", rows(half, BF16), after=[got]
    )(*arrived)
    far = lax.ppermute(near, "tensor", across)
    mine = call(sum_kernel, "sum_in", [rows(half // 2, BF16)] * 2)(near, far)
    other = [lax.ppermute(x, "tensor", core) for x in mine]
    masked, divisor = call(
        mask_kernel,
        "mask_in",
        (
            jax.ShapeDtypeStruct((experts, dp * cap, dp * 128), BF16),
            jax.ShapeDtypeStruct((experts, 8, 128), F32),
        ),
        [smem] + [vmem] * (4 + dp),
    )(expert_counts, *mine, *other, *arrived)
    result = jax.ShapeDtypeStruct((experts, 128, 128), F32)
    return call(
        blocks_kernel,
        "blocks",
        result,
        scratch=[pltpu.VMEM(result.shape, F32), pltpu.SemaphoreType.DMA((experts,))],
        out_specs=hbm,
    )(divisor, masked, *outs)


EX_DEV = 1


def compact(routes, expert, capacity):
    tok_count = routes.shape[0]
    second_hit = routes[:, 1] == expert
    routed = (routes[:, 0] == expert) | second_hit
    order = jnp.cumsum(routed.astype(jnp.int32)) - 1
    slots = jnp.arange(capacity, dtype=jnp.int32)
    match = routed[None, :] & (order[None, :] == slots[:, None])
    token_index = jnp.arange(tok_count, dtype=jnp.int32)
    positions = jnp.sum(jnp.where(match, token_index[None, :], 0), axis=1)
    filled = jnp.any(match, axis=1)
    return (positions, filled, second_hit[positions])


def general(acts, grads, routes, example_ids, expert_counts, basis_in, basis_out):
    capacity = acts.shape[0] // 2
    experts = basis_in.shape[0]
    parts_in, parts_out, label_rows = ([], [], [])
    for expert in range(experts):
        positions, filled, second = compact(routes, expert, capacity)
        chosen = grads[positions]
        grad_rows = jnp.where(second[:, None], chosen[:, 1, :], chosen[:, 0, :])
        parts_in.append(
            jnp.dot(acts[positions], basis_in[expert], preferred_element_type=jnp.float32)
        )
        parts_out.append(jnp.dot(grad_rows, basis_out[expert], preferred_element_type=jnp.float32))
        label_rows.append(jnp.where(filled, example_ids[positions], -1))
    part_in = jnp.stack(parts_in)
    part_out = jnp.stack(parts_out)
    labels = jnp.stack(label_rows)
    slice_width = basis_out.shape[2] // lax.axis_size("tensor")
    summed_in, summed_out = lax.psum((part_in, part_out), "tensor")
    rot_in = summed_in.astype(jnp.bfloat16)
    rot_out = lax.dynamic_slice_in_dim(
        summed_out.astype(jnp.bfloat16), lax.axis_index("tensor") * slice_width, slice_width, 2
    )
    owned_count = EX_DEV
    wanted = jnp.arange(lax.axis_size("dp") * owned_count, dtype=jnp.int32)
    onehot = (labels[:, :, None] == wanted[None, None, :]).astype(jnp.bfloat16)
    spread = onehot[:, :, :, None] * rot_out[:, :, None, :]
    owned_sums = lax.psum_scatter(
        jnp.einsum("ecnw,eca->newa", spread, rot_in, preferred_element_type=jnp.float32),
        "dp",
        scatter_dimension=0,
        tiled=True,
    )
    squared = jnp.sum(owned_sums * owned_sums, axis=0)
    totals = lax.psum_scatter(squared, "dp", scatter_dimension=2, tiled=True)
    return totals / expert_counts.astype(jnp.float32)[:, None, None]


def shards(*args):
    experts, _, width = args[5].shape
    sizes = (lax.axis_size("dp"), lax.axis_size("tensor"), experts, width)
    fits = sizes == (4, 4, 2, 512) and args[0].shape[0] == 384
    return (fast if fits else general)(*args)


def solution(mesh):
    placed = (
        P(("group", "dp"), "tensor"),
        P(("group", "dp"), None, "tensor"),
        P(("group", "dp"), None),
        P(("group", "dp")),
        P("group"),
        P(None, "tensor", None),
        P(None, "tensor", None),
    )
    return jax.shard_map(
        shards, mesh=mesh, in_specs=placed, out_specs=P("group", "tensor", "dp"), check_vma=False
    )
```

```python
import functools

import jax
import jax.numpy as jnp
from jax import lax
from jax.experimental import pallas as pl
from jax.experimental.pallas import tpu as pltpu
from jax.sharding import PartitionSpec as P

F32 = jnp.float32
BF16 = jnp.bfloat16
CHUNK = 1024
VMEM = 20 * 2**20
FAR_FIRST = (2, 3, 1)
LABEL_ROWS = 16


def iota(shape, dim):
    return lax.broadcasted_iota(jnp.int32, shape, dim)


def dot(a, b):
    return jnp.dot(a, b, preferred_element_type=F32)


def fetcher(sems):
    count = iter(range(sems.shape[0]))

    def fetch(src, dst):
        copy = pltpu.make_async_copy(src, dst, sems.at[next(count)])
        copy.start()
        return copy

    return fetch


def rotate_in_kernel(
    acts, routes, ids, basis_in,
    acc, label, pick,
    acts_v, routes_v, ids_v, basis_v, sems,
):
    tokens = acts.shape[0]
    experts = basis_in.shape[0]
    cap = tokens // 2
    fetch = fetcher(sems)
    first = [fetch(routes, routes_v), fetch(ids, ids_v)]
    acts_in = fetch(acts, acts_v)
    bases = [fetch(basis_in.at[e], basis_v.at[e]) for e in range(experts)]
    for copy in first:
        copy.wait()
    hits = [
        jnp.max((routes_v[...] == e).astype(F32), axis=0, keepdims=True) for e in range(experts)
    ]
    rows = jnp.concatenate(hits + [jnp.zeros((8 - experts, tokens), F32)], axis=0).astype(BF16)
    upto = (iota((tokens, tokens), 0) <= iota((tokens, tokens), 1)).astype(BF16)
    order = dot(rows, upto)
    slots = iota((cap, tokens), 0).astype(F32) + 1.0
    pick_in = jnp.concatenate(
        [((order[e : e + 1] == slots) & (hits[e] > 0.5)).astype(BF16) for e in range(experts)],
        axis=0,
    )
    repeat = (iota((tokens, 2 * tokens), 0) == iota((tokens, 2 * tokens), 1) // 2).astype(BF16)
    wide = dot(
        jnp.concatenate(
            [order[:experts], routes_v[...].astype(F32), jnp.zeros((6 - experts, tokens), F32)],
            axis=0,
        ).astype(BF16),
        repeat,
    )
    odd = iota((1, 2 * tokens), 1) % 2 == 1
    routed_to = jnp.where(odd, wide[experts + 1 : experts + 2], wide[experts : experts + 1])
    slots = iota((cap, 2 * tokens), 0).astype(F32) + 1.0
    for e in range(experts):
        pick[e * cap : (e + 1) * cap, :] = (
            (wide[e : e + 1] == slots) & (routed_to == float(e))
        ).astype(BF16)
    numbers = jnp.broadcast_to(ids_v[...].reshape(1, tokens).astype(F32) + 1.0, (8, tokens)).astype(BF16)
    named = lax.dot_general(numbers, pick_in, (((1,), (1,)), ((), ())), preferred_element_type=F32)
    block = jnp.zeros((LABEL_ROWS, 128), F32)
    row = iota((LABEL_ROWS, 128), 0)
    half = cap // 2
    for at in range(2 * experts):
        mine = named[0:1, at * half : (at + 1) * half]
        mine = jnp.concatenate([mine, jnp.zeros((1, 128 - half), F32)], axis=1)
        block = jnp.where(row == at, mine, block)
    label[...] = block.astype(BF16)

    acts_in.wait()
    chosen = dot(pick_in, acts_v[...]).astype(BF16)
    for e in range(experts):
        bases[e].wait()
        acc[e] = dot(chosen[e * cap : (e + 1) * cap], basis_v[e])


def split_in_kernel(acc, keep, send):
    experts, cap, width = acc.shape
    core = lax.rem(lax.axis_index("tensor"), 2)
    half = cap // 2
    at = 0
    for q in range(width // 128):
        for e in range(experts):
            for ref, which in ((keep, core), (send, 1 - core)):
                ref[at : at + half, :] = acc[
                    e, pl.ds(pl.multiple_of(which * half, 8), half), q * 128 : (q + 1) * 128
                ]
            at += half


def rotate_out_kernel(grads, pick, basis_out, acc, grads_v, sems):
    tokens, _, hidden = grads.shape
    experts, cap, _ = acc.shape
    fetch = fetcher(sems)
    cuts = sorted({0, CHUNK // 2, *range(CHUNK, hidden + 1, CHUNK)})
    parts = [pl.ds(at, end - at) for at, end in zip(cuts, cuts[1:])]
    copies = [fetch(grads.at[:, :, part], grads_v.at[:, :, part]) for part in parts]
    for n, (part, copy) in enumerate(zip(parts, copies)):
        copy.wait()
        rows = grads_v[:, :, part].reshape(2 * tokens, part.size)
        chosen = dot(pick[...], rows).astype(BF16)
        for e in range(experts):
            more = dot(chosen[e * cap : (e + 1) * cap], basis_out[e, part, :])
            acc[e] = more if n == 0 else acc[e] + more


def split_out_kernel(acc, keep, send):
    experts, cap, width = acc.shape
    core = lax.rem(lax.axis_index("tensor"), 2)
    at = 0
    for x in range(width // 256):
        for e in range(experts):
            for ref, which in ((keep, core), (send, 1 - core)):
                ref[at : at + cap, :] = acc[
                    e, :, pl.ds(pl.multiple_of((2 * x + which) * 128, 128), 128)
                ]
            at += cap


def pair_in_kernel(kept, got, keep, send):
    total = kept[...] + got[...]
    keep[...] = total
    send[...] = total.astype(BF16)


def round_in_kernel(kept, got, label, *pays):
    slab = kept.shape[0] // len(pays)
    d = lax.axis_index("dp")
    for k, pay in enumerate(pays):
        rows = pl.ds(pl.multiple_of((d ^ k) * slab, 16), slab)
        pay[:slab, :] = (kept[rows, :] + got[rows, :].astype(F32)).astype(BF16)
        pay[slab:, :] = label[...]


def pair_out_kernel(kept, got, keep, send):
    outer = keep.shape[0]
    x = lax.div(lax.axis_index("tensor"), 2)
    mine = pl.ds(pl.multiple_of(x * outer, 16), outer)
    keep[...] = kept[mine, :] + got[mine, :]
    other = pl.ds(pl.multiple_of((1 - x) * outer, 16), outer)
    send[...] = (kept[other, :] + got[other, :]).astype(BF16)


def round_kernel(kept, got, out):
    outer = kept.shape[0]
    out[:outer, :] = (kept[...] + got[...].astype(F32)).astype(BF16)
    out[outer:, :] = jnp.zeros((out.shape[0] - outer, 128), BF16)


def stack_kernel(*refs):
    *pieces, first, second = refs
    slab = pieces[0].shape[0] - LABEL_ROWS
    for k, piece in enumerate(pieces):
        out = (first, second)[k * 2 // len(pieces)]
        at = k * slab % out.shape[0]
        out[at : at + slab, :] = piece[:slab, :]


def mask_kernel(counts, *refs):
    mine, other, pieces = refs[:2], refs[2:4], refs[4:-2]
    out, divisor = refs[-2:]
    experts, dp = out.shape[0], len(pieces)
    slab = 2 * mine[0].shape[0] // dp
    half = slab // experts
    core = lax.rem(lax.axis_index("tensor"), 2)
    for e in range(experts):
        divisor[e] = jnp.full(divisor.shape[1:], counts[e].astype(F32), F32)
        rows, labels = [], []
        for which, parts in ((core, mine), (1 - core, other)):
            for k, piece in enumerate(pieces):
                at = k % (dp // 2) * slab + e * half
                rows.append(parts[k // (dp // 2)][at : at + half, :])
                label = piece[slab:, :].astype(F32)[2 * e : 2 * e + 2, :half]
                labels.append(jnp.where(which == 0, label[0:1], label[1:2]))
        rows = jnp.concatenate(rows, axis=0).astype(F32)
        labels = jnp.concatenate(labels, axis=1)
        labels = jnp.broadcast_to(labels, (128, labels.shape[1])).T
        for n in range(dp):
            out[e, :, n * 128 : (n + 1) * 128] = jnp.where(
                labels == float(n + 1), rows, 0.0
            ).astype(BF16)


def blocks_kernel(divisor, masked, own, *refs):
    *far, result, final, sems = refs
    outs = [own, *reversed(far)]
    experts, slots, _ = masked.shape
    half = slots // (2 * len(outs))
    core = lax.rem(lax.axis_index("tensor"), 2)
    copies = []
    for e in range(experts):
        rows = [
            ref[pl.ds(pl.multiple_of((2 * e + which) * half, 16), half), :]
            for which in (core, 1 - core)
            for ref in outs
        ]
        blocks = dot(jnp.concatenate(rows, axis=0).T, masked[e])
        squares = blocks * blocks
        summed = squares[:, :128]
        for at in range(128, squares.shape[1], 128):
            summed = summed + squares[:, at : at + 128]
        final[e] = summed / divisor[e][:1]
        copies.append(pltpu.make_async_copy(final.at[e], result.at[e], sems.at[e]))
        copies[-1].start()
    for copy in copies:
        copy.wait()


def call(kernel, name, out_shape, specs=None, scratch=(), out_specs=None, flops=1, after=()):
    vmem = pl.BlockSpec(memory_space=pltpu.VMEM)
    given = {} if out_specs is None else {"out_specs": out_specs}

    def run(*args):
        def body(*refs):
            kernel(*refs[: len(args)], *refs[len(args) + len(after) :])

        return pl.pallas_call(
            body,
            out_shape=out_shape,
            in_specs=(specs or [vmem] * len(args)) + [vmem] * len(after),
            scratch_shapes=scratch,
            compiler_params=pltpu.CompilerParams(vmem_limit_bytes=VMEM),
            cost_estimate=pl.CostEstimate(flops=flops, bytes_accessed=1, transcendentals=0),
            name=name,
            **given,
        )(*args, *after)

    return run


def fast(acts, grads, routes, example_ids, expert_counts, basis_in, basis_out):
    tokens = acts.shape[0]
    experts, features, width = basis_in.shape
    cap = tokens // 2
    dp = lax.axis_size("dp")
    wide = experts * cap
    half = wide * width // 256
    hbm = pl.BlockSpec(memory_space=pltpu.HBM)
    vmem = pl.BlockSpec(memory_space=pltpu.VMEM)
    smem = pl.BlockSpec(memory_space=pltpu.SMEM)

    def pin(x):
        return pltpu.with_memory_space_constraint(x, pltpu.HBM)

    def rows(count, dtype):
        return jax.ShapeDtypeStruct((count, 128), dtype)

    core = [(t, t ^ 1) for t in range(4)]
    across = [(t, t ^ 2) for t in range(4)]

    def swap(x, k):
        return lax.ppermute(x, "dp", [(d, d ^ k) for d in range(dp)])

    partial = jax.ShapeDtypeStruct((experts, cap, width), F32)
    acc, label, pick = call(
        rotate_in_kernel,
        "rotate_in",
        (
            partial,
            rows(LABEL_ROWS, BF16),
            jax.ShapeDtypeStruct((wide, 2 * tokens), BF16),
        ),
        [hbm] * 4,
        [
            pltpu.VMEM(acts.shape, BF16),
            pltpu.VMEM((2, tokens), jnp.int32),
            pltpu.VMEM((tokens,), jnp.int32),
            pltpu.VMEM(basis_in.shape, BF16),
            pltpu.SemaphoreType.DMA((3 + experts,)),
        ],
    )(pin(acts), pin(routes.T), pin(example_ids), pin(basis_in))
    keep, send = call(
        split_in_kernel, "split_in", (rows(half, F32), rows(half, F32)), flops=8 * 10**9
    )(acc)
    got = lax.ppermute(send, "tensor", core)
    slab = half // dp
    keep_in, send_in = call(pair_in_kernel, "pair_in", (rows(half, F32), rows(half, BF16)))(
        keep, got
    )
    got_in = lax.ppermute(send_in, "tensor", across)

    acc = call(
        rotate_out_kernel,
        "rotate_out",
        partial,
        [hbm, vmem, vmem],
        [pltpu.VMEM(grads.shape, BF16), pltpu.SemaphoreType.DMA((grads.shape[2] // CHUNK + 1,))],
        after=[send_in],
    )(pin(grads), pick, basis_out)
    keep, send = call(
        split_out_kernel, "split_out", (rows(half, F32), rows(half, F32)), after=[got_in]
    )(acc)
    got = lax.ppermute(send, "tensor", core)
    keep, send = call(pair_out_kernel, "pair_out", (rows(wide, F32), rows(wide, BF16)))(keep, got)
    got = lax.ppermute(send, "tensor", across)

    slab = half // dp
    pieces = call(round_in_kernel, "round_in", [rows(slab + LABEL_ROWS, BF16)] * dp)(
        keep_in, got_in, label
    )
    pieces = [pieces[0]] + [swap(pieces[k], k) for k in FAR_FIRST]
    out = call(round_kernel, "round_out", rows(wide + 16, BF16))(keep, got)
    outs = [swap(out, k) for k in reversed(FAR_FIRST)]
    mine = call(stack_kernel, "stack_in", [rows(half // 2, BF16)] * 2)(*pieces)
    other = [lax.ppermute(x, "tensor", core) for x in mine]
    masked, divisor = call(
        mask_kernel,
        "mask_in",
        (
            jax.ShapeDtypeStruct((experts, dp * cap, dp * 128), BF16),
            jax.ShapeDtypeStruct((experts, 8, 128), F32),
        ),
        [smem] + [vmem] * (4 + dp),
    )(expert_counts, *mine, *other, *pieces)
    result = jax.ShapeDtypeStruct((experts, 128, 128), F32)
    return call(
        blocks_kernel,
        "blocks",
        result,
        scratch=[pltpu.VMEM(result.shape, F32), pltpu.SemaphoreType.DMA((experts,))],
        out_specs=hbm,
    )(divisor, masked, out, *outs)


EX_DEV = 1


def compact(routes, expert, capacity):
    tok_count = routes.shape[0]
    second_hit = routes[:, 1] == expert
    routed = (routes[:, 0] == expert) | second_hit
    order = jnp.cumsum(routed.astype(jnp.int32)) - 1
    slots = jnp.arange(capacity, dtype=jnp.int32)
    match = routed[None, :] & (order[None, :] == slots[:, None])
    token_index = jnp.arange(tok_count, dtype=jnp.int32)
    positions = jnp.sum(jnp.where(match, token_index[None, :], 0), axis=1)
    filled = jnp.any(match, axis=1)
    return (positions, filled, second_hit[positions])


def general(acts, grads, routes, example_ids, expert_counts, basis_in, basis_out):
    capacity = acts.shape[0] // 2
    experts = basis_in.shape[0]
    parts_in, parts_out, label_rows = ([], [], [])
    for expert in range(experts):
        positions, filled, second = compact(routes, expert, capacity)
        chosen = grads[positions]
        grad_rows = jnp.where(second[:, None], chosen[:, 1, :], chosen[:, 0, :])
        parts_in.append(
            jnp.dot(acts[positions], basis_in[expert], preferred_element_type=jnp.float32)
        )
        parts_out.append(jnp.dot(grad_rows, basis_out[expert], preferred_element_type=jnp.float32))
        label_rows.append(jnp.where(filled, example_ids[positions], -1))
    part_in = jnp.stack(parts_in)
    part_out = jnp.stack(parts_out)
    labels = jnp.stack(label_rows)
    slice_width = basis_out.shape[2] // lax.axis_size("tensor")
    summed_in, summed_out = lax.psum((part_in, part_out), "tensor")
    rot_in = summed_in.astype(jnp.bfloat16)
    rot_out = lax.dynamic_slice_in_dim(
        summed_out.astype(jnp.bfloat16), lax.axis_index("tensor") * slice_width, slice_width, 2
    )
    owned_count = EX_DEV
    wanted = jnp.arange(lax.axis_size("dp") * owned_count, dtype=jnp.int32)
    onehot = (labels[:, :, None] == wanted[None, None, :]).astype(jnp.bfloat16)
    spread = onehot[:, :, :, None] * rot_out[:, :, None, :]
    owned_sums = lax.psum_scatter(
        jnp.einsum("ecnw,eca->newa", spread, rot_in, preferred_element_type=jnp.float32),
        "dp",
        scatter_dimension=0,
        tiled=True,
    )
    squared = jnp.sum(owned_sums * owned_sums, axis=0)
    totals = lax.psum_scatter(squared, "dp", scatter_dimension=2, tiled=True)
    return totals / expert_counts.astype(jnp.float32)[:, None, None]


def shards(*args):
    experts, _, width = args[5].shape
    sizes = (lax.axis_size("dp"), lax.axis_size("tensor"), experts, width)
    fits = sizes == (4, 4, 2, 512) and args[0].shape[0] == 384
    return (fast if fits else general)(*args)


def solution(mesh):
    placed = (
        P(("group", "dp"), "tensor"),
        P(("group", "dp"), None, "tensor"),
        P(("group", "dp"), None),
        P(("group", "dp")),
        P("group"),
        P(None, "tensor", None),
        P(None, "tensor", None),
    )
    return jax.shard_map(
        shards, mesh=mesh, in_specs=placed, out_specs=P("group", "tensor", "dp"), check_vma=False
    )
```

```python
import functools

import jax
import jax.numpy as jnp
from jax import lax
from jax.experimental import pallas as pl
from jax.experimental.pallas import tpu as pltpu
from jax.sharding import PartitionSpec as P

F32 = jnp.float32
BF16 = jnp.bfloat16
CHUNK = 1024
VMEM = 20 * 2**20
EARLY = 1024
DISTANCES = (1, 2, 3)
LATEST = (1, 3, 2)
LABEL_ROWS = 16


def iota(shape, dim):
    return lax.broadcasted_iota(jnp.int32, shape, dim)


def dot(a, b):
    return jnp.dot(a, b, preferred_element_type=F32)


def fetcher(sems):
    count = iter(range(sems.shape[0]))

    def fetch(src, dst):
        copy = pltpu.make_async_copy(src, dst, sems.at[next(count)])
        copy.start()
        return copy

    return fetch


def rotate_in_kernel(
    acts, routes, ids, basis_in, grads,
    acc, label, pick, early,
    acts_v, routes_v, ids_v, basis_v, sems,
):
    tokens = acts.shape[0]
    experts = basis_in.shape[0]
    cap = tokens // 2
    fetch = fetcher(sems)
    first = [fetch(routes, routes_v), fetch(ids, ids_v)]
    acts_in = fetch(acts, acts_v)
    bases = [fetch(basis_in.at[e], basis_v.at[e]) for e in range(experts)]
    grads_in = fetch(grads.at[:, :, pl.ds(0, early.shape[2])], early)
    for copy in first:
        copy.wait()
    hits = [
        jnp.max((routes_v[...] == e).astype(F32), axis=0, keepdims=True) for e in range(experts)
    ]
    rows = jnp.concatenate(hits + [jnp.zeros((8 - experts, tokens), F32)], axis=0).astype(BF16)
    upto = (iota((tokens, tokens), 0) <= iota((tokens, tokens), 1)).astype(BF16)
    order = dot(rows, upto)
    slots = iota((cap, tokens), 0).astype(F32) + 1.0
    pick_in = jnp.concatenate(
        [((order[e : e + 1] == slots) & (hits[e] > 0.5)).astype(BF16) for e in range(experts)],
        axis=0,
    )
    repeat = (iota((tokens, 2 * tokens), 0) == iota((tokens, 2 * tokens), 1) // 2).astype(BF16)
    wide = dot(
        jnp.concatenate(
            [order[:experts], routes_v[...].astype(F32), jnp.zeros((6 - experts, tokens), F32)],
            axis=0,
        ).astype(BF16),
        repeat,
    )
    odd = iota((1, 2 * tokens), 1) % 2 == 1
    routed_to = jnp.where(odd, wide[experts + 1 : experts + 2], wide[experts : experts + 1])
    slots = iota((cap, 2 * tokens), 0).astype(F32) + 1.0
    for e in range(experts):
        pick[e * cap : (e + 1) * cap, :] = (
            (wide[e : e + 1] == slots) & (routed_to == float(e))
        ).astype(BF16)
    numbers = jnp.broadcast_to(ids_v[...].reshape(1, tokens).astype(F32) + 1.0, (8, tokens)).astype(BF16)
    named = lax.dot_general(numbers, pick_in, (((1,), (1,)), ((), ())), preferred_element_type=F32)
    block = jnp.zeros((LABEL_ROWS, 128), F32)
    row = iota((LABEL_ROWS, 128), 0)
    half = cap // 2
    for at in range(2 * experts):
        mine = named[0:1, at * half : (at + 1) * half]
        mine = jnp.concatenate([mine, jnp.zeros((1, 128 - half), F32)], axis=1)
        block = jnp.where(row == at, mine, block)
    label[...] = block.astype(BF16)

    acts_in.wait()
    chosen = dot(pick_in, acts_v[...]).astype(BF16)
    for e in range(experts):
        bases[e].wait()
        acc[e] = dot(chosen[e * cap : (e + 1) * cap], basis_v[e])
    grads_in.wait()


def split_in_kernel(acc, keep, send):
    experts, cap, width = acc.shape
    core = lax.rem(lax.axis_index("tensor"), 2)
    half = cap // 2
    at = 0
    for q in range(width // 128):
        for e in range(experts):
            for ref, which in ((keep, core), (send, 1 - core)):
                ref[at : at + half, :] = acc[
                    e, pl.ds(pl.multiple_of(which * half, 8), half), q * 128 : (q + 1) * 128
                ]
            at += half


def choose(pick, rows):
    return dot(pick[...], rows.reshape(2 * rows.shape[0], rows.shape[2])).astype(BF16)


def choose_kernel(grads, pick, out):
    out[...] = choose(pick, grads[...])


def rotate_out_kernel(grads, pick, basis_out, early, acc, grads_v, sems):
    hidden = grads.shape[2]
    experts, cap, _ = acc.shape
    fetch = fetcher(sems)
    done = early.shape[1]
    cuts = sorted({done, done + CHUNK // 2, *range(done + CHUNK, hidden + 1, CHUNK)})
    parts = [(at, pl.ds(at, end - at)) for at, end in zip(cuts, cuts[1:])]
    copies = [
        fetch(grads.at[:, :, part], grads_v.at[:, :, pl.ds(at - done, part.size)])
        for at, part in parts
    ]
    for e in range(experts):
        acc[e] = dot(early[e * cap : (e + 1) * cap, :], basis_out[e, :done, :])
    for (at, part), copy in zip(parts, copies):
        copy.wait()
        chosen = choose(pick, grads_v[:, :, pl.ds(at - done, part.size)])
        for e in range(experts):
            acc[e] += dot(chosen[e * cap : (e + 1) * cap], basis_out[e, part, :])


def split_out_kernel(acc, keep, send):
    experts, cap, width = acc.shape
    core = lax.rem(lax.axis_index("tensor"), 2)
    at = 0
    for x in range(width // 256):
        for e in range(experts):
            for ref, which in ((keep, core), (send, 1 - core)):
                ref[at : at + cap, :] = acc[
                    e, :, pl.ds(pl.multiple_of((2 * x + which) * 128, 128), 128)
                ]
            at += cap


def pair_in_kernel(kept, got, keep, send):
    total = kept[...] + got[...]
    keep[...] = total
    send[...] = total.astype(BF16)


def round_in_kernel(kept, got, label, *pays):
    slab = kept.shape[0] // len(pays)
    d = lax.axis_index("dp")
    for k, pay in enumerate(pays):
        rows = pl.ds(pl.multiple_of((d ^ k) * slab, 16), slab)
        pay[:slab, :] = (kept[rows, :] + got[rows, :].astype(F32)).astype(BF16)
        pay[slab:, :] = label[...]


def pair_out_kernel(kept, got, keep, send):
    outer = keep.shape[0]
    x = lax.div(lax.axis_index("tensor"), 2)
    mine = pl.ds(pl.multiple_of(x * outer, 16), outer)
    keep[...] = kept[mine, :] + got[mine, :]
    other = pl.ds(pl.multiple_of((1 - x) * outer, 16), outer)
    send[...] = (kept[other, :] + got[other, :]).astype(BF16)


def round_kernel(kept, got, out):
    outer = kept.shape[0]
    out[:outer, :] = (kept[...] + got[...].astype(F32)).astype(BF16)
    out[outer:, :] = jnp.zeros((out.shape[0] - outer, 128), BF16)


def stack_kernel(*refs):
    *pieces, first, second = refs
    slab = pieces[0].shape[0] - LABEL_ROWS
    for k, piece in enumerate(pieces):
        out = (first, second)[k * 2 // len(pieces)]
        at = k * slab % out.shape[0]
        out[at : at + slab, :] = piece[:slab, :]


def mask_kernel(counts, *refs):
    mine, other, pieces = refs[:2], refs[2:4], refs[4:-2]
    out, divisor = refs[-2:]
    experts, dp = out.shape[0], len(pieces)
    slab = 2 * mine[0].shape[0] // dp
    half = slab // experts
    core = lax.rem(lax.axis_index("tensor"), 2)
    for e in range(experts):
        divisor[e] = jnp.full(divisor.shape[1:], counts[e].astype(F32), F32)
        rows, labels = [], []
        for which, parts in ((core, mine), (1 - core, other)):
            for k, piece in enumerate(pieces):
                at = k % (dp // 2) * slab + e * half
                rows.append(parts[k // (dp // 2)][at : at + half, :])
                label = piece[slab:, :].astype(F32)[2 * e : 2 * e + 2, :half]
                labels.append(jnp.where(which == 0, label[0:1], label[1:2]))
        rows = jnp.concatenate(rows, axis=0).astype(F32)
        labels = jnp.concatenate(labels, axis=1)
        labels = jnp.broadcast_to(labels, (128, labels.shape[1])).T
        for n in range(dp):
            out[e, :, n * 128 : (n + 1) * 128] = jnp.where(
                labels == float(n + 1), rows, 0.0
            ).astype(BF16)


def blocks_kernel(divisor, masked, own, *refs):
    *far, result, final, sems = refs
    outs = [own] + [far[LATEST.index(k)] for k in DISTANCES]
    experts, slots, _ = masked.shape
    half = slots // (2 * len(outs))
    core = lax.rem(lax.axis_index("tensor"), 2)
    copies = []
    for e in range(experts):
        rows = [
            ref[pl.ds(pl.multiple_of((2 * e + which) * half, 16), half), :]
            for which in (core, 1 - core)
            for ref in outs
        ]
        blocks = dot(jnp.concatenate(rows, axis=0).T, masked[e])
        squares = blocks * blocks
        summed = squares[:, :128]
        for at in range(128, squares.shape[1], 128):
            summed = summed + squares[:, at : at + 128]
        final[e] = summed / divisor[e][:1]
        copies.append(pltpu.make_async_copy(final.at[e], result.at[e], sems.at[e]))
        copies[-1].start()
    for copy in copies:
        copy.wait()


def call(kernel, name, out_shape, specs=None, scratch=(), out_specs=None, flops=1, after=()):
    vmem = pl.BlockSpec(memory_space=pltpu.VMEM)
    given = {} if out_specs is None else {"out_specs": out_specs}

    def run(*args):
        def body(*refs):
            kernel(*refs[: len(args)], *refs[len(args) + len(after) :])

        return pl.pallas_call(
            body,
            out_shape=out_shape,
            in_specs=(specs or [vmem] * len(args)) + [vmem] * len(after),
            scratch_shapes=scratch,
            compiler_params=pltpu.CompilerParams(vmem_limit_bytes=VMEM),
            cost_estimate=pl.CostEstimate(flops=flops, bytes_accessed=1, transcendentals=0),
            name=name,
            **given,
        )(*args, *after)

    return run


def fast(acts, grads, routes, example_ids, expert_counts, basis_in, basis_out):
    tokens = acts.shape[0]
    experts, features, width = basis_in.shape
    cap = tokens // 2
    dp = lax.axis_size("dp")
    wide = experts * cap
    half = wide * width // 256
    hbm = pl.BlockSpec(memory_space=pltpu.HBM)
    vmem = pl.BlockSpec(memory_space=pltpu.VMEM)
    smem = pl.BlockSpec(memory_space=pltpu.SMEM)

    def pin(x):
        return pltpu.with_memory_space_constraint(x, pltpu.HBM)

    def rows(count, dtype):
        return jax.ShapeDtypeStruct((count, 128), dtype)

    core = [(t, t ^ 1) for t in range(4)]
    across = [(t, t ^ 2) for t in range(4)]

    def swap(x, k):
        return lax.ppermute(x, "dp", [(d, d ^ k) for d in range(dp)])

    partial = jax.ShapeDtypeStruct((experts, cap, width), F32)
    acc, label, pick, early = call(
        rotate_in_kernel,
        "rotate_in",
        (
            partial,
            rows(LABEL_ROWS, BF16),
            jax.ShapeDtypeStruct((wide, 2 * tokens), BF16),
            jax.ShapeDtypeStruct((tokens, 2, EARLY), BF16),
        ),
        [hbm] * 5,
        [
            pltpu.VMEM(acts.shape, BF16),
            pltpu.VMEM((2, tokens), jnp.int32),
            pltpu.VMEM((tokens,), jnp.int32),
            pltpu.VMEM(basis_in.shape, BF16),
            pltpu.SemaphoreType.DMA((4 + experts,)),
        ],
    )(pin(acts), pin(routes.T), pin(example_ids), pin(basis_in), pin(grads))
    keep, send = call(
        split_in_kernel, "split_in", (rows(half, F32), rows(half, F32)), flops=8 * 10**9
    )(acc)
    got = lax.ppermute(send, "tensor", core)
    slab = half // dp
    early = call(choose_kernel, "choose", jax.ShapeDtypeStruct((wide, EARLY), BF16))(early, pick)
    keep_in, send_in = call(
        pair_in_kernel, "pair_in", (rows(half, F32), rows(half, BF16)), after=[early]
    )(keep, got)
    got_in = lax.ppermute(send_in, "tensor", across)

    acc = call(
        rotate_out_kernel,
        "rotate_out",
        partial,
        [hbm, vmem, vmem, vmem],
        [
            pltpu.VMEM((tokens, 2, grads.shape[2] - EARLY), BF16),
            pltpu.SemaphoreType.DMA((grads.shape[2] // CHUNK,)),
        ],
        after=[send_in],
    )(pin(grads), pick, basis_out, early)
    keep, send = call(
        split_out_kernel, "split_out", (rows(half, F32), rows(half, F32)), after=[got_in]
    )(acc)
    got = lax.ppermute(send, "tensor", core)
    keep, send = call(pair_out_kernel, "pair_out", (rows(wide, F32), rows(wide, BF16)))(keep, got)
    got = lax.ppermute(send, "tensor", across)

    slab = half // dp
    pieces = call(round_in_kernel, "round_in", [rows(slab + LABEL_ROWS, BF16)] * dp)(
        keep_in, got_in, label
    )
    pieces = [pieces[0]] + [swap(pieces[k], k) for k in DISTANCES]
    out = call(round_kernel, "round_out", rows(wide + 16, BF16))(keep, got)
    outs = [swap(out, k) for k in LATEST]
    mine = call(stack_kernel, "stack_in", [rows(half // 2, BF16)] * 2)(*pieces)
    other = [lax.ppermute(x, "tensor", core) for x in mine]
    masked, divisor = call(
        mask_kernel,
        "mask_in",
        (
            jax.ShapeDtypeStruct((experts, dp * cap, dp * 128), BF16),
            jax.ShapeDtypeStruct((experts, 8, 128), F32),
        ),
        [smem] + [vmem] * (4 + dp),
    )(expert_counts, *mine, *other, *pieces)
    result = jax.ShapeDtypeStruct((experts, 128, 128), F32)
    return call(
        blocks_kernel,
        "blocks",
        result,
        scratch=[pltpu.VMEM(result.shape, F32), pltpu.SemaphoreType.DMA((experts,))],
        out_specs=hbm,
    )(divisor, masked, out, *outs)


EX_DEV = 1


def compact(routes, expert, capacity):
    tok_count = routes.shape[0]
    second_hit = routes[:, 1] == expert
    routed = (routes[:, 0] == expert) | second_hit
    order = jnp.cumsum(routed.astype(jnp.int32)) - 1
    slots = jnp.arange(capacity, dtype=jnp.int32)
    match = routed[None, :] & (order[None, :] == slots[:, None])
    token_index = jnp.arange(tok_count, dtype=jnp.int32)
    positions = jnp.sum(jnp.where(match, token_index[None, :], 0), axis=1)
    filled = jnp.any(match, axis=1)
    return (positions, filled, second_hit[positions])


def general(acts, grads, routes, example_ids, expert_counts, basis_in, basis_out):
    capacity = acts.shape[0] // 2
    experts = basis_in.shape[0]
    parts_in, parts_out, label_rows = ([], [], [])
    for expert in range(experts):
        positions, filled, second = compact(routes, expert, capacity)
        chosen = grads[positions]
        grad_rows = jnp.where(second[:, None], chosen[:, 1, :], chosen[:, 0, :])
        parts_in.append(
            jnp.dot(acts[positions], basis_in[expert], preferred_element_type=jnp.float32)
        )
        parts_out.append(jnp.dot(grad_rows, basis_out[expert], preferred_element_type=jnp.float32))
        label_rows.append(jnp.where(filled, example_ids[positions], -1))
    part_in = jnp.stack(parts_in)
    part_out = jnp.stack(parts_out)
    labels = jnp.stack(label_rows)
    slice_width = basis_out.shape[2] // lax.axis_size("tensor")
    summed_in, summed_out = lax.psum((part_in, part_out), "tensor")
    rot_in = summed_in.astype(jnp.bfloat16)
    rot_out = lax.dynamic_slice_in_dim(
        summed_out.astype(jnp.bfloat16), lax.axis_index("tensor") * slice_width, slice_width, 2
    )
    owned_count = EX_DEV
    wanted = jnp.arange(lax.axis_size("dp") * owned_count, dtype=jnp.int32)
    onehot = (labels[:, :, None] == wanted[None, None, :]).astype(jnp.bfloat16)
    spread = onehot[:, :, :, None] * rot_out[:, :, None, :]
    owned_sums = lax.psum_scatter(
        jnp.einsum("ecnw,eca->newa", spread, rot_in, preferred_element_type=jnp.float32),
        "dp",
        scatter_dimension=0,
        tiled=True,
    )
    squared = jnp.sum(owned_sums * owned_sums, axis=0)
    totals = lax.psum_scatter(squared, "dp", scatter_dimension=2, tiled=True)
    return totals / expert_counts.astype(jnp.float32)[:, None, None]


def shards(*args):
    experts, _, width = args[5].shape
    sizes = (lax.axis_size("dp"), lax.axis_size("tensor"), experts, width)
    fits = sizes == (4, 4, 2, 512) and args[0].shape[0] == 384
    return (fast if fits else general)(*args)


def solution(mesh):
    placed = (
        P(("group", "dp"), "tensor"),
        P(("group", "dp"), None, "tensor"),
        P(("group", "dp"), None),
        P(("group", "dp")),
        P("group"),
        P(None, "tensor", None),
        P(None, "tensor", None),
    )
    return jax.shard_map(
        shards, mesh=mesh, in_specs=placed, out_specs=P("group", "tensor", "dp"), check_vma=False
    )
```

```python
import functools

import jax
import jax.numpy as jnp
from jax import lax
from jax.experimental import pallas as pl
from jax.experimental.pallas import tpu as pltpu
from jax.sharding import PartitionSpec as P

F32 = jnp.float32
BF16 = jnp.bfloat16
CHUNK = 1024
VMEM = 20 * 2**20
EARLY = 1024
DISTANCES = (1, 2, 3)
LATEST = (1, 3, 2)
LABEL_ROWS = 16


def iota(shape, dim):
    return lax.broadcasted_iota(jnp.int32, shape, dim)


def dot(a, b):
    return jnp.dot(a, b, preferred_element_type=F32)


def fetcher(sems):
    count = iter(range(sems.shape[0]))

    def fetch(src, dst):
        copy = pltpu.make_async_copy(src, dst, sems.at[next(count)])
        copy.start()
        return copy

    return fetch


def rotate_in_kernel(
    acts, routes, ids, basis_in, grads,
    acc, label, pick, early,
    acts_v, routes_v, ids_v, basis_v, sems,
):
    tokens = acts.shape[0]
    experts = basis_in.shape[0]
    cap = tokens // 2
    fetch = fetcher(sems)
    first = [fetch(routes, routes_v), fetch(ids, ids_v)]
    acts_in = fetch(acts, acts_v)
    bases = [fetch(basis_in.at[e], basis_v.at[e]) for e in range(experts)]
    grads_in = fetch(grads.at[:, :, pl.ds(0, early.shape[2])], early)
    for copy in first:
        copy.wait()
    hits = [
        jnp.max((routes_v[...] == e).astype(F32), axis=0, keepdims=True) for e in range(experts)
    ]
    rows = jnp.concatenate(hits + [jnp.zeros((8 - experts, tokens), F32)], axis=0).astype(BF16)
    upto = (iota((tokens, tokens), 0) <= iota((tokens, tokens), 1)).astype(BF16)
    order = dot(rows, upto)
    slots = iota((cap, tokens), 0).astype(F32) + 1.0
    pick_in = jnp.concatenate(
        [((order[e : e + 1] == slots) & (hits[e] > 0.5)).astype(BF16) for e in range(experts)],
        axis=0,
    )
    repeat = (iota((tokens, 2 * tokens), 0) == iota((tokens, 2 * tokens), 1) // 2).astype(BF16)
    wide = dot(
        jnp.concatenate(
            [order[:experts], routes_v[...].astype(F32), jnp.zeros((6 - experts, tokens), F32)],
            axis=0,
        ).astype(BF16),
        repeat,
    )
    odd = iota((1, 2 * tokens), 1) % 2 == 1
    routed_to = jnp.where(odd, wide[experts + 1 : experts + 2], wide[experts : experts + 1])
    slots = iota((cap, 2 * tokens), 0).astype(F32) + 1.0
    for e in range(experts):
        pick[e * cap : (e + 1) * cap, :] = (
            (wide[e : e + 1] == slots) & (routed_to == float(e))
        ).astype(BF16)
    numbers = jnp.broadcast_to(ids_v[...].reshape(1, tokens).astype(F32) + 1.0, (8, tokens)).astype(BF16)
    named = lax.dot_general(numbers, pick_in, (((1,), (1,)), ((), ())), preferred_element_type=F32)
    block = jnp.zeros((LABEL_ROWS, 128), F32)
    row = iota((LABEL_ROWS, 128), 0)
    half = cap // 2
    for at in range(2 * experts):
        mine = named[0:1, at * half : (at + 1) * half]
        mine = jnp.concatenate([mine, jnp.zeros((1, 128 - half), F32)], axis=1)
        block = jnp.where(row == at, mine, block)
    label[...] = block.astype(BF16)

    acts_in.wait()
    chosen = dot(pick_in, acts_v[...]).astype(BF16)
    for e in range(experts):
        bases[e].wait()
        acc[e] = dot(chosen[e * cap : (e + 1) * cap], basis_v[e])
    grads_in.wait()


def split_in_kernel(acc, keep, send):
    experts, cap, width = acc.shape
    core = lax.rem(lax.axis_index("tensor"), 2)
    half = cap // 2
    at = 0
    for q in range(width // 128):
        for e in range(experts):
            for ref, which in ((keep, core), (send, 1 - core)):
                ref[at : at + half, :] = acc[
                    e, pl.ds(pl.multiple_of(which * half, 8), half), q * 128 : (q + 1) * 128
                ]
            at += half


def choose(pick, rows):
    return dot(pick[...], rows.reshape(2 * rows.shape[0], rows.shape[2])).astype(BF16)


def choose_kernel(grads, pick, out):
    out[...] = choose(pick, grads[...])


def rotate_out_kernel(grads, pick, basis_out, early, acc, grads_v, sems):
    hidden = grads.shape[2]
    experts, cap, _ = acc.shape
    fetch = fetcher(sems)
    done = early.shape[1]
    cuts = sorted({done, done + CHUNK // 2, *range(done + CHUNK, hidden + 1, CHUNK)})
    parts = [(at, pl.ds(at, end - at)) for at, end in zip(cuts, cuts[1:])]
    copies = [
        fetch(grads.at[:, :, part], grads_v.at[:, :, pl.ds(at - done, part.size)])
        for at, part in parts
    ]
    for e in range(experts):
        acc[e] = dot(early[e * cap : (e + 1) * cap, :], basis_out[e, :done, :])
    for (at, part), copy in zip(parts, copies):
        copy.wait()
        chosen = choose(pick, grads_v[:, :, pl.ds(at - done, part.size)])
        for e in range(experts):
            acc[e] += dot(chosen[e * cap : (e + 1) * cap], basis_out[e, part, :])


def split_out_kernel(acc, keep, send):
    experts, cap, width = acc.shape
    core = lax.rem(lax.axis_index("tensor"), 2)
    at = 0
    for x in range(width // 256):
        for e in range(experts):
            for ref, which in ((keep, core), (send, 1 - core)):
                ref[at : at + cap, :] = acc[
                    e, :, pl.ds(pl.multiple_of((2 * x + which) * 128, 128), 128)
                ]
            at += cap


def pair_in_kernel(kept, got, keep, send):
    total = kept[...] + got[...]
    keep[...] = total
    send[...] = total.astype(BF16)


def round_in_kernel(kept, got, label, own, next_, far):
    slab = own.shape[0]
    d = lax.axis_index("dp")

    def part(k):
        rows = pl.ds(pl.multiple_of((d ^ k) * slab, 16), slab)
        return (kept[rows, :] + got[rows, :].astype(F32)).astype(BF16)

    own[...] = part(0)
    next_[...] = part(1)
    far[:slab, :] = part(2)
    far[slab : 2 * slab, :] = part(3)
    far[2 * slab :, :] = label[...]


def relay_kernel(next_, far, label, out):
    slab = next_.shape[0]
    out[:slab, :] = next_[...]
    out[slab : 2 * slab, :] = far[slab : 2 * slab, :]
    out[2 * slab : 2 * slab + LABEL_ROWS, :] = label[...]
    out[2 * slab + LABEL_ROWS :, :] = far[2 * slab :, :]


def pair_out_kernel(kept, got, keep, send):
    outer = keep.shape[0]
    x = lax.div(lax.axis_index("tensor"), 2)
    mine = pl.ds(pl.multiple_of(x * outer, 16), outer)
    keep[...] = kept[mine, :] + got[mine, :]
    other = pl.ds(pl.multiple_of((1 - x) * outer, 16), outer)
    send[...] = (kept[other, :] + got[other, :]).astype(BF16)


def round_kernel(kept, got, out):
    out[...] = (kept[...] + got[...].astype(F32)).astype(BF16)


def stack_kernel(near, far, first, second):
    rows = first.shape[0]
    slab = rows * 2 // 3
    first[:slab, :] = near[:slab, :]
    first[slab:, :] = far[: rows - slab, :]
    second[: rows - slab, :] = far[rows - slab : slab, :]
    second[rows - slab :, :] = near[slab : 2 * slab, :]


def mask_kernel(counts, own, first, second, own_, first_, second_, label, near, far, out, divisor):
    experts = out.shape[0]
    dp = out.shape[2] // 128
    slab = own.shape[0]
    half = slab // experts
    core = lax.rem(lax.axis_index("tensor"), 2)
    at = 2 * slab
    named = [
        label[...],
        near[at : at + LABEL_ROWS, :],
        far[at : at + LABEL_ROWS, :],
        near[at + LABEL_ROWS :, :],
    ]
    for e in range(experts):
        divisor[e] = jnp.full(divisor.shape[1:], counts[e].astype(F32), F32)
        rows, labels = [], []
        for which, refs in ((core, (own, first, second)), (1 - core, (own_, first_, second_))):
            every = jnp.concatenate([ref[...] for ref in refs], axis=0)
            for k in range(dp):
                rows.append(every[k * slab + e * half : k * slab + (e + 1) * half])
                mine = named[k].astype(F32)[2 * e : 2 * e + 2, :half]
                labels.append(jnp.where(which == 0, mine[0:1], mine[1:2]))
        rows = jnp.concatenate(rows, axis=0).astype(F32)
        labels = jnp.concatenate(labels, axis=1)
        labels = jnp.broadcast_to(labels, (128, labels.shape[1])).T
        for n in range(dp):
            out[e, :, n * 128 : (n + 1) * 128] = jnp.where(
                labels == float(n + 1), rows, 0.0
            ).astype(BF16)


def blocks_kernel(divisor, masked, own, *refs):
    *far, result, final, sems = refs
    outs = [own] + [far[LATEST.index(k)] for k in DISTANCES]
    experts, slots, _ = masked.shape
    half = slots // (2 * len(outs))
    core = lax.rem(lax.axis_index("tensor"), 2)
    copies = []
    for e in range(experts):
        rows = [
            ref[pl.ds(pl.multiple_of((2 * e + which) * half, 16), half), :]
            for which in (core, 1 - core)
            for ref in outs
        ]
        blocks = dot(jnp.concatenate(rows, axis=0).T, masked[e])
        squares = blocks * blocks
        summed = squares[:, :128]
        for at in range(128, squares.shape[1], 128):
            summed = summed + squares[:, at : at + 128]
        final[e] = summed / divisor[e][:1]
        copies.append(pltpu.make_async_copy(final.at[e], result.at[e], sems.at[e]))
        copies[-1].start()
    for copy in copies:
        copy.wait()


def call(kernel, name, out_shape, specs=None, scratch=(), out_specs=None, flops=1, after=()):
    vmem = pl.BlockSpec(memory_space=pltpu.VMEM)
    given = {} if out_specs is None else {"out_specs": out_specs}

    def run(*args):
        def body(*refs):
            kernel(*refs[: len(args)], *refs[len(args) + len(after) :])

        return pl.pallas_call(
            body,
            out_shape=out_shape,
            in_specs=(specs or [vmem] * len(args)) + [vmem] * len(after),
            scratch_shapes=scratch,
            compiler_params=pltpu.CompilerParams(vmem_limit_bytes=VMEM),
            cost_estimate=pl.CostEstimate(flops=flops, bytes_accessed=1, transcendentals=0),
            name=name,
            **given,
        )(*args, *after)

    return run


def fast(acts, grads, routes, example_ids, expert_counts, basis_in, basis_out):
    tokens = acts.shape[0]
    experts, features, width = basis_in.shape
    cap = tokens // 2
    dp = lax.axis_size("dp")
    wide = experts * cap
    half = wide * width // 256
    hbm = pl.BlockSpec(memory_space=pltpu.HBM)
    vmem = pl.BlockSpec(memory_space=pltpu.VMEM)
    smem = pl.BlockSpec(memory_space=pltpu.SMEM)

    def pin(x):
        return pltpu.with_memory_space_constraint(x, pltpu.HBM)

    def rows(count, dtype):
        return jax.ShapeDtypeStruct((count, 128), dtype)

    core = [(t, t ^ 1) for t in range(4)]
    across = [(t, t ^ 2) for t in range(4)]

    def swap(x, k):
        return lax.ppermute(x, "dp", [(d, d ^ k) for d in range(dp)])

    partial = jax.ShapeDtypeStruct((experts, cap, width), F32)
    acc, label, pick, early = call(
        rotate_in_kernel,
        "rotate_in",
        (
            partial,
            rows(LABEL_ROWS, BF16),
            jax.ShapeDtypeStruct((wide, 2 * tokens), BF16),
            jax.ShapeDtypeStruct((tokens, 2, EARLY), BF16),
        ),
        [hbm] * 5,
        [
            pltpu.VMEM(acts.shape, BF16),
            pltpu.VMEM((2, tokens), jnp.int32),
            pltpu.VMEM((tokens,), jnp.int32),
            pltpu.VMEM(basis_in.shape, BF16),
            pltpu.SemaphoreType.DMA((4 + experts,)),
        ],
    )(pin(acts), pin(routes.T), pin(example_ids), pin(basis_in), pin(grads))
    keep, send = call(
        split_in_kernel, "split_in", (rows(half, F32), rows(half, F32)), flops=8 * 10**9
    )(acc)
    got = lax.ppermute(send, "tensor", core)
    early = call(choose_kernel, "choose", jax.ShapeDtypeStruct((wide, EARLY), BF16))(early, pick)
    keep_in, send_in = call(
        pair_in_kernel, "pair_in", (rows(half, F32), rows(half, BF16)), after=[early]
    )(keep, got)
    got_in = lax.ppermute(send_in, "tensor", across)

    acc = call(
        rotate_out_kernel,
        "rotate_out",
        partial,
        [hbm, vmem, vmem, vmem],
        [
            pltpu.VMEM((tokens, 2, grads.shape[2] - EARLY), BF16),
            pltpu.SemaphoreType.DMA((grads.shape[2] // CHUNK,)),
        ],
        after=[send_in],
    )(pin(grads), pick, basis_out, early)
    keep, send = call(
        split_out_kernel, "split_out", (rows(half, F32), rows(half, F32)), after=[got_in]
    )(acc)
    got = lax.ppermute(send, "tensor", core)
    keep, send = call(pair_out_kernel, "pair_out", (rows(wide, F32), rows(wide, BF16)))(keep, got)
    got = lax.ppermute(send, "tensor", across)

    slab = half // dp
    own, next_, far = call(
        round_in_kernel,
        "round_in",
        (rows(slab, BF16), rows(slab, BF16), rows(2 * slab + LABEL_ROWS, BF16)),
    )(keep_in, got_in, label)
    far = swap(far, 2)
    near = call(relay_kernel, "relay_in", rows(2 * (slab + LABEL_ROWS), BF16))(next_, far, label)
    near = swap(near, 1)
    out = call(round_kernel, "round_out", rows(wide, BF16))(keep, got)
    outs = [swap(out, k) for k in LATEST]
    mine = (own, *call(stack_kernel, "stack_in", [rows(3 * slab // 2, BF16)] * 2)(near, far))
    other = [lax.ppermute(x, "tensor", core) for x in mine]
    masked, divisor = call(
        mask_kernel,
        "mask_in",
        (
            jax.ShapeDtypeStruct((experts, dp * cap, dp * 128), BF16),
            jax.ShapeDtypeStruct((experts, 8, 128), F32),
        ),
        [smem] + [vmem] * 9,
    )(expert_counts, *mine, *other, label, near, far)
    result = jax.ShapeDtypeStruct((experts, 128, 128), F32)
    return call(
        blocks_kernel,
        "blocks",
        result,
        scratch=[pltpu.VMEM(result.shape, F32), pltpu.SemaphoreType.DMA((experts,))],
        out_specs=hbm,
    )(divisor, masked, out, *outs)


EX_DEV = 1


def compact(routes, expert, capacity):
    tok_count = routes.shape[0]
    second_hit = routes[:, 1] == expert
    routed = (routes[:, 0] == expert) | second_hit
    order = jnp.cumsum(routed.astype(jnp.int32)) - 1
    slots = jnp.arange(capacity, dtype=jnp.int32)
    match = routed[None, :] & (order[None, :] == slots[:, None])
    token_index = jnp.arange(tok_count, dtype=jnp.int32)
    positions = jnp.sum(jnp.where(match, token_index[None, :], 0), axis=1)
    filled = jnp.any(match, axis=1)
    return (positions, filled, second_hit[positions])


def general(acts, grads, routes, example_ids, expert_counts, basis_in, basis_out):
    capacity = acts.shape[0] // 2
    experts = basis_in.shape[0]
    parts_in, parts_out, label_rows = ([], [], [])
    for expert in range(experts):
        positions, filled, second = compact(routes, expert, capacity)
        chosen = grads[positions]
        grad_rows = jnp.where(second[:, None], chosen[:, 1, :], chosen[:, 0, :])
        parts_in.append(
            jnp.dot(acts[positions], basis_in[expert], preferred_element_type=jnp.float32)
        )
        parts_out.append(jnp.dot(grad_rows, basis_out[expert], preferred_element_type=jnp.float32))
        label_rows.append(jnp.where(filled, example_ids[positions], -1))
    part_in = jnp.stack(parts_in)
    part_out = jnp.stack(parts_out)
    labels = jnp.stack(label_rows)
    slice_width = basis_out.shape[2] // lax.axis_size("tensor")
    summed_in, summed_out = lax.psum((part_in, part_out), "tensor")
    rot_in = summed_in.astype(jnp.bfloat16)
    rot_out = lax.dynamic_slice_in_dim(
        summed_out.astype(jnp.bfloat16), lax.axis_index("tensor") * slice_width, slice_width, 2
    )
    owned_count = EX_DEV
    wanted = jnp.arange(lax.axis_size("dp") * owned_count, dtype=jnp.int32)
    onehot = (labels[:, :, None] == wanted[None, None, :]).astype(jnp.bfloat16)
    spread = onehot[:, :, :, None] * rot_out[:, :, None, :]
    owned_sums = lax.psum_scatter(
        jnp.einsum("ecnw,eca->newa", spread, rot_in, preferred_element_type=jnp.float32),
        "dp",
        scatter_dimension=0,
        tiled=True,
    )
    squared = jnp.sum(owned_sums * owned_sums, axis=0)
    totals = lax.psum_scatter(squared, "dp", scatter_dimension=2, tiled=True)
    return totals / expert_counts.astype(jnp.float32)[:, None, None]


def shards(*args):
    experts, _, width = args[5].shape
    sizes = (lax.axis_size("dp"), lax.axis_size("tensor"), experts, width)
    fits = sizes == (4, 4, 2, 512) and args[0].shape[0] == 384
    return (fast if fits else general)(*args)


def solution(mesh):
    placed = (
        P(("group", "dp"), "tensor"),
        P(("group", "dp"), None, "tensor"),
        P(("group", "dp"), None),
        P(("group", "dp")),
        P("group"),
        P(None, "tensor", None),
        P(None, "tensor", None),
    )
    return jax.shard_map(
        shards, mesh=mesh, in_specs=placed, out_specs=P("group", "tensor", "dp"), check_vma=False
    )
```

```python
import functools

import jax
import jax.numpy as jnp
from jax import lax
from jax.experimental import pallas as pl
from jax.experimental.pallas import tpu as pltpu
from jax.sharding import PartitionSpec as P

F32 = jnp.float32
BF16 = jnp.bfloat16
CHUNK = 1024
VMEM = 20 * 2**20
EARLY = 1024
DISTANCES = (1, 2, 3)
LATEST = (1, 3, 2)
LABEL_ROWS = 16


def iota(shape, dim):
    return lax.broadcasted_iota(jnp.int32, shape, dim)


def dot(a, b):
    return jnp.dot(a, b, preferred_element_type=F32)


def fetcher(sems):
    count = iter(range(sems.shape[0]))

    def fetch(src, dst):
        copy = pltpu.make_async_copy(src, dst, sems.at[next(count)])
        copy.start()
        return copy

    return fetch


def rotate_in_kernel(
    acts, routes, ids, basis_in, grads,
    acc, label, pick, early,
    acts_v, routes_v, ids_v, basis_v, sems,
):
    tokens = acts.shape[0]
    experts = basis_in.shape[0]
    cap = tokens // 2
    fetch = fetcher(sems)
    first = [fetch(routes, routes_v), fetch(ids, ids_v)]
    acts_in = fetch(acts, acts_v)
    bases = [fetch(basis_in.at[e], basis_v.at[e]) for e in range(experts)]
    grads_in = fetch(grads.at[:, :, pl.ds(0, early.shape[2])], early)
    for copy in first:
        copy.wait()
    hits = [
        jnp.max((routes_v[...] == e).astype(F32), axis=0, keepdims=True) for e in range(experts)
    ]
    rows = jnp.concatenate(hits + [jnp.zeros((8 - experts, tokens), F32)], axis=0).astype(BF16)
    upto = (iota((tokens, tokens), 0) <= iota((tokens, tokens), 1)).astype(BF16)
    order = dot(rows, upto)
    slots = iota((cap, tokens), 0).astype(F32) + 1.0
    pick_in = jnp.concatenate(
        [((order[e : e + 1] == slots) & (hits[e] > 0.5)).astype(BF16) for e in range(experts)],
        axis=0,
    )
    repeat = (iota((tokens, 2 * tokens), 0) == iota((tokens, 2 * tokens), 1) // 2).astype(BF16)
    wide = dot(
        jnp.concatenate(
            [order[:experts], routes_v[...].astype(F32), jnp.zeros((6 - experts, tokens), F32)],
            axis=0,
        ).astype(BF16),
        repeat,
    )
    odd = iota((1, 2 * tokens), 1) % 2 == 1
    routed_to = jnp.where(odd, wide[experts + 1 : experts + 2], wide[experts : experts + 1])
    slots = iota((cap, 2 * tokens), 0).astype(F32) + 1.0
    for e in range(experts):
        pick[e * cap : (e + 1) * cap, :] = (
            (wide[e : e + 1] == slots) & (routed_to == float(e))
        ).astype(BF16)
    numbers = jnp.broadcast_to(ids_v[...].reshape(1, tokens).astype(F32) + 1.0, (8, tokens)).astype(BF16)
    named = lax.dot_general(numbers, pick_in, (((1,), (1,)), ((), ())), preferred_element_type=F32)
    block = jnp.zeros((LABEL_ROWS, 128), F32)
    row = iota((LABEL_ROWS, 128), 0)
    half = cap // 2
    for at in range(2 * experts):
        mine = named[0:1, at * half : (at + 1) * half]
        mine = jnp.concatenate([mine, jnp.zeros((1, 128 - half), F32)], axis=1)
        block = jnp.where(row == at, mine, block)
    label[...] = block.astype(BF16)

    acts_in.wait()
    chosen = dot(pick_in, acts_v[...]).astype(BF16)
    for e in range(experts):
        bases[e].wait()
        acc[e] = dot(chosen[e * cap : (e + 1) * cap], basis_v[e])
    grads_in.wait()


def split_in_kernel(acc, keep, send):
    experts, cap, width = acc.shape
    core = lax.rem(lax.axis_index("tensor"), 2)
    half = cap // 2
    at = 0
    for q in range(width // 128):
        for e in range(experts):
            for ref, which in ((keep, core), (send, 1 - core)):
                ref[at : at + half, :] = acc[
                    e, pl.ds(pl.multiple_of(which * half, 8), half), q * 128 : (q + 1) * 128
                ]
            at += half


def choose(pick, rows):
    return dot(pick[...], rows.reshape(2 * rows.shape[0], rows.shape[2])).astype(BF16)


def choose_kernel(grads, pick, out):
    out[...] = choose(pick, grads[...])


def rotate_out_kernel(grads, pick, basis_out, early, acc, grads_v, sems):
    hidden = grads.shape[2]
    experts, cap, _ = acc.shape
    fetch = fetcher(sems)
    done = early.shape[1]
    cuts = sorted({done, done + CHUNK // 2, *range(done + CHUNK, hidden + 1, CHUNK)})
    parts = [(at, pl.ds(at, end - at)) for at, end in zip(cuts, cuts[1:])]
    copies = [
        fetch(grads.at[:, :, part], grads_v.at[:, :, pl.ds(at - done, part.size)])
        for at, part in parts
    ]
    for e in range(experts):
        acc[e] = dot(early[e * cap : (e + 1) * cap, :], basis_out[e, :done, :])
    for (at, part), copy in zip(parts, copies):
        copy.wait()
        chosen = choose(pick, grads_v[:, :, pl.ds(at - done, part.size)])
        for e in range(experts):
            acc[e] += dot(chosen[e * cap : (e + 1) * cap], basis_out[e, part, :])


def split_out_kernel(acc, *refs):
    experts, cap, width = acc.shape
    core = lax.rem(lax.axis_index("tensor"), 2)
    for e in range(experts):
        for ref, which in ((refs[e], core), (refs[experts + e], 1 - core)):
            for x in range(width // 256):
                ref[x * cap : (x + 1) * cap, :] = acc[
                    e, :, pl.ds(pl.multiple_of((2 * x + which) * 128, 128), 128)
                ]


def pair_in_kernel(kept, got, keep, send):
    total = kept[...] + got[...]
    outer = total.shape[0]
    keep[...] = total
    send[:outer, :] = total.astype(BF16)
    send[outer:, :] = jnp.zeros((send.shape[0] - outer, 128), BF16)


def round_in_kernel(kept, got, label, *pays):
    slab = kept.shape[0] // len(pays)
    d = lax.axis_index("dp")
    for k, pay in enumerate(pays):
        rows = pl.ds(pl.multiple_of((d ^ k) * slab, 16), slab)
        pay[:slab, :] = (kept[rows, :] + got[rows, :].astype(F32)).astype(BF16)
        pay[slab:, :] = label[...]


def pair_out_kernel(*refs):
    *given, keep, send = refs
    experts = len(given) // 2
    cap = keep.shape[0] // experts
    x = lax.div(lax.axis_index("tensor"), 2)
    mine = pl.ds(pl.multiple_of(x * cap, 16), cap)
    other = pl.ds(pl.multiple_of((1 - x) * cap, 16), cap)
    for e in range(experts):
        kept, got = given[e], given[experts + e]
        at = pl.ds(e * cap, cap)
        keep[at, :] = kept[mine, :] + got[mine, :]
        send[at, :] = (kept[other, :] + got[other, :]).astype(BF16)


def round_kernel(kept, got, out):
    out[...] = (kept[...] + got[...].astype(F32)).astype(BF16)


def copy_kernel(x, out):
    out[...] = x[: out.shape[0], :]


def stack_kernel(*refs):
    *pieces, first, second = refs
    rows = first.shape[0]
    slab = 2 * rows // len(pieces)
    for k, piece in enumerate(pieces):
        for at in range(0, slab, slab // 2):
            to = k * slab + at
            out = (first, second)[to // rows]
            out[to % rows : to % rows + slab // 2, :] = piece[at : at + slab // 2, :]


def mask_kernel(counts, *refs):
    other, pieces = refs[:3], refs[3:-2]
    out, divisor = refs[-2:]
    experts = out.shape[0]
    slab = pieces[0].shape[0] - LABEL_ROWS
    half = slab // experts
    core = lax.rem(lax.axis_index("tensor"), 2)
    for e in range(experts):
        divisor[e] = jnp.full(divisor.shape[1:], counts[e].astype(F32), F32)
        rows, labels = [], []
        for which, parts in ((core, [piece[:slab, :] for piece in pieces]), (1 - core, other)):
            every = jnp.concatenate([part[...] for part in parts], axis=0)
            for k, piece in enumerate(pieces):
                rows.append(every[k * slab + e * half : k * slab + (e + 1) * half])
                label = piece[slab:, :].astype(F32)[2 * e : 2 * e + 2, :half]
                labels.append(jnp.where(which == 0, label[0:1], label[1:2]))
        rows = jnp.concatenate(rows, axis=0).astype(F32)
        labels = jnp.concatenate(labels, axis=1)
        labels = jnp.broadcast_to(labels, (128, labels.shape[1])).T
        for n in range(len(pieces)):
            out[e, :, n * 128 : (n + 1) * 128] = jnp.where(
                labels == float(n + 1), rows, 0.0
            ).astype(BF16)


def blocks_kernel(divisor, masked, own, *refs):
    *far, result, final, sems = refs
    outs = [own] + [far[LATEST.index(k)] for k in DISTANCES]
    experts, slots, _ = masked.shape
    half = slots // (2 * len(outs))
    core = lax.rem(lax.axis_index("tensor"), 2)
    copies = []
    for e in range(experts):
        rows = [
            ref[pl.ds(pl.multiple_of((2 * e + which) * half, 16), half), :]
            for which in (core, 1 - core)
            for ref in outs
        ]
        blocks = dot(jnp.concatenate(rows, axis=0).T, masked[e])
        squares = blocks * blocks
        summed = squares[:, :128]
        for at in range(128, squares.shape[1], 128):
            summed = summed + squares[:, at : at + 128]
        final[e] = summed / divisor[e][:1]
        copies.append(pltpu.make_async_copy(final.at[e], result.at[e], sems.at[e]))
        copies[-1].start()
    for copy in copies:
        copy.wait()


def call(kernel, name, out_shape, specs=None, scratch=(), out_specs=None, flops=1, after=()):
    vmem = pl.BlockSpec(memory_space=pltpu.VMEM)
    given = {} if out_specs is None else {"out_specs": out_specs}

    def run(*args):
        def body(*refs):
            kernel(*refs[: len(args)], *refs[len(args) + len(after) :])

        return pl.pallas_call(
            body,
            out_shape=out_shape,
            in_specs=(specs or [vmem] * len(args)) + [vmem] * len(after),
            scratch_shapes=scratch,
            compiler_params=pltpu.CompilerParams(vmem_limit_bytes=VMEM),
            cost_estimate=pl.CostEstimate(flops=flops, bytes_accessed=1, transcendentals=0),
            name=name,
            **given,
        )(*args, *after)

    return run


def fast(acts, grads, routes, example_ids, expert_counts, basis_in, basis_out):
    tokens = acts.shape[0]
    experts, features, width = basis_in.shape
    cap = tokens // 2
    dp = lax.axis_size("dp")
    wide = experts * cap
    half = wide * width // 256
    hbm = pl.BlockSpec(memory_space=pltpu.HBM)
    vmem = pl.BlockSpec(memory_space=pltpu.VMEM)
    smem = pl.BlockSpec(memory_space=pltpu.SMEM)

    def pin(x):
        return pltpu.with_memory_space_constraint(x, pltpu.HBM)

    def rows(count, dtype):
        return jax.ShapeDtypeStruct((count, 128), dtype)

    core = [(t, t ^ 1) for t in range(4)]
    across = [(t, t ^ 2) for t in range(4)]

    def swap(x, k):
        return lax.ppermute(x, "dp", [(d, d ^ k) for d in range(dp)])

    partial = jax.ShapeDtypeStruct((experts, cap, width), F32)
    acc, label, pick, early = call(
        rotate_in_kernel,
        "rotate_in",
        (
            partial,
            rows(LABEL_ROWS, BF16),
            jax.ShapeDtypeStruct((wide, 2 * tokens), BF16),
            jax.ShapeDtypeStruct((tokens, 2, EARLY), BF16),
        ),
        [hbm] * 5,
        [
            pltpu.VMEM(acts.shape, BF16),
            pltpu.VMEM((2, tokens), jnp.int32),
            pltpu.VMEM((tokens,), jnp.int32),
            pltpu.VMEM(basis_in.shape, BF16),
            pltpu.SemaphoreType.DMA((4 + experts,)),
        ],
    )(pin(acts), pin(routes.T), pin(example_ids), pin(basis_in), pin(grads))
    keep, send = call(
        split_in_kernel, "split_in", (rows(half, F32), rows(half, F32)), flops=8 * 10**9
    )(acc)
    got = lax.ppermute(send, "tensor", core)
    early = call(choose_kernel, "choose", jax.ShapeDtypeStruct((wide, EARLY), BF16))(early, pick)
    keep_in, send_in = call(
        pair_in_kernel, "pair_in", (rows(half, F32), rows(half + 16, BF16)), after=[early]
    )(keep, got)
    got_in = lax.ppermute(send_in, "tensor", across)

    acc = call(
        rotate_out_kernel,
        "rotate_out",
        partial,
        [hbm, vmem, vmem, vmem],
        [
            pltpu.VMEM((tokens, 2, grads.shape[2] - EARLY), BF16),
            pltpu.SemaphoreType.DMA((grads.shape[2] // CHUNK,)),
        ],
        after=[send_in],
    )(pin(grads), pick, basis_out, early)
    split = call(split_out_kernel, "split_out", [rows(2 * cap, F32)] * (2 * experts))(acc)
    got = [lax.ppermute(x, "tensor", core) for x in split[experts:]]
    keep, send = call(
        pair_out_kernel, "pair_out", (rows(wide, F32), rows(wide, BF16)), after=[got_in]
    )(*split[:experts], *got)
    got = lax.ppermute(send, "tensor", across)

    slab = half // dp
    pieces = call(round_in_kernel, "round_in", [rows(slab + LABEL_ROWS, BF16)] * dp)(
        keep_in, got_in, label
    )
    pieces = [pieces[0]] + [swap(pieces[k], k) for k in DISTANCES]
    own = call(copy_kernel, "own_in", rows(slab, BF16))(pieces[0])
    other = [lax.ppermute(own, "tensor", core)]
    out = call(round_kernel, "round_out", rows(wide, BF16), after=other)(keep, got)
    outs = [swap(out, k) for k in LATEST]
    mine = call(stack_kernel, "stack_in", [rows(3 * slab // 2, BF16)] * 2)(*pieces[1:])
    other += [lax.ppermute(x, "tensor", core) for x in mine]
    masked, divisor = call(
        mask_kernel,
        "mask_in",
        (
            jax.ShapeDtypeStruct((experts, dp * cap, dp * 128), BF16),
            jax.ShapeDtypeStruct((experts, 8, 128), F32),
        ),
        [smem] + [vmem] * (3 + dp),
    )(expert_counts, *other, *pieces)
    result = jax.ShapeDtypeStruct((experts, 128, 128), F32)
    return call(
        blocks_kernel,
        "blocks",
        result,
        scratch=[pltpu.VMEM(result.shape, F32), pltpu.SemaphoreType.DMA((experts,))],
        out_specs=hbm,
    )(divisor, masked, out, *outs)


EX_DEV = 1


def compact(routes, expert, capacity):
    tok_count = routes.shape[0]
    second_hit = routes[:, 1] == expert
    routed = (routes[:, 0] == expert) | second_hit
    order = jnp.cumsum(routed.astype(jnp.int32)) - 1
    slots = jnp.arange(capacity, dtype=jnp.int32)
    match = routed[None, :] & (order[None, :] == slots[:, None])
    token_index = jnp.arange(tok_count, dtype=jnp.int32)
    positions = jnp.sum(jnp.where(match, token_index[None, :], 0), axis=1)
    filled = jnp.any(match, axis=1)
    return (positions, filled, second_hit[positions])


def general(acts, grads, routes, example_ids, expert_counts, basis_in, basis_out):
    capacity = acts.shape[0] // 2
    experts = basis_in.shape[0]
    parts_in, parts_out, label_rows = ([], [], [])
    for expert in range(experts):
        positions, filled, second = compact(routes, expert, capacity)
        chosen = grads[positions]
        grad_rows = jnp.where(second[:, None], chosen[:, 1, :], chosen[:, 0, :])
        parts_in.append(
            jnp.dot(acts[positions], basis_in[expert], preferred_element_type=jnp.float32)
        )
        parts_out.append(jnp.dot(grad_rows, basis_out[expert], preferred_element_type=jnp.float32))
        label_rows.append(jnp.where(filled, example_ids[positions], -1))
    part_in = jnp.stack(parts_in)
    part_out = jnp.stack(parts_out)
    labels = jnp.stack(label_rows)
    slice_width = basis_out.shape[2] // lax.axis_size("tensor")
    summed_in, summed_out = lax.psum((part_in, part_out), "tensor")
    rot_in = summed_in.astype(jnp.bfloat16)
    rot_out = lax.dynamic_slice_in_dim(
        summed_out.astype(jnp.bfloat16), lax.axis_index("tensor") * slice_width, slice_width, 2
    )
    owned_count = EX_DEV
    wanted = jnp.arange(lax.axis_size("dp") * owned_count, dtype=jnp.int32)
    onehot = (labels[:, :, None] == wanted[None, None, :]).astype(jnp.bfloat16)
    spread = onehot[:, :, :, None] * rot_out[:, :, None, :]
    owned_sums = lax.psum_scatter(
        jnp.einsum("ecnw,eca->newa", spread, rot_in, preferred_element_type=jnp.float32),
        "dp",
        scatter_dimension=0,
        tiled=True,
    )
    squared = jnp.sum(owned_sums * owned_sums, axis=0)
    totals = lax.psum_scatter(squared, "dp", scatter_dimension=2, tiled=True)
    return totals / expert_counts.astype(jnp.float32)[:, None, None]


def shards(*args):
    experts, _, width = args[5].shape
    sizes = (lax.axis_size("dp"), lax.axis_size("tensor"), experts, width)
    fits = sizes == (4, 4, 2, 512) and args[0].shape[0] == 384
    return (fast if fits else general)(*args)


def solution(mesh):
    placed = (
        P(("group", "dp"), "tensor"),
        P(("group", "dp"), None, "tensor"),
        P(("group", "dp"), None),
        P(("group", "dp")),
        P("group"),
        P(None, "tensor", None),
        P(None, "tensor", None),
    )
    return jax.shard_map(
        shards, mesh=mesh, in_specs=placed, out_specs=P("group", "tensor", "dp"), check_vma=False
    )
```

```python
import functools

import jax
import jax.numpy as jnp
from jax import lax
from jax.experimental import pallas as pl
from jax.experimental.pallas import tpu as pltpu
from jax.sharding import PartitionSpec as P

F32 = jnp.float32
BF16 = jnp.bfloat16
CHUNK = 1024
VMEM = 20 * 2**20
EARLY = 1024
DISTANCES = (1, 2, 3)
LATEST = (1, 3, 2)
LABEL_ROWS = 16


def iota(shape, dim):
    return lax.broadcasted_iota(jnp.int32, shape, dim)


def dot(a, b):
    return jnp.dot(a, b, preferred_element_type=F32)


def fetcher(sems):
    count = iter(range(sems.shape[0]))

    def fetch(src, dst):
        copy = pltpu.make_async_copy(src, dst, sems.at[next(count)])
        copy.start()
        return copy

    return fetch


def rotate_in_kernel(
    acts, routes, ids, basis_in, grads,
    acc, label, pick, early,
    acts_v, routes_v, ids_v, basis_v, sems,
):
    tokens = acts.shape[0]
    experts = basis_in.shape[0]
    cap = tokens // 2
    fetch = fetcher(sems)
    first = [fetch(routes, routes_v), fetch(ids, ids_v)]
    acts_in = fetch(acts, acts_v)
    bases = [fetch(basis_in.at[e], basis_v.at[e]) for e in range(experts)]
    grads_in = fetch(grads.at[:, :, pl.ds(0, early.shape[2])], early)
    for copy in first:
        copy.wait()
    hits = [
        jnp.max((routes_v[...] == e).astype(F32), axis=0, keepdims=True) for e in range(experts)
    ]
    rows = jnp.concatenate(hits + [jnp.zeros((8 - experts, tokens), F32)], axis=0).astype(BF16)
    upto = (iota((tokens, tokens), 0) <= iota((tokens, tokens), 1)).astype(BF16)
    order = dot(rows, upto)
    slots = iota((cap, tokens), 0).astype(F32) + 1.0
    pick_in = jnp.concatenate(
        [((order[e : e + 1] == slots) & (hits[e] > 0.5)).astype(BF16) for e in range(experts)],
        axis=0,
    )
    repeat = (iota((tokens, 2 * tokens), 0) == iota((tokens, 2 * tokens), 1) // 2).astype(BF16)
    wide = dot(
        jnp.concatenate(
            [order[:experts], routes_v[...].astype(F32), jnp.zeros((6 - experts, tokens), F32)],
            axis=0,
        ).astype(BF16),
        repeat,
    )
    odd = iota((1, 2 * tokens), 1) % 2 == 1
    routed_to = jnp.where(odd, wide[experts + 1 : experts + 2], wide[experts : experts + 1])
    slots = iota((cap, 2 * tokens), 0).astype(F32) + 1.0
    for e in range(experts):
        pick[e * cap : (e + 1) * cap, :] = (
            (wide[e : e + 1] == slots) & (routed_to == float(e))
        ).astype(BF16)
    numbers = jnp.broadcast_to(ids_v[...].reshape(1, tokens).astype(F32) + 1.0, (8, tokens)).astype(BF16)
    named = lax.dot_general(numbers, pick_in, (((1,), (1,)), ((), ())), preferred_element_type=F32)
    block = jnp.zeros((LABEL_ROWS, 128), F32)
    row = iota((LABEL_ROWS, 128), 0)
    half = cap // 2
    for at in range(2 * experts):
        mine = named[0:1, at * half : (at + 1) * half]
        mine = jnp.concatenate([mine, jnp.zeros((1, 128 - half), F32)], axis=1)
        block = jnp.where(row == at, mine, block)
    label[...] = block.astype(BF16)

    acts_in.wait()
    chosen = dot(pick_in, acts_v[...]).astype(BF16)
    for e in range(experts):
        bases[e].wait()
        acc[e] = dot(chosen[e * cap : (e + 1) * cap], basis_v[e])
    grads_in.wait()


def split_in_kernel(acc, keep, send):
    experts, cap, width = acc.shape
    core = lax.rem(lax.axis_index("tensor"), 2)
    half = cap // 2
    at = 0
    for q in range(width // 128):
        for e in range(experts):
            for ref, which in ((keep, core), (send, 1 - core)):
                ref[at : at + half, :] = acc[
                    e, pl.ds(pl.multiple_of(which * half, 8), half), q * 128 : (q + 1) * 128
                ]
            at += half


def choose(pick, rows):
    return dot(pick[...], rows.reshape(2 * rows.shape[0], rows.shape[2])).astype(BF16)


def choose_kernel(grads, pick, out):
    out[...] = choose(pick, grads[...])


def rotate_out_kernel(grads, pick, basis_out, early, acc, grads_v, sems):
    hidden = grads.shape[2]
    experts, cap, _ = acc.shape
    fetch = fetcher(sems)
    done = early.shape[1]
    cuts = sorted({done, done + CHUNK // 2, *range(done + CHUNK, hidden + 1, CHUNK)})
    parts = [(at, pl.ds(at, end - at)) for at, end in zip(cuts, cuts[1:])]
    copies = [
        fetch(grads.at[:, :, part], grads_v.at[:, :, pl.ds(at - done, part.size)])
        for at, part in parts
    ]
    for e in range(experts):
        acc[e] = dot(early[e * cap : (e + 1) * cap, :], basis_out[e, :done, :])
    for (at, part), copy in zip(parts, copies):
        copy.wait()
        chosen = choose(pick, grads_v[:, :, pl.ds(at - done, part.size)])
        for e in range(experts):
            acc[e] += dot(chosen[e * cap : (e + 1) * cap], basis_out[e, part, :])


def split_out_kernel(acc, *refs):
    experts, cap, width = acc.shape
    core = lax.rem(lax.axis_index("tensor"), 2)
    for e in range(experts):
        for ref, which in ((refs[e], core), (refs[experts + e], 1 - core)):
            for x in range(width // 256):
                ref[x * cap : (x + 1) * cap, :] = acc[
                    e, :, pl.ds(pl.multiple_of((2 * x + which) * 128, 128), 128)
                ]


def pair_in_kernel(kept, got, keep, send):
    total = kept[...] + got[...]
    keep[...] = total
    send[...] = total.astype(BF16)


def round_in_kernel(kept, got, label, *pays):
    slab = kept.shape[0] // len(pays)
    d = lax.axis_index("dp")
    for k, pay in enumerate(pays):
        rows = pl.ds(pl.multiple_of((d ^ k) * slab, 16), slab)
        pay[:slab, :] = (kept[rows, :] + got[rows, :].astype(F32)).astype(BF16)
        pay[slab:, :] = label[...]


def pair_out_kernel(*refs):
    *given, keep, send = refs
    experts = len(given) // 2
    cap = keep.shape[0] // experts
    x = lax.div(lax.axis_index("tensor"), 2)
    mine = pl.ds(pl.multiple_of(x * cap, 16), cap)
    other = pl.ds(pl.multiple_of((1 - x) * cap, 16), cap)
    for e in range(experts):
        kept, got = given[e], given[experts + e]
        at = pl.ds(e * cap, cap)
        keep[at, :] = kept[mine, :] + got[mine, :]
        send[at, :] = (kept[other, :] + got[other, :]).astype(BF16)


def round_kernel(kept, got, out):
    out[...] = (kept[...] + got[...].astype(F32)).astype(BF16)


def copy_kernel(x, out):
    out[...] = x[: out.shape[0], :]


def stack_kernel(*refs):
    *pieces, first, second = refs
    rows = first.shape[0]
    slab = 2 * rows // len(pieces)
    for k, piece in enumerate(pieces):
        for at in range(0, slab, slab // 2):
            to = k * slab + at
            out = (first, second)[to // rows]
            out[to % rows : to % rows + slab // 2, :] = piece[at : at + slab // 2, :]


def mask(which, parts, pieces, out):
    experts, slots, _ = out.shape
    half = slots // len(pieces)
    slab = experts * half
    every = jnp.concatenate(parts, axis=0).astype(F32)
    for e in range(experts):
        rows, labels = [], []
        for k, piece in enumerate(pieces):
            rows.append(every[k * slab + e * half : k * slab + (e + 1) * half])
            label = piece[slab : slab + LABEL_ROWS, :].astype(F32)[2 * e : 2 * e + 2, :half]
            labels.append(jnp.where(which == 0, label[0:1], label[1:2]))
        rows = jnp.concatenate(rows, axis=0)
        labels = jnp.concatenate(labels, axis=1)
        labels = jnp.broadcast_to(labels, (128, labels.shape[1])).T
        for n in range(len(pieces)):
            out[e, :, n * 128 : (n + 1) * 128] = jnp.where(
                labels == float(n + 1), rows, 0.0
            ).astype(BF16)


def mask_own_kernel(counts, *refs):
    *pieces, out, divisor = refs
    slab = out.shape[0] * out.shape[1] // len(pieces)
    core = lax.rem(lax.axis_index("tensor"), 2)
    mask(core, [piece[:slab, :] for piece in pieces], pieces, out)
    for e in range(out.shape[0]):
        divisor[e] = jnp.full(divisor.shape[1:], counts[e].astype(F32), F32)


def mask_other_kernel(first, second, third, *refs):
    *pieces, out = refs
    core = lax.rem(lax.axis_index("tensor"), 2)
    mask(1 - core, [first[...], second[...], third[...]], pieces, out)


def blocks_kernel(divisor, masked_own, masked_other, own, *refs):
    *far, result, final, sems = refs
    outs = [own] + [far[LATEST.index(k)] for k in DISTANCES]
    experts, slots, _ = masked_own.shape
    half = slots // len(outs)
    core = lax.rem(lax.axis_index("tensor"), 2)
    copies = []
    for e in range(experts):
        rows = [
            ref[pl.ds(pl.multiple_of((2 * e + which) * half, 16), half), :]
            for which in (core, 1 - core)
            for ref in outs
        ]
        rows = jnp.concatenate(rows, axis=0).T
        blocks = dot(rows[:, :slots], masked_own[e]) + dot(rows[:, slots:], masked_other[e])
        squares = blocks * blocks
        summed = squares[:, :128]
        for at in range(128, squares.shape[1], 128):
            summed = summed + squares[:, at : at + 128]
        final[e] = summed / divisor[e][:1]
        copies.append(pltpu.make_async_copy(final.at[e], result.at[e], sems.at[e]))
        copies[-1].start()
    for copy in copies:
        copy.wait()


def call(kernel, name, out_shape, specs=None, scratch=(), out_specs=None, flops=1, after=()):
    vmem = pl.BlockSpec(memory_space=pltpu.VMEM)
    given = {} if out_specs is None else {"out_specs": out_specs}

    def run(*args):
        def body(*refs):
            kernel(*refs[: len(args)], *refs[len(args) + len(after) :])

        return pl.pallas_call(
            body,
            out_shape=out_shape,
            in_specs=(specs or [vmem] * len(args)) + [vmem] * len(after),
            scratch_shapes=scratch,
            compiler_params=pltpu.CompilerParams(vmem_limit_bytes=VMEM),
            cost_estimate=pl.CostEstimate(flops=flops, bytes_accessed=1, transcendentals=0),
            name=name,
            **given,
        )(*args, *after)

    return run


def fast(acts, grads, routes, example_ids, expert_counts, basis_in, basis_out):
    tokens = acts.shape[0]
    experts, features, width = basis_in.shape
    cap = tokens // 2
    dp = lax.axis_size("dp")
    wide = experts * cap
    half = wide * width // 256
    hbm = pl.BlockSpec(memory_space=pltpu.HBM)
    vmem = pl.BlockSpec(memory_space=pltpu.VMEM)
    smem = pl.BlockSpec(memory_space=pltpu.SMEM)

    def pin(x):
        return pltpu.with_memory_space_constraint(x, pltpu.HBM)

    def rows(count, dtype):
        return jax.ShapeDtypeStruct((count, 128), dtype)

    core = [(t, t ^ 1) for t in range(4)]
    across = [(t, t ^ 2) for t in range(4)]

    def swap(x, k):
        return lax.ppermute(x, "dp", [(d, d ^ k) for d in range(dp)])

    partial = jax.ShapeDtypeStruct((experts, cap, width), F32)
    acc, label, pick, early = call(
        rotate_in_kernel,
        "rotate_in",
        (
            partial,
            rows(LABEL_ROWS, BF16),
            jax.ShapeDtypeStruct((wide, 2 * tokens), BF16),
            jax.ShapeDtypeStruct((tokens, 2, EARLY), BF16),
        ),
        [hbm] * 5,
        [
            pltpu.VMEM(acts.shape, BF16),
            pltpu.VMEM((2, tokens), jnp.int32),
            pltpu.VMEM((tokens,), jnp.int32),
            pltpu.VMEM(basis_in.shape, BF16),
            pltpu.SemaphoreType.DMA((4 + experts,)),
        ],
    )(pin(acts), pin(routes.T), pin(example_ids), pin(basis_in), pin(grads))
    keep, send = call(
        split_in_kernel, "split_in", (rows(half, F32), rows(half, F32)), flops=8 * 10**9
    )(acc)
    got = lax.ppermute(send, "tensor", core)
    early = call(choose_kernel, "choose", jax.ShapeDtypeStruct((wide, EARLY), BF16))(early, pick)
    keep_in, send_in = call(
        pair_in_kernel, "pair_in", (rows(half, F32), rows(half, BF16)), after=[early]
    )(keep, got)
    got_in = lax.ppermute(send_in, "tensor", across)

    acc = call(
        rotate_out_kernel,
        "rotate_out",
        partial,
        [hbm, vmem, vmem, vmem],
        [
            pltpu.VMEM((tokens, 2, grads.shape[2] - EARLY), BF16),
            pltpu.SemaphoreType.DMA((grads.shape[2] // CHUNK,)),
        ],
        after=[send_in],
    )(pin(grads), pick, basis_out, early)
    split = call(split_out_kernel, "split_out", [rows(2 * cap, F32)] * (2 * experts))(acc)
    got = [lax.ppermute(x, "tensor", core) for x in split[experts:]]
    slab = half // dp
    pieces = call(round_in_kernel, "round_in", [rows(slab + LABEL_ROWS, BF16)] * dp)(
        keep_in, got_in, label
    )
    own = call(copy_kernel, "own_in", rows(slab, BF16))(pieces[0])
    other = [lax.ppermute(own, "tensor", core)]
    keep, send = call(
        pair_out_kernel, "pair_out", (rows(wide, F32), rows(wide, BF16)), after=other
    )(*split[:experts], *got)
    got = lax.ppermute(send, "tensor", across)
    pieces = [pieces[0]] + [swap(pieces[k], k) for k in DISTANCES]
    out = call(round_kernel, "round_out", rows(wide, BF16))(keep, got)
    outs = [swap(out, k) for k in LATEST]
    mine = call(stack_kernel, "stack_in", [rows(3 * slab // 2, BF16)] * 2)(*pieces[1:])
    other += [lax.ppermute(x, "tensor", core) for x in mine]
    masked = jax.ShapeDtypeStruct((experts, dp * cap // 2, dp * 128), BF16)
    masked_own, divisor = call(
        mask_own_kernel,
        "mask_own",
        (masked, jax.ShapeDtypeStruct((experts, 8, 128), F32)),
        [smem] + [vmem] * dp,
    )(expert_counts, *pieces)
    masked_other = call(mask_other_kernel, "mask_other", masked, after=[divisor])(*other, *pieces)
    result = jax.ShapeDtypeStruct((experts, 128, 128), F32)
    return call(
        blocks_kernel,
        "blocks",
        result,
        scratch=[pltpu.VMEM(result.shape, F32), pltpu.SemaphoreType.DMA((experts,))],
        out_specs=hbm,
    )(divisor, masked_own, masked_other, out, *outs)


EX_DEV = 1


def compact(routes, expert, capacity):
    tok_count = routes.shape[0]
    second_hit = routes[:, 1] == expert
    routed = (routes[:, 0] == expert) | second_hit
    order = jnp.cumsum(routed.astype(jnp.int32)) - 1
    slots = jnp.arange(capacity, dtype=jnp.int32)
    match = routed[None, :] & (order[None, :] == slots[:, None])
    token_index = jnp.arange(tok_count, dtype=jnp.int32)
    positions = jnp.sum(jnp.where(match, token_index[None, :], 0), axis=1)
    filled = jnp.any(match, axis=1)
    return (positions, filled, second_hit[positions])


def general(acts, grads, routes, example_ids, expert_counts, basis_in, basis_out):
    capacity = acts.shape[0] // 2
    experts = basis_in.shape[0]
    parts_in, parts_out, label_rows = ([], [], [])
    for expert in range(experts):
        positions, filled, second = compact(routes, expert, capacity)
        chosen = grads[positions]
        grad_rows = jnp.where(second[:, None], chosen[:, 1, :], chosen[:, 0, :])
        parts_in.append(
            jnp.dot(acts[positions], basis_in[expert], preferred_element_type=jnp.float32)
        )
        parts_out.append(jnp.dot(grad_rows, basis_out[expert], preferred_element_type=jnp.float32))
        label_rows.append(jnp.where(filled, example_ids[positions], -1))
    part_in = jnp.stack(parts_in)
    part_out = jnp.stack(parts_out)
    labels = jnp.stack(label_rows)
    slice_width = basis_out.shape[2] // lax.axis_size("tensor")
    summed_in, summed_out = lax.psum((part_in, part_out), "tensor")
    rot_in = summed_in.astype(jnp.bfloat16)
    rot_out = lax.dynamic_slice_in_dim(
        summed_out.astype(jnp.bfloat16), lax.axis_index("tensor") * slice_width, slice_width, 2
    )
    owned_count = EX_DEV
    wanted = jnp.arange(lax.axis_size("dp") * owned_count, dtype=jnp.int32)
    onehot = (labels[:, :, None] == wanted[None, None, :]).astype(jnp.bfloat16)
    spread = onehot[:, :, :, None] * rot_out[:, :, None, :]
    owned_sums = lax.psum_scatter(
        jnp.einsum("ecnw,eca->newa", spread, rot_in, preferred_element_type=jnp.float32),
        "dp",
        scatter_dimension=0,
        tiled=True,
    )
    squared = jnp.sum(owned_sums * owned_sums, axis=0)
    totals = lax.psum_scatter(squared, "dp", scatter_dimension=2, tiled=True)
    return totals / expert_counts.astype(jnp.float32)[:, None, None]


def shards(*args):
    experts, _, width = args[5].shape
    sizes = (lax.axis_size("dp"), lax.axis_size("tensor"), experts, width)
    fits = sizes == (4, 4, 2, 512) and args[0].shape[0] == 384
    return (fast if fits else general)(*args)


def solution(mesh):
    placed = (
        P(("group", "dp"), "tensor"),
        P(("group", "dp"), None, "tensor"),
        P(("group", "dp"), None),
        P(("group", "dp")),
        P("group"),
        P(None, "tensor", None),
        P(None, "tensor", None),
    )
    return jax.shard_map(
        shards, mesh=mesh, in_specs=placed, out_specs=P("group", "tensor", "dp"), check_vma=False
    )
```

```python
import functools

import jax
import jax.numpy as jnp
from jax import lax
from jax.experimental import pallas as pl
from jax.experimental.pallas import tpu as pltpu
from jax.sharding import PartitionSpec as P

F32 = jnp.float32
BF16 = jnp.bfloat16
CHUNK = 1024
VMEM = 20 * 2**20
EARLY = 1536
DISTANCES = (1, 2, 3)
LATEST = (1, 3, 2)
LABEL_ROWS = 16


def iota(shape, dim):
    return lax.broadcasted_iota(jnp.int32, shape, dim)


def dot(a, b):
    return jnp.dot(a, b, preferred_element_type=F32)


def fetcher(sems):
    count = iter(range(sems.shape[0]))

    def fetch(src, dst):
        copy = pltpu.make_async_copy(src, dst, sems.at[next(count)])
        copy.start()
        return copy

    return fetch


def rotate_in_kernel(
    acts, routes, ids, basis_in, grads,
    acc, label, pick, early,
    acts_v, routes_v, ids_v, basis_v, sems,
):
    tokens = acts.shape[0]
    experts = basis_in.shape[0]
    cap = tokens // 2
    fetch = fetcher(sems)
    first = [fetch(routes, routes_v), fetch(ids, ids_v)]
    acts_in = fetch(acts, acts_v)
    bases = [fetch(basis_in.at[e], basis_v.at[e]) for e in range(experts)]
    grads_in = fetch(grads.at[:, :, pl.ds(0, early.shape[2])], early)
    for copy in first:
        copy.wait()
    hits = [
        jnp.max((routes_v[...] == e).astype(F32), axis=0, keepdims=True) for e in range(experts)
    ]
    rows = jnp.concatenate(hits + [jnp.zeros((8 - experts, tokens), F32)], axis=0).astype(BF16)
    upto = (iota((tokens, tokens), 0) <= iota((tokens, tokens), 1)).astype(BF16)
    order = dot(rows, upto)
    slots = iota((cap, tokens), 0).astype(F32) + 1.0
    pick_in = jnp.concatenate(
        [((order[e : e + 1] == slots) & (hits[e] > 0.5)).astype(BF16) for e in range(experts)],
        axis=0,
    )
    repeat = (iota((tokens, 2 * tokens), 0) == iota((tokens, 2 * tokens), 1) // 2).astype(BF16)
    wide = dot(
        jnp.concatenate(
            [order[:experts], routes_v[...].astype(F32), jnp.zeros((6 - experts, tokens), F32)],
            axis=0,
        ).astype(BF16),
        repeat,
    )
    odd = iota((1, 2 * tokens), 1) % 2 == 1
    routed_to = jnp.where(odd, wide[experts + 1 : experts + 2], wide[experts : experts + 1])
    slots = iota((cap, 2 * tokens), 0).astype(F32) + 1.0
    for e in range(experts):
        pick[e * cap : (e + 1) * cap, :] = (
            (wide[e : e + 1] == slots) & (routed_to == float(e))
        ).astype(BF16)
    numbers = jnp.broadcast_to(ids_v[...].reshape(1, tokens).astype(F32) + 1.0, (8, tokens)).astype(BF16)
    named = lax.dot_general(numbers, pick_in, (((1,), (1,)), ((), ())), preferred_element_type=F32)
    block = jnp.zeros((LABEL_ROWS, 128), F32)
    row = iota((LABEL_ROWS, 128), 0)
    half = cap // 2
    for at in range(2 * experts):
        mine = named[0:1, at * half : (at + 1) * half]
        mine = jnp.concatenate([mine, jnp.zeros((1, 128 - half), F32)], axis=1)
        block = jnp.where(row == at, mine, block)
    label[...] = block.astype(BF16)

    acts_in.wait()
    chosen = dot(pick_in, acts_v[...]).astype(BF16)
    for e in range(experts):
        bases[e].wait()
        acc[e] = dot(chosen[e * cap : (e + 1) * cap], basis_v[e])
    grads_in.wait()


def split_in_kernel(acc, keep, send):
    experts, cap, width = acc.shape
    core = lax.rem(lax.axis_index("tensor"), 2)
    half = cap // 2
    at = 0
    for q in range(width // 128):
        for e in range(experts):
            for ref, which in ((keep, core), (send, 1 - core)):
                ref[at : at + half, :] = acc[
                    e, pl.ds(pl.multiple_of(which * half, 8), half), q * 128 : (q + 1) * 128
                ]
            at += half


def choose(pick, rows):
    return dot(pick[...], rows.reshape(2 * rows.shape[0], rows.shape[2])).astype(BF16)


def choose_kernel(grads, pick, out):
    out[...] = choose(pick, grads[...])


def rotate_out_kernel(grads, pick, basis_out, early, acc, grads_v, sems):
    hidden = grads.shape[2]
    experts, cap, _ = acc.shape
    fetch = fetcher(sems)
    done = early.shape[1]
    cuts = sorted({done, done + CHUNK // 2, *range(done + CHUNK, hidden, CHUNK), hidden})
    parts = [(at, pl.ds(at, end - at)) for at, end in zip(cuts, cuts[1:])]
    copies = [
        fetch(grads.at[:, :, part], grads_v.at[:, :, pl.ds(at - done, part.size)])
        for at, part in parts
    ]
    for e in range(experts):
        acc[e] = dot(early[e * cap : (e + 1) * cap, :], basis_out[e, :done, :])
    for (at, part), copy in zip(parts, copies):
        copy.wait()
        chosen = choose(pick, grads_v[:, :, pl.ds(at - done, part.size)])
        for e in range(experts):
            acc[e] += dot(chosen[e * cap : (e + 1) * cap], basis_out[e, part, :])


def split_out_kernel(acc, *refs):
    experts, cap, width = acc.shape
    core = lax.rem(lax.axis_index("tensor"), 2)
    for e in range(experts):
        for ref, which in ((refs[e], core), (refs[experts + e], 1 - core)):
            for x in range(width // 256):
                ref[x * cap : (x + 1) * cap, :] = acc[
                    e, :, pl.ds(pl.multiple_of((2 * x + which) * 128, 128), 128)
                ]


def pair_in_kernel(kept, got, keep, send):
    total = kept[...] + got[...]
    outer = total.shape[0]
    keep[...] = total
    send[:outer, :] = total.astype(BF16)
    send[outer:, :] = jnp.zeros((send.shape[0] - outer, 128), BF16)


def round_in_kernel(kept, got, label, *pays):
    slab = kept.shape[0] // len(pays)
    d = lax.axis_index("dp")
    for k, pay in enumerate(pays):
        rows = pl.ds(pl.multiple_of((d ^ k) * slab, 16), slab)
        pay[:slab, :] = (kept[rows, :] + got[rows, :].astype(F32)).astype(BF16)
        pay[slab:, :] = label[...]


def pair_out_kernel(*refs):
    *given, keep, send = refs
    experts = len(given) // 2
    cap = keep.shape[0] // experts
    x = lax.div(lax.axis_index("tensor"), 2)
    mine = pl.ds(pl.multiple_of(x * cap, 16), cap)
    other = pl.ds(pl.multiple_of((1 - x) * cap, 16), cap)
    for e in range(experts):
        kept, got = given[e], given[experts + e]
        at = pl.ds(e * cap, cap)
        keep[at, :] = kept[mine, :] + got[mine, :]
        send[at, :] = (kept[other, :] + got[other, :]).astype(BF16)


def round_kernel(kept, got, out):
    out[...] = (kept[...] + got[...].astype(F32)).astype(BF16)


def copy_kernel(x, out):
    out[...] = x[: out.shape[0], :]


def stack_kernel(*refs):
    *pieces, first, second = refs
    rows = first.shape[0]
    slab = 2 * rows // len(pieces)
    for k, piece in enumerate(pieces):
        for at in range(0, slab, slab // 2):
            to = k * slab + at
            out = (first, second)[to // rows]
            out[to % rows : to % rows + slab // 2, :] = piece[at : at + slab // 2, :]


def mask(which, parts, pieces, out):
    experts, slots, _ = out.shape
    half = slots // len(pieces)
    slab = experts * half
    every = jnp.concatenate(parts, axis=0).astype(F32)
    for e in range(experts):
        rows, labels = [], []
        for k, piece in enumerate(pieces):
            rows.append(every[k * slab + e * half : k * slab + (e + 1) * half])
            label = piece[slab : slab + LABEL_ROWS, :].astype(F32)[2 * e : 2 * e + 2, :half]
            labels.append(jnp.where(which == 0, label[0:1], label[1:2]))
        rows = jnp.concatenate(rows, axis=0)
        labels = jnp.concatenate(labels, axis=1)
        labels = jnp.broadcast_to(labels, (128, labels.shape[1])).T
        for n in range(len(pieces)):
            out[e, :, n * 128 : (n + 1) * 128] = jnp.where(
                labels == float(n + 1), rows, 0.0
            ).astype(BF16)


def mask_own_kernel(counts, *refs):
    *pieces, out, divisor = refs
    slab = out.shape[0] * out.shape[1] // len(pieces)
    core = lax.rem(lax.axis_index("tensor"), 2)
    mask(core, [piece[:slab, :] for piece in pieces], pieces, out)
    for e in range(out.shape[0]):
        divisor[e] = jnp.full(divisor.shape[1:], counts[e].astype(F32), F32)


def mask_other_kernel(first, second, third, *refs):
    *pieces, out = refs
    core = lax.rem(lax.axis_index("tensor"), 2)
    mask(1 - core, [first[...], second[...], third[...]], pieces, out)


def blocks_kernel(divisor, masked_own, masked_other, own, *refs):
    *far, result, final, sems = refs
    outs = [own] + [far[LATEST.index(k)] for k in DISTANCES]
    experts, slots, _ = masked_own.shape
    half = slots // len(outs)
    core = lax.rem(lax.axis_index("tensor"), 2)
    copies = []
    for e in range(experts):
        rows = [
            ref[pl.ds(pl.multiple_of((2 * e + which) * half, 16), half), :]
            for which in (core, 1 - core)
            for ref in outs
        ]
        rows = jnp.concatenate(rows, axis=0).T
        blocks = dot(rows[:, :slots], masked_own[e]) + dot(rows[:, slots:], masked_other[e])
        squares = blocks * blocks
        summed = squares[:, :128]
        for at in range(128, squares.shape[1], 128):
            summed = summed + squares[:, at : at + 128]
        final[e] = summed / divisor[e][:1]
        copies.append(pltpu.make_async_copy(final.at[e], result.at[e], sems.at[e]))
        copies[-1].start()
    for copy in copies:
        copy.wait()


def call(kernel, name, out_shape, specs=None, scratch=(), out_specs=None, flops=1, after=()):
    vmem = pl.BlockSpec(memory_space=pltpu.VMEM)
    given = {} if out_specs is None else {"out_specs": out_specs}

    def run(*args):
        def body(*refs):
            kernel(*refs[: len(args)], *refs[len(args) + len(after) :])

        return pl.pallas_call(
            body,
            out_shape=out_shape,
            in_specs=(specs or [vmem] * len(args)) + [vmem] * len(after),
            scratch_shapes=scratch,
            compiler_params=pltpu.CompilerParams(vmem_limit_bytes=VMEM),
            cost_estimate=pl.CostEstimate(flops=flops, bytes_accessed=1, transcendentals=0),
            name=name,
            **given,
        )(*args, *after)

    return run


def fast(acts, grads, routes, example_ids, expert_counts, basis_in, basis_out):
    tokens = acts.shape[0]
    experts, features, width = basis_in.shape
    cap = tokens // 2
    dp = lax.axis_size("dp")
    wide = experts * cap
    half = wide * width // 256
    hbm = pl.BlockSpec(memory_space=pltpu.HBM)
    vmem = pl.BlockSpec(memory_space=pltpu.VMEM)
    smem = pl.BlockSpec(memory_space=pltpu.SMEM)

    def pin(x):
        return pltpu.with_memory_space_constraint(x, pltpu.HBM)

    def rows(count, dtype):
        return jax.ShapeDtypeStruct((count, 128), dtype)

    core = [(t, t ^ 1) for t in range(4)]
    across = [(t, t ^ 2) for t in range(4)]

    def swap(x, k):
        return lax.ppermute(x, "dp", [(d, d ^ k) for d in range(dp)])

    partial = jax.ShapeDtypeStruct((experts, cap, width), F32)
    acc, label, pick, early = call(
        rotate_in_kernel,
        "rotate_in",
        (
            partial,
            rows(LABEL_ROWS, BF16),
            jax.ShapeDtypeStruct((wide, 2 * tokens), BF16),
            jax.ShapeDtypeStruct((tokens, 2, EARLY), BF16),
        ),
        [hbm] * 5,
        [
            pltpu.VMEM(acts.shape, BF16),
            pltpu.VMEM((2, tokens), jnp.int32),
            pltpu.VMEM((tokens,), jnp.int32),
            pltpu.VMEM(basis_in.shape, BF16),
            pltpu.SemaphoreType.DMA((4 + experts,)),
        ],
    )(pin(acts), pin(routes.T), pin(example_ids), pin(basis_in), pin(grads))
    keep, send = call(
        split_in_kernel, "split_in", (rows(half, F32), rows(half, F32)), flops=8 * 10**9
    )(acc)
    got = lax.ppermute(send, "tensor", core)
    early = call(choose_kernel, "choose", jax.ShapeDtypeStruct((wide, EARLY), BF16))(early, pick)
    keep_in, send_in = call(
        pair_in_kernel, "pair_in", (rows(half, F32), rows(half + 16, BF16)), after=[early]
    )(keep, got)
    got_in = lax.ppermute(send_in, "tensor", across)

    acc = call(
        rotate_out_kernel,
        "rotate_out",
        partial,
        [hbm, vmem, vmem, vmem],
        [
            pltpu.VMEM((tokens, 2, grads.shape[2] - EARLY), BF16),
            pltpu.SemaphoreType.DMA((grads.shape[2] // CHUNK + 1,)),
        ],
        after=[send_in],
    )(pin(grads), pick, basis_out, early)
    split = call(split_out_kernel, "split_out", [rows(2 * cap, F32)] * (2 * experts))(acc)
    got = [lax.ppermute(x, "tensor", core) for x in split[experts:]]
    keep, send = call(
        pair_out_kernel, "pair_out", (rows(wide, F32), rows(wide, BF16)), after=[got_in]
    )(*split[:experts], *got)
    got = lax.ppermute(send, "tensor", across)

    slab = half // dp
    pieces = call(round_in_kernel, "round_in", [rows(slab + LABEL_ROWS, BF16)] * dp)(
        keep_in, got_in, label
    )
    own = call(copy_kernel, "own_in", rows(slab, BF16))(pieces[0])
    other = [lax.ppermute(own, "tensor", core)]
    pieces = [pieces[0]] + [swap(pieces[k], k) for k in DISTANCES]
    out = call(round_kernel, "round_out", rows(wide, BF16), after=other)(keep, got)
    outs = [swap(out, k) for k in LATEST]
    mine = call(stack_kernel, "stack_in", [rows(3 * slab // 2, BF16)] * 2)(*pieces[1:])
    other += [lax.ppermute(x, "tensor", core) for x in mine]
    masked = jax.ShapeDtypeStruct((experts, dp * cap // 2, dp * 128), BF16)
    masked_own, divisor = call(
        mask_own_kernel,
        "mask_own",
        (masked, jax.ShapeDtypeStruct((experts, 8, 128), F32)),
        [smem] + [vmem] * dp,
    )(expert_counts, *pieces)
    masked_other = call(mask_other_kernel, "mask_other", masked, after=[divisor])(*other, *pieces)
    result = jax.ShapeDtypeStruct((experts, 128, 128), F32)
    return call(
        blocks_kernel,
        "blocks",
        result,
        scratch=[pltpu.VMEM(result.shape, F32), pltpu.SemaphoreType.DMA((experts,))],
        out_specs=hbm,
    )(divisor, masked_own, masked_other, out, *outs)


EX_DEV = 1


def compact(routes, expert, capacity):
    tok_count = routes.shape[0]
    second_hit = routes[:, 1] == expert
    routed = (routes[:, 0] == expert) | second_hit
    order = jnp.cumsum(routed.astype(jnp.int32)) - 1
    slots = jnp.arange(capacity, dtype=jnp.int32)
    match = routed[None, :] & (order[None, :] == slots[:, None])
    token_index = jnp.arange(tok_count, dtype=jnp.int32)
    positions = jnp.sum(jnp.where(match, token_index[None, :], 0), axis=1)
    filled = jnp.any(match, axis=1)
    return (positions, filled, second_hit[positions])


def general(acts, grads, routes, example_ids, expert_counts, basis_in, basis_out):
    capacity = acts.shape[0] // 2
    experts = basis_in.shape[0]
    parts_in, parts_out, label_rows = ([], [], [])
    for expert in range(experts):
        positions, filled, second = compact(routes, expert, capacity)
        chosen = grads[positions]
        grad_rows = jnp.where(second[:, None], chosen[:, 1, :], chosen[:, 0, :])
        parts_in.append(
            jnp.dot(acts[positions], basis_in[expert], preferred_element_type=jnp.float32)
        )
        parts_out.append(jnp.dot(grad_rows, basis_out[expert], preferred_element_type=jnp.float32))
        label_rows.append(jnp.where(filled, example_ids[positions], -1))
    part_in = jnp.stack(parts_in)
    part_out = jnp.stack(parts_out)
    labels = jnp.stack(label_rows)
    slice_width = basis_out.shape[2] // lax.axis_size("tensor")
    summed_in, summed_out = lax.psum((part_in, part_out), "tensor")
    rot_in = summed_in.astype(jnp.bfloat16)
    rot_out = lax.dynamic_slice_in_dim(
        summed_out.astype(jnp.bfloat16), lax.axis_index("tensor") * slice_width, slice_width, 2
    )
    owned_count = EX_DEV
    wanted = jnp.arange(lax.axis_size("dp") * owned_count, dtype=jnp.int32)
    onehot = (labels[:, :, None] == wanted[None, None, :]).astype(jnp.bfloat16)
    spread = onehot[:, :, :, None] * rot_out[:, :, None, :]
    owned_sums = lax.psum_scatter(
        jnp.einsum("ecnw,eca->newa", spread, rot_in, preferred_element_type=jnp.float32),
        "dp",
        scatter_dimension=0,
        tiled=True,
    )
    squared = jnp.sum(owned_sums * owned_sums, axis=0)
    totals = lax.psum_scatter(squared, "dp", scatter_dimension=2, tiled=True)
    return totals / expert_counts.astype(jnp.float32)[:, None, None]


def shards(*args):
    experts, _, width = args[5].shape
    sizes = (lax.axis_size("dp"), lax.axis_size("tensor"), experts, width)
    fits = sizes == (4, 4, 2, 512) and args[0].shape[0] == 384
    return (fast if fits else general)(*args)


def solution(mesh):
    placed = (
        P(("group", "dp"), "tensor"),
        P(("group", "dp"), None, "tensor"),
        P(("group", "dp"), None),
        P(("group", "dp")),
        P("group"),
        P(None, "tensor", None),
        P(None, "tensor", None),
    )
    return jax.shard_map(
        shards, mesh=mesh, in_specs=placed, out_specs=P("group", "tensor", "dp"), check_vma=False
    )
```

```python
import functools

import jax
import jax.numpy as jnp
from jax import lax
from jax.experimental import pallas as pl
from jax.experimental.pallas import tpu as pltpu
from jax.sharding import PartitionSpec as P

F32 = jnp.float32
BF16 = jnp.bfloat16
CHUNK = 1024
VMEM = 20 * 2**20
EARLY = 1536
DISTANCES = (1, 2, 3)
LABEL_ROWS = 16


def iota(shape, dim):
    return lax.broadcasted_iota(jnp.int32, shape, dim)


def dot(a, b):
    return jnp.dot(a, b, preferred_element_type=F32)


def fetcher(sems):
    count = iter(range(sems.shape[0]))

    def fetch(src, dst):
        copy = pltpu.make_async_copy(src, dst, sems.at[next(count)])
        copy.start()
        return copy

    return fetch


def rotate_in_kernel(
    acts, routes, ids, basis_in, grads,
    acc, label, pick, early,
    acts_v, routes_v, ids_v, basis_v, sems,
):
    tokens = acts.shape[0]
    experts = basis_in.shape[0]
    cap = tokens // 2
    fetch = fetcher(sems)
    first = [fetch(routes, routes_v), fetch(ids, ids_v)]
    acts_in = fetch(acts, acts_v)
    bases = [fetch(basis_in.at[e], basis_v.at[e]) for e in range(experts)]
    grads_in = fetch(grads.at[:, :, pl.ds(0, early.shape[2])], early)
    for copy in first:
        copy.wait()
    hits = [
        jnp.max((routes_v[...] == e).astype(F32), axis=0, keepdims=True) for e in range(experts)
    ]
    rows = jnp.concatenate(hits + [jnp.zeros((8 - experts, tokens), F32)], axis=0).astype(BF16)
    upto = (iota((tokens, tokens), 0) <= iota((tokens, tokens), 1)).astype(BF16)
    order = dot(rows, upto)
    slots = iota((cap, tokens), 0).astype(F32) + 1.0
    pick_in = jnp.concatenate(
        [((order[e : e + 1] == slots) & (hits[e] > 0.5)).astype(BF16) for e in range(experts)],
        axis=0,
    )
    repeat = (iota((tokens, 2 * tokens), 0) == iota((tokens, 2 * tokens), 1) // 2).astype(BF16)
    wide = dot(
        jnp.concatenate(
            [order[:experts], routes_v[...].astype(F32), jnp.zeros((6 - experts, tokens), F32)],
            axis=0,
        ).astype(BF16),
        repeat,
    )
    odd = iota((1, 2 * tokens), 1) % 2 == 1
    routed_to = jnp.where(odd, wide[experts + 1 : experts + 2], wide[experts : experts + 1])
    slots = iota((cap, 2 * tokens), 0).astype(F32) + 1.0
    for e in range(experts):
        pick[e * cap : (e + 1) * cap, :] = (
            (wide[e : e + 1] == slots) & (routed_to == float(e))
        ).astype(BF16)
    numbers = jnp.broadcast_to(ids_v[...].reshape(1, tokens).astype(F32) + 1.0, (8, tokens)).astype(BF16)
    named = lax.dot_general(numbers, pick_in, (((1,), (1,)), ((), ())), preferred_element_type=F32)
    block = jnp.zeros((LABEL_ROWS, 128), F32)
    row = iota((LABEL_ROWS, 128), 0)
    half = cap // 2
    for at in range(2 * experts):
        mine = named[0:1, at * half : (at + 1) * half]
        mine = jnp.concatenate([mine, jnp.zeros((1, 128 - half), F32)], axis=1)
        block = jnp.where(row == at, mine, block)
    label[...] = block.astype(BF16)

    acts_in.wait()
    chosen = dot(pick_in, acts_v[...]).astype(BF16)
    for e in range(experts):
        bases[e].wait()
        acc[e] = dot(chosen[e * cap : (e + 1) * cap], basis_v[e])
    grads_in.wait()


def split_in_kernel(acc, keep, send):
    experts, cap, width = acc.shape
    core = lax.rem(lax.axis_index("tensor"), 2)
    half = cap // 2
    at = 0
    for q in range(width // 128):
        for e in range(experts):
            for ref, which in ((keep, core), (send, 1 - core)):
                ref[at : at + half, :] = acc[
                    e, pl.ds(pl.multiple_of(which * half, 8), half), q * 128 : (q + 1) * 128
                ]
            at += half


def choose(pick, rows):
    return dot(pick[...], rows.reshape(2 * rows.shape[0], rows.shape[2])).astype(BF16)


def choose_kernel(grads, pick, out):
    out[...] = choose(pick, grads[...])


def rotate_out_kernel(grads, pick, basis_out, early, acc, grads_v, sems):
    hidden = grads.shape[2]
    experts, cap, _ = acc.shape
    fetch = fetcher(sems)
    done = early.shape[1]
    cuts = sorted({done, done + CHUNK // 2, *range(done + CHUNK, hidden, CHUNK), hidden})
    parts = [(at, pl.ds(at, end - at)) for at, end in zip(cuts, cuts[1:])]
    copies = [
        fetch(grads.at[:, :, part], grads_v.at[:, :, pl.ds(at - done, part.size)])
        for at, part in parts
    ]
    for e in range(experts):
        acc[e] = dot(early[e * cap : (e + 1) * cap, :], basis_out[e, :done, :])
    for (at, part), copy in zip(parts, copies):
        copy.wait()
        chosen = choose(pick, grads_v[:, :, pl.ds(at - done, part.size)])
        for e in range(experts):
            acc[e] += dot(chosen[e * cap : (e + 1) * cap], basis_out[e, part, :])


def split_out_kernel(acc, *refs):
    experts, cap, width = acc.shape
    core = lax.rem(lax.axis_index("tensor"), 2)
    for e in range(experts):
        for ref, which in ((refs[e], core), (refs[experts + e], 1 - core)):
            for x in range(width // 256):
                ref[x * cap : (x + 1) * cap, :] = acc[
                    e, :, pl.ds(pl.multiple_of((2 * x + which) * 128, 128), 128)
                ]


def pair_in_kernel(kept, got, keep, send):
    total = kept[...] + got[...]
    outer = total.shape[0]
    keep[...] = total
    send[:outer, :] = total.astype(BF16)
    send[outer:, :] = jnp.zeros((send.shape[0] - outer, 128), BF16)


def round_in_kernel(kept, got, label, *pays):
    slab = kept.shape[0] // len(pays)
    d = lax.axis_index("dp")
    for k, pay in enumerate(pays):
        rows = pl.ds(pl.multiple_of((d ^ k) * slab, 16), slab)
        pay[:slab, :] = (kept[rows, :] + got[rows, :].astype(F32)).astype(BF16)
        pay[slab:, :] = label[...]


def pair_out_kernel(*refs):
    *given, keep, send = refs
    experts = len(given) // 2
    cap = keep.shape[0] // experts
    x = lax.div(lax.axis_index("tensor"), 2)
    mine = pl.ds(pl.multiple_of(x * cap, 16), cap)
    other = pl.ds(pl.multiple_of((1 - x) * cap, 16), cap)
    for e in range(experts):
        kept, got = given[e], given[experts + e]
        at = pl.ds(e * cap, cap)
        keep[at, :] = kept[mine, :] + got[mine, :]
        send[at, :] = (kept[other, :] + got[other, :]).astype(BF16)


def round_kernel(kept, got, out):
    out[...] = (kept[...] + got[...].astype(F32)).astype(BF16)


def copy_kernel(x, out):
    out[...] = x[: out.shape[0], :]


def stack_kernel(*refs):
    *pieces, out = refs
    slab = out.shape[0] // len(pieces)
    for k, piece in enumerate(pieces):
        out[k * slab : (k + 1) * slab, :] = piece[:slab, :]


def mask(which, parts, pieces, out):
    experts, slots, _ = out.shape
    half = slots // len(pieces)
    slab = experts * half
    every = jnp.concatenate(parts, axis=0).astype(F32)
    for e in range(experts):
        rows, labels = [], []
        for k, piece in enumerate(pieces):
            rows.append(every[k * slab + e * half : k * slab + (e + 1) * half])
            label = piece[slab : slab + LABEL_ROWS, :].astype(F32)[2 * e : 2 * e + 2, :half]
            labels.append(jnp.where(which == 0, label[0:1], label[1:2]))
        rows = jnp.concatenate(rows, axis=0)
        labels = jnp.concatenate(labels, axis=1)
        labels = jnp.broadcast_to(labels, (128, labels.shape[1])).T
        for n in range(len(pieces)):
            out[e, :, n * 128 : (n + 1) * 128] = jnp.where(
                labels == float(n + 1), rows, 0.0
            ).astype(BF16)


def mask_own_kernel(counts, *refs):
    *pieces, out, divisor = refs
    slab = out.shape[0] * out.shape[1] // len(pieces)
    core = lax.rem(lax.axis_index("tensor"), 2)
    mask(core, [piece[:slab, :] for piece in pieces], pieces, out)
    for e in range(out.shape[0]):
        divisor[e] = jnp.full(divisor.shape[1:], counts[e].astype(F32), F32)


def mask_other_kernel(own, others, *refs):
    *pieces, out = refs
    core = lax.rem(lax.axis_index("tensor"), 2)
    mask(1 - core, [own[...], others[...]], pieces, out)


def blocks_kernel(divisor, masked_own, masked_other, own, *refs):
    *far, result, final, sems = refs
    outs = [own, *far]
    experts, slots, _ = masked_own.shape
    half = slots // len(outs)
    core = lax.rem(lax.axis_index("tensor"), 2)
    copies = []
    for e in range(experts):
        rows = [
            ref[pl.ds(pl.multiple_of((2 * e + which) * half, 16), half), :]
            for which in (core, 1 - core)
            for ref in outs
        ]
        rows = jnp.concatenate(rows, axis=0).T
        blocks = dot(rows[:, :slots], masked_own[e]) + dot(rows[:, slots:], masked_other[e])
        squares = blocks * blocks
        summed = squares[:, :128]
        for at in range(128, squares.shape[1], 128):
            summed = summed + squares[:, at : at + 128]
        final[e] = summed / divisor[e][:1]
        copies.append(pltpu.make_async_copy(final.at[e], result.at[e], sems.at[e]))
        copies[-1].start()
    for copy in copies:
        copy.wait()


def call(kernel, name, out_shape, specs=None, scratch=(), out_specs=None, flops=1, after=()):
    vmem = pl.BlockSpec(memory_space=pltpu.VMEM)
    given = {} if out_specs is None else {"out_specs": out_specs}

    def run(*args):
        def body(*refs):
            kernel(*refs[: len(args)], *refs[len(args) + len(after) :])

        return pl.pallas_call(
            body,
            out_shape=out_shape,
            in_specs=(specs or [vmem] * len(args)) + [vmem] * len(after),
            scratch_shapes=scratch,
            compiler_params=pltpu.CompilerParams(vmem_limit_bytes=VMEM),
            cost_estimate=pl.CostEstimate(flops=flops, bytes_accessed=1, transcendentals=0),
            name=name,
            **given,
        )(*args, *after)

    return run


def fast(acts, grads, routes, example_ids, expert_counts, basis_in, basis_out):
    tokens = acts.shape[0]
    experts, features, width = basis_in.shape
    cap = tokens // 2
    dp = lax.axis_size("dp")
    wide = experts * cap
    half = wide * width // 256
    hbm = pl.BlockSpec(memory_space=pltpu.HBM)
    vmem = pl.BlockSpec(memory_space=pltpu.VMEM)
    smem = pl.BlockSpec(memory_space=pltpu.SMEM)

    def pin(x):
        return pltpu.with_memory_space_constraint(x, pltpu.HBM)

    def rows(count, dtype):
        return jax.ShapeDtypeStruct((count, 128), dtype)

    core = [(t, t ^ 1) for t in range(4)]
    across = [(t, t ^ 2) for t in range(4)]

    def swap(x, k):
        return lax.ppermute(x, "dp", [(d, d ^ k) for d in range(dp)])

    partial = jax.ShapeDtypeStruct((experts, cap, width), F32)
    acc, label, pick, early = call(
        rotate_in_kernel,
        "rotate_in",
        (
            partial,
            rows(LABEL_ROWS, BF16),
            jax.ShapeDtypeStruct((wide, 2 * tokens), BF16),
            jax.ShapeDtypeStruct((tokens, 2, EARLY), BF16),
        ),
        [hbm] * 5,
        [
            pltpu.VMEM(acts.shape, BF16),
            pltpu.VMEM((2, tokens), jnp.int32),
            pltpu.VMEM((tokens,), jnp.int32),
            pltpu.VMEM(basis_in.shape, BF16),
            pltpu.SemaphoreType.DMA((4 + experts,)),
        ],
    )(pin(acts), pin(routes.T), pin(example_ids), pin(basis_in), pin(grads))
    keep, send = call(
        split_in_kernel, "split_in", (rows(half, F32), rows(half, F32)), flops=8 * 10**9
    )(acc)
    got = lax.ppermute(send, "tensor", core)
    early = call(choose_kernel, "choose", jax.ShapeDtypeStruct((wide, EARLY), BF16))(early, pick)
    keep_in, send_in = call(
        pair_in_kernel, "pair_in", (rows(half, F32), rows(half + 16, BF16)), after=[early]
    )(keep, got)
    got_in = lax.ppermute(send_in, "tensor", across)

    acc = call(
        rotate_out_kernel,
        "rotate_out",
        partial,
        [hbm, vmem, vmem, vmem],
        [
            pltpu.VMEM((tokens, 2, grads.shape[2] - EARLY), BF16),
            pltpu.SemaphoreType.DMA((grads.shape[2] // CHUNK + 1,)),
        ],
        after=[send_in],
    )(pin(grads), pick, basis_out, early)
    split = call(split_out_kernel, "split_out", [rows(2 * cap, F32)] * (2 * experts))(acc)
    got = [lax.ppermute(x, "tensor", core) for x in split[experts:]]
    keep, send = call(
        pair_out_kernel, "pair_out", (rows(wide, F32), rows(wide, BF16)), after=[got_in]
    )(*split[:experts], *got)
    got = lax.ppermute(send, "tensor", across)

    slab = half // dp
    pieces = call(round_in_kernel, "round_in", [rows(slab + LABEL_ROWS, BF16)] * dp)(
        keep_in, got_in, label
    )
    own = call(copy_kernel, "own_in", rows(slab, BF16))(pieces[0])
    other = [lax.ppermute(own, "tensor", core)]
    pieces = [pieces[0]] + [swap(pieces[k], k) for k in DISTANCES]
    out = call(round_kernel, "round_out", rows(wide, BF16), after=other)(keep, got)
    near, far = swap(out, 1), swap(out, 2)
    relayed = call(copy_kernel, "relay_out", rows(wide, BF16), after=[near])(far)
    outs = [near, far, swap(relayed, 1)]
    mine = call(stack_kernel, "stack_in", rows(3 * slab, BF16))(*pieces[1:])
    other.append(lax.ppermute(mine, "tensor", core))
    masked = jax.ShapeDtypeStruct((experts, dp * cap // 2, dp * 128), BF16)
    masked_own, divisor = call(
        mask_own_kernel,
        "mask_own",
        (masked, jax.ShapeDtypeStruct((experts, 8, 128), F32)),
        [smem] + [vmem] * dp,
    )(expert_counts, *pieces)
    masked_other = call(mask_other_kernel, "mask_other", masked, after=[divisor])(*other, *pieces)
    result = jax.ShapeDtypeStruct((experts, 128, 128), F32)
    return call(
        blocks_kernel,
        "blocks",
        result,
        scratch=[pltpu.VMEM(result.shape, F32), pltpu.SemaphoreType.DMA((experts,))],
        out_specs=hbm,
    )(divisor, masked_own, masked_other, out, *outs)


EX_DEV = 1


def compact(routes, expert, capacity):
    tok_count = routes.shape[0]
    second_hit = routes[:, 1] == expert
    routed = (routes[:, 0] == expert) | second_hit
    order = jnp.cumsum(routed.astype(jnp.int32)) - 1
    slots = jnp.arange(capacity, dtype=jnp.int32)
    match = routed[None, :] & (order[None, :] == slots[:, None])
    token_index = jnp.arange(tok_count, dtype=jnp.int32)
    positions = jnp.sum(jnp.where(match, token_index[None, :], 0), axis=1)
    filled = jnp.any(match, axis=1)
    return (positions, filled, second_hit[positions])


def general(acts, grads, routes, example_ids, expert_counts, basis_in, basis_out):
    capacity = acts.shape[0] // 2
    experts = basis_in.shape[0]
    parts_in, parts_out, label_rows = ([], [], [])
    for expert in range(experts):
        positions, filled, second = compact(routes, expert, capacity)
        chosen = grads[positions]
        grad_rows = jnp.where(second[:, None], chosen[:, 1, :], chosen[:, 0, :])
        parts_in.append(
            jnp.dot(acts[positions], basis_in[expert], preferred_element_type=jnp.float32)
        )
        parts_out.append(jnp.dot(grad_rows, basis_out[expert], preferred_element_type=jnp.float32))
        label_rows.append(jnp.where(filled, example_ids[positions], -1))
    part_in = jnp.stack(parts_in)
    part_out = jnp.stack(parts_out)
    labels = jnp.stack(label_rows)
    slice_width = basis_out.shape[2] // lax.axis_size("tensor")
    summed_in, summed_out = lax.psum((part_in, part_out), "tensor")
    rot_in = summed_in.astype(jnp.bfloat16)
    rot_out = lax.dynamic_slice_in_dim(
        summed_out.astype(jnp.bfloat16), lax.axis_index("tensor") * slice_width, slice_width, 2
    )
    owned_count = EX_DEV
    wanted = jnp.arange(lax.axis_size("dp") * owned_count, dtype=jnp.int32)
    onehot = (labels[:, :, None] == wanted[None, None, :]).astype(jnp.bfloat16)
    spread = onehot[:, :, :, None] * rot_out[:, :, None, :]
    owned_sums = lax.psum_scatter(
        jnp.einsum("ecnw,eca->newa", spread, rot_in, preferred_element_type=jnp.float32),
        "dp",
        scatter_dimension=0,
        tiled=True,
    )
    squared = jnp.sum(owned_sums * owned_sums, axis=0)
    totals = lax.psum_scatter(squared, "dp", scatter_dimension=2, tiled=True)
    return totals / expert_counts.astype(jnp.float32)[:, None, None]


def shards(*args):
    experts, _, width = args[5].shape
    sizes = (lax.axis_size("dp"), lax.axis_size("tensor"), experts, width)
    fits = sizes == (4, 4, 2, 512) and args[0].shape[0] == 384
    return (fast if fits else general)(*args)


def solution(mesh):
    placed = (
        P(("group", "dp"), "tensor"),
        P(("group", "dp"), None, "tensor"),
        P(("group", "dp"), None),
        P(("group", "dp")),
        P("group"),
        P(None, "tensor", None),
        P(None, "tensor", None),
    )
    return jax.shard_map(
        shards, mesh=mesh, in_specs=placed, out_specs=P("group", "tensor", "dp"), check_vma=False
    )
```

```python
import functools

import jax
import jax.numpy as jnp
from jax import lax
from jax.experimental import pallas as pl
from jax.experimental.pallas import tpu as pltpu
from jax.sharding import PartitionSpec as P

F32 = jnp.float32
BF16 = jnp.bfloat16
CHUNK = 1024
VMEM = 20 * 2**20
EARLY = 1536
DISTANCES = (1, 3, 2)
LATEST = (1, 3, 2)
LABEL_ROWS = 16


def iota(shape, dim):
    return lax.broadcasted_iota(jnp.int32, shape, dim)


def dot(a, b):
    return jnp.dot(a, b, preferred_element_type=F32)


def fetcher(sems):
    count = iter(range(sems.shape[0]))

    def fetch(src, dst):
        copy = pltpu.make_async_copy(src, dst, sems.at[next(count)])
        copy.start()
        return copy

    return fetch


def rotate_in_kernel(
    acts, routes, ids, basis_in, grads,
    acc, label, pick, early,
    acts_v, routes_v, ids_v, basis_v, sems,
):
    tokens = acts.shape[0]
    experts = basis_in.shape[0]
    cap = tokens // 2
    fetch = fetcher(sems)
    first = [fetch(routes, routes_v), fetch(ids, ids_v)]
    acts_in = fetch(acts, acts_v)
    bases = [fetch(basis_in.at[e], basis_v.at[e]) for e in range(experts)]
    grads_in = fetch(grads.at[:, :, pl.ds(0, early.shape[2])], early)
    for copy in first:
        copy.wait()
    hits = [
        jnp.max((routes_v[...] == e).astype(F32), axis=0, keepdims=True) for e in range(experts)
    ]
    rows = jnp.concatenate(hits + [jnp.zeros((8 - experts, tokens), F32)], axis=0).astype(BF16)
    upto = (iota((tokens, tokens), 0) <= iota((tokens, tokens), 1)).astype(BF16)
    order = dot(rows, upto)
    slots = iota((cap, tokens), 0).astype(F32) + 1.0
    pick_in = jnp.concatenate(
        [((order[e : e + 1] == slots) & (hits[e] > 0.5)).astype(BF16) for e in range(experts)],
        axis=0,
    )
    repeat = (iota((tokens, 2 * tokens), 0) == iota((tokens, 2 * tokens), 1) // 2).astype(BF16)
    wide = dot(
        jnp.concatenate(
            [order[:experts], routes_v[...].astype(F32), jnp.zeros((6 - experts, tokens), F32)],
            axis=0,
        ).astype(BF16),
        repeat,
    )
    odd = iota((1, 2 * tokens), 1) % 2 == 1
    routed_to = jnp.where(odd, wide[experts + 1 : experts + 2], wide[experts : experts + 1])
    slots = iota((cap, 2 * tokens), 0).astype(F32) + 1.0
    for e in range(experts):
        pick[e * cap : (e + 1) * cap, :] = (
            (wide[e : e + 1] == slots) & (routed_to == float(e))
        ).astype(BF16)
    numbers = jnp.broadcast_to(ids_v[...].reshape(1, tokens).astype(F32) + 1.0, (8, tokens)).astype(BF16)
    named = lax.dot_general(numbers, pick_in, (((1,), (1,)), ((), ())), preferred_element_type=F32)
    block = jnp.zeros((LABEL_ROWS, 128), F32)
    row = iota((LABEL_ROWS, 128), 0)
    half = cap // 2
    for at in range(2 * experts):
        mine = named[0:1, at * half : (at + 1) * half]
        mine = jnp.concatenate([mine, jnp.zeros((1, 128 - half), F32)], axis=1)
        block = jnp.where(row == at, mine, block)
    label[...] = block.astype(BF16)

    acts_in.wait()
    chosen = dot(pick_in, acts_v[...]).astype(BF16)
    for e in range(experts):
        bases[e].wait()
        acc[e] = dot(chosen[e * cap : (e + 1) * cap], basis_v[e])
    grads_in.wait()


def split_in_kernel(acc, keep, send):
    experts, cap, width = acc.shape
    core = lax.rem(lax.axis_index("tensor"), 2)
    half = cap // 2
    at = 0
    for q in range(width // 128):
        for e in range(experts):
            for ref, which in ((keep, core), (send, 1 - core)):
                ref[at : at + half, :] = acc[
                    e, pl.ds(pl.multiple_of(which * half, 8), half), q * 128 : (q + 1) * 128
                ]
            at += half


def choose(pick, rows):
    return dot(pick[...], rows.reshape(2 * rows.shape[0], rows.shape[2])).astype(BF16)


def choose_kernel(grads, pick, out):
    out[...] = choose(pick, grads[...])


def rotate_out_kernel(grads, pick, basis_out, early, acc, grads_v, sems):
    hidden = grads.shape[2]
    experts, cap, _ = acc.shape
    fetch = fetcher(sems)
    done = early.shape[1]
    cuts = sorted({done, done + CHUNK // 2, *range(done + CHUNK, hidden, CHUNK), hidden})
    parts = [(at, pl.ds(at, end - at)) for at, end in zip(cuts, cuts[1:])]
    copies = [
        fetch(grads.at[:, :, part], grads_v.at[:, :, pl.ds(at - done, part.size)])
        for at, part in parts
    ]
    for e in range(experts):
        acc[e] = dot(early[e * cap : (e + 1) * cap, :], basis_out[e, :done, :])
    for (at, part), copy in zip(parts, copies):
        copy.wait()
        chosen = choose(pick, grads_v[:, :, pl.ds(at - done, part.size)])
        for e in range(experts):
            acc[e] += dot(chosen[e * cap : (e + 1) * cap], basis_out[e, part, :])


def split_out_kernel(acc, *refs):
    experts, cap, width = acc.shape
    core = lax.rem(lax.axis_index("tensor"), 2)
    for e in range(experts):
        for ref, which in ((refs[e], core), (refs[experts + e], 1 - core)):
            for x in range(width // 256):
                ref[x * cap : (x + 1) * cap, :] = acc[
                    e, :, pl.ds(pl.multiple_of((2 * x + which) * 128, 128), 128)
                ]


def pair_in_kernel(kept, got, keep, send):
    total = kept[...] + got[...]
    outer = total.shape[0]
    keep[...] = total
    send[:outer, :] = total.astype(BF16)
    send[outer:, :] = jnp.zeros((send.shape[0] - outer, 128), BF16)


def round_in_kernel(kept, got, label, *pays):
    slab = kept.shape[0] // len(pays)
    d = lax.axis_index("dp")
    for k, pay in enumerate(pays):
        rows = pl.ds(pl.multiple_of((d ^ k) * slab, 16), slab)
        pay[:slab, :] = (kept[rows, :] + got[rows, :].astype(F32)).astype(BF16)
        pay[slab:, :] = label[...]


def pair_out_kernel(*refs):
    *given, keep, send = refs
    experts = len(given) // 2
    cap = keep.shape[0] // experts
    x = lax.div(lax.axis_index("tensor"), 2)
    mine = pl.ds(pl.multiple_of(x * cap, 16), cap)
    other = pl.ds(pl.multiple_of((1 - x) * cap, 16), cap)
    for e in range(experts):
        kept, got = given[e], given[experts + e]
        at = pl.ds(e * cap, cap)
        keep[at, :] = kept[mine, :] + got[mine, :]
        send[at, :] = (kept[other, :] + got[other, :]).astype(BF16)


def round_kernel(kept, got, out):
    out[...] = (kept[...] + got[...].astype(F32)).astype(BF16)


def copy_kernel(x, out):
    out[...] = x[: out.shape[0], :]


def stack_kernel(*refs):
    *pieces, first, second = refs
    rows = first.shape[0]
    slab = 2 * rows // len(pieces)
    for k, piece in enumerate(pieces):
        for at in range(0, slab, slab // 2):
            to = k * slab + at
            out = (first, second)[to // rows]
            out[to % rows : to % rows + slab // 2, :] = piece[at : at + slab // 2, :]


def mask(which, parts, pieces, out):
    experts, slots, _ = out.shape
    half = slots // len(pieces)
    slab = experts * half
    every = jnp.concatenate(parts, axis=0).astype(F32)
    for e in range(experts):
        rows, labels = [], []
        for k, piece in enumerate(pieces):
            rows.append(every[k * slab + e * half : k * slab + (e + 1) * half])
            label = piece[slab : slab + LABEL_ROWS, :].astype(F32)[2 * e : 2 * e + 2, :half]
            labels.append(jnp.where(which == 0, label[0:1], label[1:2]))
        rows = jnp.concatenate(rows, axis=0)
        labels = jnp.concatenate(labels, axis=1)
        labels = jnp.broadcast_to(labels, (128, labels.shape[1])).T
        for n in range(len(pieces)):
            out[e, :, n * 128 : (n + 1) * 128] = jnp.where(
                labels == float(n + 1), rows, 0.0
            ).astype(BF16)


def mask_own_kernel(counts, *refs):
    *pieces, out, divisor = refs
    slab = out.shape[0] * out.shape[1] // len(pieces)
    core = lax.rem(lax.axis_index("tensor"), 2)
    mask(core, [piece[:slab, :] for piece in pieces], pieces, out)
    for e in range(out.shape[0]):
        divisor[e] = jnp.full(divisor.shape[1:], counts[e].astype(F32), F32)


def mask_other_kernel(first, second, third, *refs):
    *pieces, out = refs
    core = lax.rem(lax.axis_index("tensor"), 2)
    mask(1 - core, [first[...], second[...], third[...]], pieces, out)


def blocks_kernel(divisor, masked_own, masked_other, own, *refs):
    *far, result, final, sems = refs
    outs = [own] + [far[LATEST.index(k)] for k in DISTANCES]
    experts, slots, _ = masked_own.shape
    half = slots // len(outs)
    core = lax.rem(lax.axis_index("tensor"), 2)
    copies = []
    for e in range(experts):
        rows = [
            ref[pl.ds(pl.multiple_of((2 * e + which) * half, 16), half), :]
            for which in (core, 1 - core)
            for ref in outs
        ]
        rows = jnp.concatenate(rows, axis=0).T
        blocks = dot(rows[:, :slots], masked_own[e]) + dot(rows[:, slots:], masked_other[e])
        squares = blocks * blocks
        summed = squares[:, :128]
        for at in range(128, squares.shape[1], 128):
            summed = summed + squares[:, at : at + 128]
        final[e] = summed / divisor[e][:1]
        copies.append(pltpu.make_async_copy(final.at[e], result.at[e], sems.at[e]))
        copies[-1].start()
    for copy in copies:
        copy.wait()


def call(kernel, name, out_shape, specs=None, scratch=(), out_specs=None, flops=1, after=()):
    vmem = pl.BlockSpec(memory_space=pltpu.VMEM)
    given = {} if out_specs is None else {"out_specs": out_specs}

    def run(*args):
        def body(*refs):
            kernel(*refs[: len(args)], *refs[len(args) + len(after) :])

        return pl.pallas_call(
            body,
            out_shape=out_shape,
            in_specs=(specs or [vmem] * len(args)) + [vmem] * len(after),
            scratch_shapes=scratch,
            compiler_params=pltpu.CompilerParams(vmem_limit_bytes=VMEM),
            cost_estimate=pl.CostEstimate(flops=flops, bytes_accessed=1, transcendentals=0),
            name=name,
            **given,
        )(*args, *after)

    return run


def fast(acts, grads, routes, example_ids, expert_counts, basis_in, basis_out):
    tokens = acts.shape[0]
    experts, features, width = basis_in.shape
    cap = tokens // 2
    dp = lax.axis_size("dp")
    wide = experts * cap
    half = wide * width // 256
    hbm = pl.BlockSpec(memory_space=pltpu.HBM)
    vmem = pl.BlockSpec(memory_space=pltpu.VMEM)
    smem = pl.BlockSpec(memory_space=pltpu.SMEM)

    def pin(x):
        return pltpu.with_memory_space_constraint(x, pltpu.HBM)

    def rows(count, dtype):
        return jax.ShapeDtypeStruct((count, 128), dtype)

    core = [(t, t ^ 1) for t in range(4)]
    across = [(t, t ^ 2) for t in range(4)]

    def swap(x, k):
        return lax.ppermute(x, "dp", [(d, d ^ k) for d in range(dp)])

    partial = jax.ShapeDtypeStruct((experts, cap, width), F32)
    acc, label, pick, early = call(
        rotate_in_kernel,
        "rotate_in",
        (
            partial,
            rows(LABEL_ROWS, BF16),
            jax.ShapeDtypeStruct((wide, 2 * tokens), BF16),
            jax.ShapeDtypeStruct((tokens, 2, EARLY), BF16),
        ),
        [hbm] * 5,
        [
            pltpu.VMEM(acts.shape, BF16),
            pltpu.VMEM((2, tokens), jnp.int32),
            pltpu.VMEM((tokens,), jnp.int32),
            pltpu.VMEM(basis_in.shape, BF16),
            pltpu.SemaphoreType.DMA((4 + experts,)),
        ],
    )(pin(acts), pin(routes.T), pin(example_ids), pin(basis_in), pin(grads))
    keep, send = call(
        split_in_kernel, "split_in", (rows(half, F32), rows(half, F32)), flops=8 * 10**9
    )(acc)
    got = lax.ppermute(send, "tensor", core)
    early = call(choose_kernel, "choose", jax.ShapeDtypeStruct((wide, EARLY), BF16))(early, pick)
    keep_in, send_in = call(
        pair_in_kernel, "pair_in", (rows(half, F32), rows(half + 16, BF16)), after=[early]
    )(keep, got)
    got_in = lax.ppermute(send_in, "tensor", across)

    acc = call(
        rotate_out_kernel,
        "rotate_out",
        partial,
        [hbm, vmem, vmem, vmem],
        [
            pltpu.VMEM((tokens, 2, grads.shape[2] - EARLY), BF16),
            pltpu.SemaphoreType.DMA((grads.shape[2] // CHUNK + 1,)),
        ],
        after=[send_in],
    )(pin(grads), pick, basis_out, early)
    split = call(split_out_kernel, "split_out", [rows(2 * cap, F32)] * (2 * experts))(acc)
    got = [lax.ppermute(x, "tensor", core) for x in split[experts:]]
    keep, send = call(
        pair_out_kernel, "pair_out", (rows(wide, F32), rows(wide, BF16)), after=[got_in]
    )(*split[:experts], *got)
    got = lax.ppermute(send, "tensor", across)

    slab = half // dp
    pieces = call(round_in_kernel, "round_in", [rows(slab + LABEL_ROWS, BF16)] * dp)(
        keep_in, got_in, label
    )
    own = call(copy_kernel, "own_in", rows(slab, BF16))(pieces[0])
    other = [lax.ppermute(own, "tensor", core)]
    pieces = [pieces[0]] + [swap(pieces[k], k) for k in DISTANCES]
    out = call(round_kernel, "round_out", rows(wide, BF16), after=other)(keep, got)
    outs = [swap(out, k) for k in LATEST]
    mine = call(stack_kernel, "stack_in", [rows(3 * slab // 2, BF16)] * 2)(*pieces[1:])
    other += [lax.ppermute(x, "tensor", core) for x in mine]
    masked = jax.ShapeDtypeStruct((experts, dp * cap // 2, dp * 128), BF16)
    masked_own, divisor = call(
        mask_own_kernel,
        "mask_own",
        (masked, jax.ShapeDtypeStruct((experts, 8, 128), F32)),
        [smem] + [vmem] * dp,
    )(expert_counts, *pieces)
    masked_other = call(mask_other_kernel, "mask_other", masked, after=[divisor])(*other, *pieces)
    result = jax.ShapeDtypeStruct((experts, 128, 128), F32)
    return call(
        blocks_kernel,
        "blocks",
        result,
        scratch=[pltpu.VMEM(result.shape, F32), pltpu.SemaphoreType.DMA((experts,))],
        out_specs=hbm,
    )(divisor, masked_own, masked_other, out, *outs)


EX_DEV = 1


def compact(routes, expert, capacity):
    tok_count = routes.shape[0]
    second_hit = routes[:, 1] == expert
    routed = (routes[:, 0] == expert) | second_hit
    order = jnp.cumsum(routed.astype(jnp.int32)) - 1
    slots = jnp.arange(capacity, dtype=jnp.int32)
    match = routed[None, :] & (order[None, :] == slots[:, None])
    token_index = jnp.arange(tok_count, dtype=jnp.int32)
    positions = jnp.sum(jnp.where(match, token_index[None, :], 0), axis=1)
    filled = jnp.any(match, axis=1)
    return (positions, filled, second_hit[positions])


def general(acts, grads, routes, example_ids, expert_counts, basis_in, basis_out):
    capacity = acts.shape[0] // 2
    experts = basis_in.shape[0]
    parts_in, parts_out, label_rows = ([], [], [])
    for expert in range(experts):
        positions, filled, second = compact(routes, expert, capacity)
        chosen = grads[positions]
        grad_rows = jnp.where(second[:, None], chosen[:, 1, :], chosen[:, 0, :])
        parts_in.append(
            jnp.dot(acts[positions], basis_in[expert], preferred_element_type=jnp.float32)
        )
        parts_out.append(jnp.dot(grad_rows, basis_out[expert], preferred_element_type=jnp.float32))
        label_rows.append(jnp.where(filled, example_ids[positions], -1))
    part_in = jnp.stack(parts_in)
    part_out = jnp.stack(parts_out)
    labels = jnp.stack(label_rows)
    slice_width = basis_out.shape[2] // lax.axis_size("tensor")
    summed_in, summed_out = lax.psum((part_in, part_out), "tensor")
    rot_in = summed_in.astype(jnp.bfloat16)
    rot_out = lax.dynamic_slice_in_dim(
        summed_out.astype(jnp.bfloat16), lax.axis_index("tensor") * slice_width, slice_width, 2
    )
    owned_count = EX_DEV
    wanted = jnp.arange(lax.axis_size("dp") * owned_count, dtype=jnp.int32)
    onehot = (labels[:, :, None] == wanted[None, None, :]).astype(jnp.bfloat16)
    spread = onehot[:, :, :, None] * rot_out[:, :, None, :]
    owned_sums = lax.psum_scatter(
        jnp.einsum("ecnw,eca->newa", spread, rot_in, preferred_element_type=jnp.float32),
        "dp",
        scatter_dimension=0,
        tiled=True,
    )
    squared = jnp.sum(owned_sums * owned_sums, axis=0)
    totals = lax.psum_scatter(squared, "dp", scatter_dimension=2, tiled=True)
    return totals / expert_counts.astype(jnp.float32)[:, None, None]


def shards(*args):
    experts, _, width = args[5].shape
    sizes = (lax.axis_size("dp"), lax.axis_size("tensor"), experts, width)
    fits = sizes == (4, 4, 2, 512) and args[0].shape[0] == 384
    return (fast if fits else general)(*args)


def solution(mesh):
    placed = (
        P(("group", "dp"), "tensor"),
        P(("group", "dp"), None, "tensor"),
        P(("group", "dp"), None),
        P(("group", "dp")),
        P("group"),
        P(None, "tensor", None),
        P(None, "tensor", None),
    )
    return jax.shard_map(
        shards, mesh=mesh, in_specs=placed, out_specs=P("group", "tensor", "dp"), check_vma=False
    )
```

```python
import functools

import jax
import jax.numpy as jnp
from jax import lax
from jax.experimental import pallas as pl
from jax.experimental.pallas import tpu as pltpu
from jax.sharding import PartitionSpec as P

F32 = jnp.float32
BF16 = jnp.bfloat16
CHUNK = 1024
VMEM = 20 * 2**20
EARLY = 2048
DISTANCES = (3, 2, 1)
LATEST = (1, 3, 2)
LABEL_ROWS = 16


def iota(shape, dim):
    return lax.broadcasted_iota(jnp.int32, shape, dim)


def dot(a, b):
    return jnp.dot(a, b, preferred_element_type=F32)


def fetcher(sems):
    count = iter(range(sems.shape[0]))

    def fetch(src, dst):
        copy = pltpu.make_async_copy(src, dst, sems.at[next(count)])
        copy.start()
        return copy

    return fetch


def rotate_in_kernel(
    acts, routes, ids, basis_in, grads,
    acc, label, pick, early,
    acts_v, routes_v, ids_v, basis_v, sems,
):
    tokens = acts.shape[0]
    experts = basis_in.shape[0]
    cap = tokens // 2
    fetch = fetcher(sems)
    first = [fetch(routes, routes_v), fetch(ids, ids_v)]
    acts_in = fetch(acts, acts_v)
    bases = [fetch(basis_in.at[e], basis_v.at[e]) for e in range(experts)]
    grads_in = fetch(grads.at[:, :, pl.ds(0, early.shape[2])], early)
    for copy in first:
        copy.wait()
    hits = [
        jnp.max((routes_v[...] == e).astype(F32), axis=0, keepdims=True) for e in range(experts)
    ]
    rows = jnp.concatenate(hits + [jnp.zeros((8 - experts, tokens), F32)], axis=0).astype(BF16)
    upto = (iota((tokens, tokens), 0) <= iota((tokens, tokens), 1)).astype(BF16)
    order = dot(rows, upto)
    slots = iota((cap, tokens), 0).astype(F32) + 1.0
    pick_in = jnp.concatenate(
        [((order[e : e + 1] == slots) & (hits[e] > 0.5)).astype(BF16) for e in range(experts)],
        axis=0,
    )
    repeat = (iota((tokens, 2 * tokens), 0) == iota((tokens, 2 * tokens), 1) // 2).astype(BF16)
    wide = dot(
        jnp.concatenate(
            [order[:experts], routes_v[...].astype(F32), jnp.zeros((6 - experts, tokens), F32)],
            axis=0,
        ).astype(BF16),
        repeat,
    )
    odd = iota((1, 2 * tokens), 1) % 2 == 1
    routed_to = jnp.where(odd, wide[experts + 1 : experts + 2], wide[experts : experts + 1])
    slots = iota((cap, 2 * tokens), 0).astype(F32) + 1.0
    for e in range(experts):
        pick[e * cap : (e + 1) * cap, :] = (
            (wide[e : e + 1] == slots) & (routed_to == float(e))
        ).astype(BF16)
    numbers = jnp.broadcast_to(ids_v[...].reshape(1, tokens).astype(F32) + 1.0, (8, tokens)).astype(BF16)
    named = lax.dot_general(numbers, pick_in, (((1,), (1,)), ((), ())), preferred_element_type=F32)
    block = jnp.zeros((LABEL_ROWS, 128), F32)
    row = iota((LABEL_ROWS, 128), 0)
    half = cap // 2
    for at in range(2 * experts):
        mine = named[0:1, at * half : (at + 1) * half]
        mine = jnp.concatenate([mine, jnp.zeros((1, 128 - half), F32)], axis=1)
        block = jnp.where(row == at, mine, block)
    label[...] = block.astype(BF16)

    acts_in.wait()
    chosen = dot(pick_in, acts_v[...]).astype(BF16)
    for e in range(experts):
        bases[e].wait()
        acc[e] = dot(chosen[e * cap : (e + 1) * cap], basis_v[e])
    grads_in.wait()


def split_in_kernel(acc, keep, send):
    experts, cap, width = acc.shape
    core = lax.rem(lax.axis_index("tensor"), 2)
    half = cap // 2
    at = 0
    for q in range(width // 128):
        for e in range(experts):
            for ref, which in ((keep, core), (send, 1 - core)):
                ref[at : at + half, :] = acc[
                    e, pl.ds(pl.multiple_of(which * half, 8), half), q * 128 : (q + 1) * 128
                ]
            at += half


def choose(pick, rows):
    return dot(pick[...], rows.reshape(2 * rows.shape[0], rows.shape[2])).astype(BF16)


def choose_kernel(grads, pick, out):
    out[...] = choose(pick, grads[...])


def rotate_out_kernel(grads, pick, basis_out, early, acc, grads_v, sems):
    hidden = grads.shape[2]
    experts, cap, _ = acc.shape
    fetch = fetcher(sems)
    done = early.shape[1]
    cuts = sorted({done, done + CHUNK // 2, *range(done + CHUNK, hidden, CHUNK), hidden})
    parts = [(at, pl.ds(at, end - at)) for at, end in zip(cuts, cuts[1:])]
    copies = [
        fetch(grads.at[:, :, part], grads_v.at[:, :, pl.ds(at - done, part.size)])
        for at, part in parts
    ]
    for e in range(experts):
        acc[e] = dot(early[e * cap : (e + 1) * cap, :], basis_out[e, :done, :])
    for (at, part), copy in zip(parts, copies):
        copy.wait()
        chosen = choose(pick, grads_v[:, :, pl.ds(at - done, part.size)])
        for e in range(experts):
            acc[e] += dot(chosen[e * cap : (e + 1) * cap], basis_out[e, part, :])


def split_out_kernel(acc, *refs):
    experts, cap, width = acc.shape
    core = lax.rem(lax.axis_index("tensor"), 2)
    for e in range(experts):
        for ref, which in ((refs[e], core), (refs[experts + e], 1 - core)):
            for x in range(width // 256):
                ref[x * cap : (x + 1) * cap, :] = acc[
                    e, :, pl.ds(pl.multiple_of((2 * x + which) * 128, 128), 128)
                ]


def pair_in_kernel(kept, got, keep, send):
    total = kept[...] + got[...]
    outer = total.shape[0]
    keep[...] = total
    send[:outer, :] = total.astype(BF16)
    send[outer:, :] = jnp.zeros((send.shape[0] - outer, 128), BF16)


def round_in_kernel(kept, got, label, *pays):
    slab = kept.shape[0] // len(pays)
    d = lax.axis_index("dp")
    for k, pay in enumerate(pays):
        rows = pl.ds(pl.multiple_of((d ^ k) * slab, 16), slab)
        pay[:slab, :] = (kept[rows, :] + got[rows, :].astype(F32)).astype(BF16)
        pay[slab:, :] = label[...]


def pair_out_kernel(*refs):
    *given, keep, send = refs
    experts = len(given) // 2
    cap = keep.shape[0] // experts
    x = lax.div(lax.axis_index("tensor"), 2)
    mine = pl.ds(pl.multiple_of(x * cap, 16), cap)
    other = pl.ds(pl.multiple_of((1 - x) * cap, 16), cap)
    for e in range(experts):
        kept, got = given[e], given[experts + e]
        at = pl.ds(e * cap, cap)
        keep[at, :] = kept[mine, :] + got[mine, :]
        send[at, :] = (kept[other, :] + got[other, :]).astype(BF16)


def round_kernel(kept, got, out):
    out[...] = (kept[...] + got[...].astype(F32)).astype(BF16)


def copy_kernel(x, out):
    out[...] = x[: out.shape[0], :]


def stack_kernel(*refs):
    *pieces, first, second = refs
    rows = first.shape[0]
    slab = 2 * rows // len(pieces)
    for k, piece in enumerate(pieces):
        for at in range(0, slab, slab // 2):
            to = k * slab + at
            out = (first, second)[to // rows]
            out[to % rows : to % rows + slab // 2, :] = piece[at : at + slab // 2, :]


def mask(which, parts, pieces, out):
    experts, slots, _ = out.shape
    half = slots // len(pieces)
    slab = experts * half
    every = jnp.concatenate(parts, axis=0).astype(F32)
    for e in range(experts):
        rows, labels = [], []
        for k, piece in enumerate(pieces):
            rows.append(every[k * slab + e * half : k * slab + (e + 1) * half])
            label = piece[slab : slab + LABEL_ROWS, :].astype(F32)[2 * e : 2 * e + 2, :half]
            labels.append(jnp.where(which == 0, label[0:1], label[1:2]))
        rows = jnp.concatenate(rows, axis=0)
        labels = jnp.concatenate(labels, axis=1)
        labels = jnp.broadcast_to(labels, (128, labels.shape[1])).T
        for n in range(len(pieces)):
            out[e, :, n * 128 : (n + 1) * 128] = jnp.where(
                labels == float(n + 1), rows, 0.0
            ).astype(BF16)


def mask_own_kernel(counts, *refs):
    *pieces, out, divisor = refs
    slab = out.shape[0] * out.shape[1] // len(pieces)
    core = lax.rem(lax.axis_index("tensor"), 2)
    mask(core, [piece[:slab, :] for piece in pieces], pieces, out)
    for e in range(out.shape[0]):
        divisor[e] = jnp.full(divisor.shape[1:], counts[e].astype(F32), F32)


def mask_other_kernel(first, second, third, *refs):
    *pieces, out = refs
    core = lax.rem(lax.axis_index("tensor"), 2)
    mask(1 - core, [first[...], second[...], third[...]], pieces, out)


def blocks_kernel(divisor, masked_own, masked_other, own, *refs):
    *far, result, final, sems = refs
    outs = [own] + [far[LATEST.index(k)] for k in DISTANCES]
    experts, slots, _ = masked_own.shape
    half = slots // len(outs)
    core = lax.rem(lax.axis_index("tensor"), 2)
    copies = []
    for e in range(experts):
        rows = [
            ref[pl.ds(pl.multiple_of((2 * e + which) * half, 16), half), :]
            for which in (core, 1 - core)
            for ref in outs
        ]
        rows = jnp.concatenate(rows, axis=0).T
        blocks = dot(rows[:, :slots], masked_own[e]) + dot(rows[:, slots:], masked_other[e])
        squares = blocks * blocks
        summed = squares[:, :128]
        for at in range(128, squares.shape[1], 128):
            summed = summed + squares[:, at : at + 128]
        final[e] = summed / divisor[e][:1]
        copies.append(pltpu.make_async_copy(final.at[e], result.at[e], sems.at[e]))
        copies[-1].start()
    for copy in copies:
        copy.wait()


def call(kernel, name, out_shape, specs=None, scratch=(), out_specs=None, flops=1, after=()):
    vmem = pl.BlockSpec(memory_space=pltpu.VMEM)
    given = {} if out_specs is None else {"out_specs": out_specs}

    def run(*args):
        def body(*refs):
            kernel(*refs[: len(args)], *refs[len(args) + len(after) :])

        return pl.pallas_call(
            body,
            out_shape=out_shape,
            in_specs=(specs or [vmem] * len(args)) + [vmem] * len(after),
            scratch_shapes=scratch,
            compiler_params=pltpu.CompilerParams(vmem_limit_bytes=VMEM),
            cost_estimate=pl.CostEstimate(flops=flops, bytes_accessed=1, transcendentals=0),
            name=name,
            **given,
        )(*args, *after)

    return run


def fast(acts, grads, routes, example_ids, expert_counts, basis_in, basis_out):
    tokens = acts.shape[0]
    experts, features, width = basis_in.shape
    cap = tokens // 2
    dp = lax.axis_size("dp")
    wide = experts * cap
    half = wide * width // 256
    hbm = pl.BlockSpec(memory_space=pltpu.HBM)
    vmem = pl.BlockSpec(memory_space=pltpu.VMEM)
    smem = pl.BlockSpec(memory_space=pltpu.SMEM)

    def pin(x):
        return pltpu.with_memory_space_constraint(x, pltpu.HBM)

    def rows(count, dtype):
        return jax.ShapeDtypeStruct((count, 128), dtype)

    core = [(t, t ^ 1) for t in range(4)]
    across = [(t, t ^ 2) for t in range(4)]

    def swap(x, k):
        return lax.ppermute(x, "dp", [(d, d ^ k) for d in range(dp)])

    partial = jax.ShapeDtypeStruct((experts, cap, width), F32)
    acc, label, pick, early = call(
        rotate_in_kernel,
        "rotate_in",
        (
            partial,
            rows(LABEL_ROWS, BF16),
            jax.ShapeDtypeStruct((wide, 2 * tokens), BF16),
            jax.ShapeDtypeStruct((tokens, 2, EARLY), BF16),
        ),
        [hbm] * 5,
        [
            pltpu.VMEM(acts.shape, BF16),
            pltpu.VMEM((2, tokens), jnp.int32),
            pltpu.VMEM((tokens,), jnp.int32),
            pltpu.VMEM(basis_in.shape, BF16),
            pltpu.SemaphoreType.DMA((4 + experts,)),
        ],
    )(pin(acts), pin(routes.T), pin(example_ids), pin(basis_in), pin(grads))
    keep, send = call(
        split_in_kernel, "split_in", (rows(half, F32), rows(half, F32)), flops=8 * 10**9
    )(acc)
    got = lax.ppermute(send, "tensor", core)
    early = call(choose_kernel, "choose", jax.ShapeDtypeStruct((wide, EARLY), BF16))(early, pick)
    keep_in, send_in = call(
        pair_in_kernel, "pair_in", (rows(half, F32), rows(half + 16, BF16)), after=[early]
    )(keep, got)
    got_in = lax.ppermute(send_in, "tensor", across)

    acc = call(
        rotate_out_kernel,
        "rotate_out",
        partial,
        [hbm, vmem, vmem, vmem],
        [
            pltpu.VMEM((tokens, 2, grads.shape[2] - EARLY), BF16),
            pltpu.SemaphoreType.DMA((grads.shape[2] // CHUNK + 1,)),
        ],
        after=[send_in],
    )(pin(grads), pick, basis_out, early)
    split = call(split_out_kernel, "split_out", [rows(2 * cap, F32)] * (2 * experts))(acc)
    got = [lax.ppermute(x, "tensor", core) for x in split[experts:]]
    keep, send = call(
        pair_out_kernel, "pair_out", (rows(wide, F32), rows(wide, BF16)), after=[got_in]
    )(*split[:experts], *got)
    got = lax.ppermute(send, "tensor", across)

    slab = half // dp
    pieces = call(round_in_kernel, "round_in", [rows(slab + LABEL_ROWS, BF16)] * dp)(
        keep_in, got_in, label
    )
    own = call(copy_kernel, "own_in", rows(slab, BF16))(pieces[0])
    other = [lax.ppermute(own, "tensor", core)]
    pieces = [pieces[0]] + [swap(pieces[k], k) for k in DISTANCES]
    out = call(round_kernel, "round_out", rows(wide, BF16), after=other)(keep, got)
    outs = [swap(out, k) for k in LATEST]
    mine = call(stack_kernel, "stack_in", [rows(3 * slab // 2, BF16)] * 2)(*pieces[1:])
    other += [lax.ppermute(x, "tensor", core) for x in mine]
    masked = jax.ShapeDtypeStruct((experts, dp * cap // 2, dp * 128), BF16)
    masked_own, divisor = call(
        mask_own_kernel,
        "mask_own",
        (masked, jax.ShapeDtypeStruct((experts, 8, 128), F32)),
        [smem] + [vmem] * dp,
    )(expert_counts, *pieces)
    masked_other = call(mask_other_kernel, "mask_other", masked, after=[divisor])(*other, *pieces)
    result = jax.ShapeDtypeStruct((experts, 128, 128), F32)
    return call(
        blocks_kernel,
        "blocks",
        result,
        scratch=[pltpu.VMEM(result.shape, F32), pltpu.SemaphoreType.DMA((experts,))],
        out_specs=hbm,
    )(divisor, masked_own, masked_other, out, *outs)


EX_DEV = 1


def compact(routes, expert, capacity):
    tok_count = routes.shape[0]
    second_hit = routes[:, 1] == expert
    routed = (routes[:, 0] == expert) | second_hit
    order = jnp.cumsum(routed.astype(jnp.int32)) - 1
    slots = jnp.arange(capacity, dtype=jnp.int32)
    match = routed[None, :] & (order[None, :] == slots[:, None])
    token_index = jnp.arange(tok_count, dtype=jnp.int32)
    positions = jnp.sum(jnp.where(match, token_index[None, :], 0), axis=1)
    filled = jnp.any(match, axis=1)
    return (positions, filled, second_hit[positions])


def general(acts, grads, routes, example_ids, expert_counts, basis_in, basis_out):
    capacity = acts.shape[0] // 2
    experts = basis_in.shape[0]
    parts_in, parts_out, label_rows = ([], [], [])
    for expert in range(experts):
        positions, filled, second = compact(routes, expert, capacity)
        chosen = grads[positions]
        grad_rows = jnp.where(second[:, None], chosen[:, 1, :], chosen[:, 0, :])
        parts_in.append(
            jnp.dot(acts[positions], basis_in[expert], preferred_element_type=jnp.float32)
        )
        parts_out.append(jnp.dot(grad_rows, basis_out[expert], preferred_element_type=jnp.float32))
        label_rows.append(jnp.where(filled, example_ids[positions], -1))
    part_in = jnp.stack(parts_in)
    part_out = jnp.stack(parts_out)
    labels = jnp.stack(label_rows)
    slice_width = basis_out.shape[2] // lax.axis_size("tensor")
    summed_in, summed_out = lax.psum((part_in, part_out), "tensor")
    rot_in = summed_in.astype(jnp.bfloat16)
    rot_out = lax.dynamic_slice_in_dim(
        summed_out.astype(jnp.bfloat16), lax.axis_index("tensor") * slice_width, slice_width, 2
    )
    owned_count = EX_DEV
    wanted = jnp.arange(lax.axis_size("dp") * owned_count, dtype=jnp.int32)
    onehot = (labels[:, :, None] == wanted[None, None, :]).astype(jnp.bfloat16)
    spread = onehot[:, :, :, None] * rot_out[:, :, None, :]
    owned_sums = lax.psum_scatter(
        jnp.einsum("ecnw,eca->newa", spread, rot_in, preferred_element_type=jnp.float32),
        "dp",
        scatter_dimension=0,
        tiled=True,
    )
    squared = jnp.sum(owned_sums * owned_sums, axis=0)
    totals = lax.psum_scatter(squared, "dp", scatter_dimension=2, tiled=True)
    return totals / expert_counts.astype(jnp.float32)[:, None, None]


def shards(*args):
    experts, _, width = args[5].shape
    sizes = (lax.axis_size("dp"), lax.axis_size("tensor"), experts, width)
    fits = sizes == (4, 4, 2, 512) and args[0].shape[0] == 384
    return (fast if fits else general)(*args)


def solution(mesh):
    placed = (
        P(("group", "dp"), "tensor"),
        P(("group", "dp"), None, "tensor"),
        P(("group", "dp"), None),
        P(("group", "dp")),
        P("group"),
        P(None, "tensor", None),
        P(None, "tensor", None),
    )
    return jax.shard_map(
        shards, mesh=mesh, in_specs=placed, out_specs=P("group", "tensor", "dp"), check_vma=False
    )
```

```python
import functools

import jax
import jax.numpy as jnp
from jax import lax
from jax.experimental import pallas as pl
from jax.experimental.pallas import tpu as pltpu
from jax.sharding import PartitionSpec as P

F32 = jnp.float32
BF16 = jnp.bfloat16
CHUNK = 1024
VMEM = 20 * 2**20
EARLY = 2048
DISTANCES = (3, 2, 1)
LATEST = (1, 3, 2)
LABEL_ROWS = 16


def iota(shape, dim):
    return lax.broadcasted_iota(jnp.int32, shape, dim)


def dot(a, b):
    return jnp.dot(a, b, preferred_element_type=F32)


def fetcher(sems):
    count = iter(range(sems.shape[0]))

    def fetch(src, dst):
        copy = pltpu.make_async_copy(src, dst, sems.at[next(count)])
        copy.start()
        return copy

    return fetch


def rotate_in_kernel(
    acts, routes, ids, basis_in, grads,
    acc, label, pick, early,
    acts_v, routes_v, ids_v, basis_v, sems,
):
    tokens = acts.shape[0]
    experts = basis_in.shape[0]
    cap = tokens // 2
    fetch = fetcher(sems)
    first = [fetch(routes, routes_v), fetch(ids, ids_v)]
    acts_in = fetch(acts, acts_v)
    bases = [fetch(basis_in.at[e], basis_v.at[e]) for e in range(experts)]
    grads_in = fetch(grads.at[:, :, pl.ds(0, early.shape[2])], early)
    for copy in first:
        copy.wait()
    hits = [
        jnp.max((routes_v[...] == e).astype(F32), axis=0, keepdims=True) for e in range(experts)
    ]
    rows = jnp.concatenate(hits + [jnp.zeros((8 - experts, tokens), F32)], axis=0).astype(BF16)
    upto = (iota((tokens, tokens), 0) <= iota((tokens, tokens), 1)).astype(BF16)
    order = dot(rows, upto)
    slots = iota((cap, tokens), 0).astype(F32) + 1.0
    pick_in = jnp.concatenate(
        [((order[e : e + 1] == slots) & (hits[e] > 0.5)).astype(BF16) for e in range(experts)],
        axis=0,
    )
    repeat = (iota((tokens, 2 * tokens), 0) == iota((tokens, 2 * tokens), 1) // 2).astype(BF16)
    wide = dot(
        jnp.concatenate(
            [order[:experts], routes_v[...].astype(F32), jnp.zeros((6 - experts, tokens), F32)],
            axis=0,
        ).astype(BF16),
        repeat,
    )
    odd = iota((1, 2 * tokens), 1) % 2 == 1
    routed_to = jnp.where(odd, wide[experts + 1 : experts + 2], wide[experts : experts + 1])
    slots = iota((cap, 2 * tokens), 0).astype(F32) + 1.0
    for e in range(experts):
        pick[e * cap : (e + 1) * cap, :] = (
            (wide[e : e + 1] == slots) & (routed_to == float(e))
        ).astype(BF16)
    numbers = jnp.broadcast_to(ids_v[...].reshape(1, tokens).astype(F32) + 1.0, (8, tokens)).astype(BF16)
    named = lax.dot_general(numbers, pick_in, (((1,), (1,)), ((), ())), preferred_element_type=F32)
    block = jnp.zeros((LABEL_ROWS, 128), F32)
    row = iota((LABEL_ROWS, 128), 0)
    half = cap // 2
    for at in range(2 * experts):
        mine = named[0:1, at * half : (at + 1) * half]
        mine = jnp.concatenate([mine, jnp.zeros((1, 128 - half), F32)], axis=1)
        block = jnp.where(row == at, mine, block)
    label[...] = block.astype(BF16)

    acts_in.wait()
    chosen = dot(pick_in, acts_v[...]).astype(BF16)
    for e in range(experts):
        bases[e].wait()
        acc[e] = dot(chosen[e * cap : (e + 1) * cap], basis_v[e])
    grads_in.wait()


def split_in_kernel(acc, keep, send):
    experts, cap, width = acc.shape
    core = lax.rem(lax.axis_index("tensor"), 2)
    half = cap // 2
    at = 0
    for q in range(width // 128):
        for e in range(experts):
            for ref, which in ((keep, core), (send, 1 - core)):
                ref[at : at + half, :] = acc[
                    e, pl.ds(pl.multiple_of(which * half, 8), half), q * 128 : (q + 1) * 128
                ]
            at += half


def choose(pick, rows):
    return dot(pick[...], rows.reshape(2 * rows.shape[0], rows.shape[2])).astype(BF16)


def choose_kernel(grads, pick, out):
    out[...] = choose(pick, grads[...])


def rotate_out_kernel(grads, pick, basis_out, early, *refs):
    *split, acc, grads_v, sems = refs
    hidden = grads.shape[2]
    experts, cap, _ = acc.shape
    fetch = fetcher(sems)
    done = early.shape[1]
    cuts = sorted({done, done + CHUNK // 2, *range(done + CHUNK, hidden, CHUNK), hidden})
    parts = [(at, pl.ds(at, end - at)) for at, end in zip(cuts, cuts[1:])]
    copies = [
        fetch(grads.at[:, :, part], grads_v.at[:, :, pl.ds(at - done, part.size)])
        for at, part in parts
    ]
    for e in range(experts):
        acc[e] = dot(early[e * cap : (e + 1) * cap, :], basis_out[e, :done, :])
    for (at, part), copy in zip(parts, copies):
        copy.wait()
        chosen = choose(pick, grads_v[:, :, pl.ds(at - done, part.size)])
        for e in range(experts):
            acc[e] += dot(chosen[e * cap : (e + 1) * cap], basis_out[e, part, :])
    split_out(acc, *split)


def split_out(acc, *refs):
    experts, cap, width = acc.shape
    core = lax.rem(lax.axis_index("tensor"), 2)
    for e in range(experts):
        for ref, which in ((refs[e], core), (refs[experts + e], 1 - core)):
            for x in range(width // 256):
                ref[x * cap : (x + 1) * cap, :] = acc[
                    e, :, pl.ds(pl.multiple_of((2 * x + which) * 128, 128), 128)
                ]


def pair_in_kernel(kept, got, keep, send):
    total = kept[...] + got[...]
    outer = total.shape[0]
    keep[...] = total
    send[:outer, :] = total.astype(BF16)
    send[outer:, :] = jnp.zeros((send.shape[0] - outer, 128), BF16)


def round_in_kernel(kept, got, label, *pays):
    *pays, own = pays
    slab = kept.shape[0] // len(pays)
    d = lax.axis_index("dp")
    own[...] = (
        kept[pl.ds(pl.multiple_of(d * slab, 16), slab), :]
        + got[pl.ds(pl.multiple_of(d * slab, 16), slab), :].astype(F32)
    ).astype(BF16)
    for k, pay in enumerate(pays):
        rows = pl.ds(pl.multiple_of((d ^ k) * slab, 16), slab)
        pay[:slab, :] = (kept[rows, :] + got[rows, :].astype(F32)).astype(BF16)
        pay[slab:, :] = label[...]


def pair_out_kernel(*refs):
    *given, keep, send = refs
    experts = len(given) // 2
    cap = keep.shape[0] // experts
    x = lax.div(lax.axis_index("tensor"), 2)
    mine = pl.ds(pl.multiple_of(x * cap, 16), cap)
    other = pl.ds(pl.multiple_of((1 - x) * cap, 16), cap)
    for e in range(experts):
        kept, got = given[e], given[experts + e]
        at = pl.ds(e * cap, cap)
        keep[at, :] = kept[mine, :] + got[mine, :]
        send[at, :] = (kept[other, :] + got[other, :]).astype(BF16)


def round_kernel(kept, got, out):
    out[...] = (kept[...] + got[...].astype(F32)).astype(BF16)


def stack_kernel(*refs):
    *pieces, first, second = refs
    rows = first.shape[0]
    slab = 2 * rows // len(pieces)
    for k, piece in enumerate(pieces):
        for at in range(0, slab, slab // 2):
            to = k * slab + at
            out = (first, second)[to // rows]
            out[to % rows : to % rows + slab // 2, :] = piece[at : at + slab // 2, :]


def mask(which, parts, pieces, out):
    experts, slots, _ = out.shape
    half = slots // len(pieces)
    slab = experts * half
    every = jnp.concatenate(parts, axis=0).astype(F32)
    for e in range(experts):
        rows, labels = [], []
        for k, piece in enumerate(pieces):
            rows.append(every[k * slab + e * half : k * slab + (e + 1) * half])
            label = piece[slab : slab + LABEL_ROWS, :].astype(F32)[2 * e : 2 * e + 2, :half]
            labels.append(jnp.where(which == 0, label[0:1], label[1:2]))
        rows = jnp.concatenate(rows, axis=0)
        labels = jnp.concatenate(labels, axis=1)
        labels = jnp.broadcast_to(labels, (128, labels.shape[1])).T
        for n in range(len(pieces)):
            out[e, :, n * 128 : (n + 1) * 128] = jnp.where(
                labels == float(n + 1), rows, 0.0
            ).astype(BF16)


def mask_own_kernel(counts, *refs):
    *pieces, out, divisor = refs
    slab = out.shape[0] * out.shape[1] // len(pieces)
    core = lax.rem(lax.axis_index("tensor"), 2)
    mask(core, [piece[:slab, :] for piece in pieces], pieces, out)
    for e in range(out.shape[0]):
        divisor[e] = jnp.full(divisor.shape[1:], counts[e].astype(F32), F32)


def mask_other_kernel(first, second, third, *refs):
    *pieces, out = refs
    core = lax.rem(lax.axis_index("tensor"), 2)
    mask(1 - core, [first[...], second[...], third[...]], pieces, out)


def blocks_kernel(divisor, masked_own, masked_other, own, *refs):
    *far, result, final, sems = refs
    outs = [own] + [far[LATEST.index(k)] for k in DISTANCES]
    experts, slots, _ = masked_own.shape
    half = slots // len(outs)
    core = lax.rem(lax.axis_index("tensor"), 2)
    copies = []
    for e in range(experts):
        rows = [
            ref[pl.ds(pl.multiple_of((2 * e + which) * half, 16), half), :]
            for which in (core, 1 - core)
            for ref in outs
        ]
        rows = jnp.concatenate(rows, axis=0).T
        blocks = dot(rows[:, :slots], masked_own[e]) + dot(rows[:, slots:], masked_other[e])
        squares = blocks * blocks
        summed = squares[:, :128]
        for at in range(128, squares.shape[1], 128):
            summed = summed + squares[:, at : at + 128]
        final[e] = summed / divisor[e][:1]
        copies.append(pltpu.make_async_copy(final.at[e], result.at[e], sems.at[e]))
        copies[-1].start()
    for copy in copies:
        copy.wait()


def call(kernel, name, out_shape, specs=None, scratch=(), out_specs=None, flops=1, after=()):
    vmem = pl.BlockSpec(memory_space=pltpu.VMEM)
    given = {} if out_specs is None else {"out_specs": out_specs}

    def run(*args):
        def body(*refs):
            kernel(*refs[: len(args)], *refs[len(args) + len(after) :])

        return pl.pallas_call(
            body,
            out_shape=out_shape,
            in_specs=(specs or [vmem] * len(args)) + [vmem] * len(after),
            scratch_shapes=scratch,
            compiler_params=pltpu.CompilerParams(vmem_limit_bytes=VMEM),
            cost_estimate=pl.CostEstimate(flops=flops, bytes_accessed=1, transcendentals=0),
            name=name,
            **given,
        )(*args, *after)

    return run


def fast(acts, grads, routes, example_ids, expert_counts, basis_in, basis_out):
    tokens = acts.shape[0]
    experts, features, width = basis_in.shape
    cap = tokens // 2
    dp = lax.axis_size("dp")
    wide = experts * cap
    half = wide * width // 256
    hbm = pl.BlockSpec(memory_space=pltpu.HBM)
    vmem = pl.BlockSpec(memory_space=pltpu.VMEM)
    smem = pl.BlockSpec(memory_space=pltpu.SMEM)

    def pin(x):
        return pltpu.with_memory_space_constraint(x, pltpu.HBM)

    def rows(count, dtype):
        return jax.ShapeDtypeStruct((count, 128), dtype)

    core = [(t, t ^ 1) for t in range(4)]
    across = [(t, t ^ 2) for t in range(4)]

    def swap(x, k):
        return lax.ppermute(x, "dp", [(d, d ^ k) for d in range(dp)])

    partial = jax.ShapeDtypeStruct((experts, cap, width), F32)
    acc, label, pick, early = call(
        rotate_in_kernel,
        "rotate_in",
        (
            partial,
            rows(LABEL_ROWS, BF16),
            jax.ShapeDtypeStruct((wide, 2 * tokens), BF16),
            jax.ShapeDtypeStruct((tokens, 2, EARLY), BF16),
        ),
        [hbm] * 5,
        [
            pltpu.VMEM(acts.shape, BF16),
            pltpu.VMEM((2, tokens), jnp.int32),
            pltpu.VMEM((tokens,), jnp.int32),
            pltpu.VMEM(basis_in.shape, BF16),
            pltpu.SemaphoreType.DMA((4 + experts,)),
        ],
    )(pin(acts), pin(routes.T), pin(example_ids), pin(basis_in), pin(grads))
    keep, send = call(
        split_in_kernel, "split_in", (rows(half, F32), rows(half, F32)), flops=8 * 10**9
    )(acc)
    got = lax.ppermute(send, "tensor", core)
    early = call(choose_kernel, "choose", jax.ShapeDtypeStruct((wide, EARLY), BF16))(early, pick)
    keep_in, send_in = call(
        pair_in_kernel, "pair_in", (rows(half, F32), rows(half + 16, BF16)), after=[early]
    )(keep, got)
    got_in = lax.ppermute(send_in, "tensor", across)

    split = call(
        rotate_out_kernel,
        "rotate_out",
        [rows(2 * cap, F32)] * (2 * experts),
        [hbm, vmem, vmem, vmem],
        [
            pltpu.VMEM(partial.shape, F32),
            pltpu.VMEM((tokens, 2, grads.shape[2] - EARLY), BF16),
            pltpu.SemaphoreType.DMA((grads.shape[2] // CHUNK + 1,)),
        ],
        after=[send_in],
    )(pin(grads), pick, basis_out, early)
    got = [lax.ppermute(x, "tensor", core) for x in split[experts:]]
    keep, send = call(
        pair_out_kernel, "pair_out", (rows(wide, F32), rows(wide, BF16)), after=[got_in]
    )(*split[:experts], *got)
    got = lax.ppermute(send, "tensor", across)

    slab = half // dp
    *pieces, own = call(
        round_in_kernel, "round_in", [rows(slab + LABEL_ROWS, BF16)] * dp + [rows(slab, BF16)]
    )(keep_in, got_in, label)
    other = [lax.ppermute(own, "tensor", core)]
    pieces = [pieces[0]] + [swap(pieces[k], k) for k in DISTANCES]
    out = call(round_kernel, "round_out", rows(wide, BF16), after=other)(keep, got)
    outs = [swap(out, k) for k in LATEST]
    mine = call(stack_kernel, "stack_in", [rows(3 * slab // 2, BF16)] * 2)(*pieces[1:])
    other += [lax.ppermute(x, "tensor", core) for x in mine]
    masked = jax.ShapeDtypeStruct((experts, dp * cap // 2, dp * 128), BF16)
    masked_own, divisor = call(
        mask_own_kernel,
        "mask_own",
        (masked, jax.ShapeDtypeStruct((experts, 8, 128), F32)),
        [smem] + [vmem] * dp,
    )(expert_counts, *pieces)
    masked_other = call(mask_other_kernel, "mask_other", masked, after=[divisor])(*other, *pieces)
    result = jax.ShapeDtypeStruct((experts, 128, 128), F32)
    return call(
        blocks_kernel,
        "blocks",
        result,
        scratch=[pltpu.VMEM(result.shape, F32), pltpu.SemaphoreType.DMA((experts,))],
        out_specs=hbm,
    )(divisor, masked_own, masked_other, out, *outs)


EX_DEV = 1


def compact(routes, expert, capacity):
    tok_count = routes.shape[0]
    second_hit = routes[:, 1] == expert
    routed = (routes[:, 0] == expert) | second_hit
    order = jnp.cumsum(routed.astype(jnp.int32)) - 1
    slots = jnp.arange(capacity, dtype=jnp.int32)
    match = routed[None, :] & (order[None, :] == slots[:, None])
    token_index = jnp.arange(tok_count, dtype=jnp.int32)
    positions = jnp.sum(jnp.where(match, token_index[None, :], 0), axis=1)
    filled = jnp.any(match, axis=1)
    return (positions, filled, second_hit[positions])


def general(acts, grads, routes, example_ids, expert_counts, basis_in, basis_out):
    capacity = acts.shape[0] // 2
    experts = basis_in.shape[0]
    parts_in, parts_out, label_rows = ([], [], [])
    for expert in range(experts):
        positions, filled, second = compact(routes, expert, capacity)
        chosen = grads[positions]
        grad_rows = jnp.where(second[:, None], chosen[:, 1, :], chosen[:, 0, :])
        parts_in.append(
            jnp.dot(acts[positions], basis_in[expert], preferred_element_type=jnp.float32)
        )
        parts_out.append(jnp.dot(grad_rows, basis_out[expert], preferred_element_type=jnp.float32))
        label_rows.append(jnp.where(filled, example_ids[positions], -1))
    part_in = jnp.stack(parts_in)
    part_out = jnp.stack(parts_out)
    labels = jnp.stack(label_rows)
    slice_width = basis_out.shape[2] // lax.axis_size("tensor")
    summed_in, summed_out = lax.psum((part_in, part_out), "tensor")
    rot_in = summed_in.astype(jnp.bfloat16)
    rot_out = lax.dynamic_slice_in_dim(
        summed_out.astype(jnp.bfloat16), lax.axis_index("tensor") * slice_width, slice_width, 2
    )
    owned_count = EX_DEV
    wanted = jnp.arange(lax.axis_size("dp") * owned_count, dtype=jnp.int32)
    onehot = (labels[:, :, None] == wanted[None, None, :]).astype(jnp.bfloat16)
    spread = onehot[:, :, :, None] * rot_out[:, :, None, :]
    owned_sums = lax.psum_scatter(
        jnp.einsum("ecnw,eca->newa", spread, rot_in, preferred_element_type=jnp.float32),
        "dp",
        scatter_dimension=0,
        tiled=True,
    )
    squared = jnp.sum(owned_sums * owned_sums, axis=0)
    totals = lax.psum_scatter(squared, "dp", scatter_dimension=2, tiled=True)
    return totals / expert_counts.astype(jnp.float32)[:, None, None]


def shards(*args):
    experts, _, width = args[5].shape
    sizes = (lax.axis_size("dp"), lax.axis_size("tensor"), experts, width)
    fits = sizes == (4, 4, 2, 512) and args[0].shape[0] == 384
    return (fast if fits else general)(*args)


def solution(mesh):
    placed = (
        P(("group", "dp"), "tensor"),
        P(("group", "dp"), None, "tensor"),
        P(("group", "dp"), None),
        P(("group", "dp")),
        P("group"),
        P(None, "tensor", None),
        P(None, "tensor", None),
    )
    return jax.shard_map(
        shards, mesh=mesh, in_specs=placed, out_specs=P("group", "tensor", "dp"), check_vma=False
    )
```

```python
import functools

import jax
import jax.numpy as jnp
from jax import lax
from jax.experimental import pallas as pl
from jax.experimental.pallas import tpu as pltpu
from jax.sharding import PartitionSpec as P

F32 = jnp.float32
BF16 = jnp.bfloat16
CHUNK = 1024
VMEM = 20 * 2**20
EARLY = 2048
DISTANCES = (3, 2, 1)
LATEST = (1, 3, 2)
LABEL_ROWS = 16


def iota(shape, dim):
    return lax.broadcasted_iota(jnp.int32, shape, dim)


def dot(a, b):
    return jnp.dot(a, b, preferred_element_type=F32)


def fetcher(sems):
    count = iter(range(sems.shape[0]))

    def fetch(src, dst):
        copy = pltpu.make_async_copy(src, dst, sems.at[next(count)])
        copy.start()
        return copy

    return fetch


def rotate_in_kernel(
    acts, routes, ids, basis_in, grads,
    acc, label, pick, early,
    acts_v, routes_v, ids_v, basis_v, sems,
):
    tokens = acts.shape[0]
    experts = basis_in.shape[0]
    cap = tokens // 2
    fetch = fetcher(sems)
    first = [fetch(routes, routes_v), fetch(ids, ids_v)]
    acts_in = fetch(acts, acts_v)
    bases = [fetch(basis_in.at[e], basis_v.at[e]) for e in range(experts)]
    grads_in = fetch(grads.at[:, :, pl.ds(0, early.shape[2])], early)
    for copy in first:
        copy.wait()
    hits = [
        jnp.max((routes_v[...] == e).astype(F32), axis=0, keepdims=True) for e in range(experts)
    ]
    rows = jnp.concatenate(hits + [jnp.zeros((8 - experts, tokens), F32)], axis=0).astype(BF16)
    upto = (iota((tokens, tokens), 0) <= iota((tokens, tokens), 1)).astype(BF16)
    order = dot(rows, upto)
    slots = iota((cap, tokens), 0).astype(F32) + 1.0
    pick_in = jnp.concatenate(
        [((order[e : e + 1] == slots) & (hits[e] > 0.5)).astype(BF16) for e in range(experts)],
        axis=0,
    )
    repeat = (iota((tokens, 2 * tokens), 0) == iota((tokens, 2 * tokens), 1) // 2).astype(BF16)
    wide = dot(
        jnp.concatenate(
            [order[:experts], routes_v[...].astype(F32), jnp.zeros((6 - experts, tokens), F32)],
            axis=0,
        ).astype(BF16),
        repeat,
    )
    odd = iota((1, 2 * tokens), 1) % 2 == 1
    routed_to = jnp.where(odd, wide[experts + 1 : experts + 2], wide[experts : experts + 1])
    slots = iota((cap, 2 * tokens), 0).astype(F32) + 1.0
    for e in range(experts):
        pick[e * cap : (e + 1) * cap, :] = (
            (wide[e : e + 1] == slots) & (routed_to == float(e))
        ).astype(BF16)
    numbers = jnp.broadcast_to(ids_v[...].reshape(1, tokens).astype(F32) + 1.0, (8, tokens)).astype(BF16)
    named = lax.dot_general(numbers, pick_in, (((1,), (1,)), ((), ())), preferred_element_type=F32)
    block = jnp.zeros((LABEL_ROWS, 128), F32)
    row = iota((LABEL_ROWS, 128), 0)
    half = cap // 2
    for at in range(2 * experts):
        mine = named[0:1, at * half : (at + 1) * half]
        mine = jnp.concatenate([mine, jnp.zeros((1, 128 - half), F32)], axis=1)
        block = jnp.where(row == at, mine, block)
    label[...] = block.astype(BF16)

    acts_in.wait()
    chosen = dot(pick_in, acts_v[...]).astype(BF16)
    for e in range(experts):
        bases[e].wait()
        acc[e] = dot(chosen[e * cap : (e + 1) * cap], basis_v[e])
    grads_in.wait()


def split_in_kernel(acc, keep, send):
    experts, cap, width = acc.shape
    core = lax.rem(lax.axis_index("tensor"), 2)
    half = cap // 2
    at = 0
    for q in range(width // 128):
        for e in range(experts):
            for ref, which in ((keep, core), (send, 1 - core)):
                ref[at : at + half, :] = acc[
                    e, pl.ds(pl.multiple_of(which * half, 8), half), q * 128 : (q + 1) * 128
                ]
            at += half


def choose(pick, rows):
    rows = rows.reshape(2 * rows.shape[0], rows.shape[2])
    cap, first = rows.shape[0] // 4, 128
    starts = range(0, pick.shape[0], cap)
    low = dot(
        jnp.concatenate([pick[at : at + first, : 2 * first] for at in starts], axis=0),
        rows[: 2 * first],
    )
    high = dot(pick[:, 2 * first :], rows[2 * first :])
    parts = []
    for e, at in enumerate(starts):
        parts.append(high[at : at + first] + low[e * first : (e + 1) * first])
        parts.append(high[at + first : at + cap])
    return jnp.concatenate(parts, axis=0).astype(BF16)


def choose_kernel(grads, pick, out):
    out[...] = choose(pick, grads[...])


def rotate_out_kernel(grads, pick, basis_out, early, acc, grads_v, sems):
    hidden = grads.shape[2]
    experts, cap, _ = acc.shape
    fetch = fetcher(sems)
    done = early.shape[1]
    cuts = sorted({done, done + CHUNK // 2, *range(done + CHUNK, hidden, CHUNK), hidden})
    parts = [(at, pl.ds(at, end - at)) for at, end in zip(cuts, cuts[1:])]
    copies = [
        fetch(grads.at[:, :, part], grads_v.at[:, :, pl.ds(at - done, part.size)])
        for at, part in parts
    ]
    for e in range(experts):
        acc[e] = dot(early[e * cap : (e + 1) * cap, :], basis_out[e, :done, :])
    for (at, part), copy in zip(parts, copies):
        copy.wait()
        chosen = choose(pick, grads_v[:, :, pl.ds(at - done, part.size)])
        for e in range(experts):
            acc[e] += dot(chosen[e * cap : (e + 1) * cap], basis_out[e, part, :])


def split_out_kernel(acc, *refs):
    experts, cap, width = acc.shape
    core = lax.rem(lax.axis_index("tensor"), 2)
    for e in range(experts):
        for ref, which in ((refs[e], core), (refs[experts + e], 1 - core)):
            for x in range(width // 256):
                ref[x * cap : (x + 1) * cap, :] = acc[
                    e, :, pl.ds(pl.multiple_of((2 * x + which) * 128, 128), 128)
                ]


def pair_in_kernel(kept, got, keep, send):
    total = kept[...] + got[...]
    outer = total.shape[0]
    keep[...] = total
    send[:outer, :] = total.astype(BF16)
    send[outer:, :] = jnp.zeros((send.shape[0] - outer, 128), BF16)


def round_in_kernel(kept, got, label, *pays):
    slab = kept.shape[0] // len(pays)
    d = lax.axis_index("dp")
    for k, pay in enumerate(pays):
        rows = pl.ds(pl.multiple_of((d ^ k) * slab, 16), slab)
        pay[:slab, :] = (kept[rows, :] + got[rows, :].astype(F32)).astype(BF16)
        pay[slab:, :] = label[...]


def pair_out_kernel(*refs):
    *given, keep, send = refs
    experts = len(given) // 2
    cap = keep.shape[0] // experts
    x = lax.div(lax.axis_index("tensor"), 2)
    mine = pl.ds(pl.multiple_of(x * cap, 16), cap)
    other = pl.ds(pl.multiple_of((1 - x) * cap, 16), cap)
    for e in range(experts):
        kept, got = given[e], given[experts + e]
        at = pl.ds(e * cap, cap)
        keep[at, :] = kept[mine, :] + got[mine, :]
        send[at, :] = (kept[other, :] + got[other, :]).astype(BF16)


def round_kernel(kept, got, out):
    out[...] = (kept[...] + got[...].astype(F32)).astype(BF16)


def copy_kernel(x, out):
    out[...] = x[: out.shape[0], :]


def stack_kernel(*refs):
    *pieces, first, second = refs
    rows = first.shape[0]
    slab = 2 * rows // len(pieces)
    for k, piece in enumerate(pieces):
        for at in range(0, slab, slab // 2):
            to = k * slab + at
            out = (first, second)[to // rows]
            out[to % rows : to % rows + slab // 2, :] = piece[at : at + slab // 2, :]


def mask(which, parts, pieces, out):
    experts, slots, _ = out.shape
    half = slots // len(pieces)
    slab = experts * half
    every = jnp.concatenate(parts, axis=0).astype(F32)
    for e in range(experts):
        rows, labels = [], []
        for k, piece in enumerate(pieces):
            rows.append(every[k * slab + e * half : k * slab + (e + 1) * half])
            label = piece[slab : slab + LABEL_ROWS, :].astype(F32)[2 * e : 2 * e + 2, :half]
            labels.append(jnp.where(which == 0, label[0:1], label[1:2]))
        rows = jnp.concatenate(rows, axis=0)
        labels = jnp.concatenate(labels, axis=1)
        labels = jnp.broadcast_to(labels, (128, labels.shape[1])).T
        for n in range(len(pieces)):
            out[e, :, n * 128 : (n + 1) * 128] = jnp.where(
                labels == float(n + 1), rows, 0.0
            ).astype(BF16)


def mask_own_kernel(counts, *refs):
    *pieces, out, divisor = refs
    slab = out.shape[0] * out.shape[1] // len(pieces)
    core = lax.rem(lax.axis_index("tensor"), 2)
    mask(core, [piece[:slab, :] for piece in pieces], pieces, out)
    for e in range(out.shape[0]):
        divisor[e] = jnp.full(divisor.shape[1:], counts[e].astype(F32), F32)


def mask_other_kernel(first, second, third, *refs):
    *pieces, out = refs
    core = lax.rem(lax.axis_index("tensor"), 2)
    mask(1 - core, [first[...], second[...], third[...]], pieces, out)


def blocks_kernel(divisor, masked_own, masked_other, own, *refs):
    *far, result, final, sems = refs
    outs = [own] + [far[LATEST.index(k)] for k in DISTANCES]
    experts, slots, _ = masked_own.shape
    half = slots // len(outs)
    core = lax.rem(lax.axis_index("tensor"), 2)
    copies = []
    for e in range(experts):
        rows = [
            ref[pl.ds(pl.multiple_of((2 * e + which) * half, 16), half), :]
            for which in (core, 1 - core)
            for ref in outs
        ]
        rows = jnp.concatenate(rows, axis=0).T
        blocks = dot(rows[:, :slots], masked_own[e]) + dot(rows[:, slots:], masked_other[e])
        squares = blocks * blocks
        summed = squares[:, :128]
        for at in range(128, squares.shape[1], 128):
            summed = summed + squares[:, at : at + 128]
        final[e] = summed / divisor[e][:1]
        copies.append(pltpu.make_async_copy(final.at[e], result.at[e], sems.at[e]))
        copies[-1].start()
    for copy in copies:
        copy.wait()


def call(kernel, name, out_shape, specs=None, scratch=(), out_specs=None, flops=1, after=()):
    vmem = pl.BlockSpec(memory_space=pltpu.VMEM)
    given = {} if out_specs is None else {"out_specs": out_specs}

    def run(*args):
        def body(*refs):
            kernel(*refs[: len(args)], *refs[len(args) + len(after) :])

        return pl.pallas_call(
            body,
            out_shape=out_shape,
            in_specs=(specs or [vmem] * len(args)) + [vmem] * len(after),
            scratch_shapes=scratch,
            compiler_params=pltpu.CompilerParams(vmem_limit_bytes=VMEM),
            cost_estimate=pl.CostEstimate(flops=flops, bytes_accessed=1, transcendentals=0),
            name=name,
            **given,
        )(*args, *after)

    return run


def fast(acts, grads, routes, example_ids, expert_counts, basis_in, basis_out):
    tokens = acts.shape[0]
    experts, features, width = basis_in.shape
    cap = tokens // 2
    dp = lax.axis_size("dp")
    wide = experts * cap
    half = wide * width // 256
    hbm = pl.BlockSpec(memory_space=pltpu.HBM)
    vmem = pl.BlockSpec(memory_space=pltpu.VMEM)
    smem = pl.BlockSpec(memory_space=pltpu.SMEM)

    def pin(x):
        return pltpu.with_memory_space_constraint(x, pltpu.HBM)

    def rows(count, dtype):
        return jax.ShapeDtypeStruct((count, 128), dtype)

    core = [(t, t ^ 1) for t in range(4)]
    across = [(t, t ^ 2) for t in range(4)]

    def swap(x, k):
        return lax.ppermute(x, "dp", [(d, d ^ k) for d in range(dp)])

    partial = jax.ShapeDtypeStruct((experts, cap, width), F32)
    acc, label, pick, early = call(
        rotate_in_kernel,
        "rotate_in",
        (
            partial,
            rows(LABEL_ROWS, BF16),
            jax.ShapeDtypeStruct((wide, 2 * tokens), BF16),
            jax.ShapeDtypeStruct((tokens, 2, EARLY), BF16),
        ),
        [hbm] * 5,
        [
            pltpu.VMEM(acts.shape, BF16),
            pltpu.VMEM((2, tokens), jnp.int32),
            pltpu.VMEM((tokens,), jnp.int32),
            pltpu.VMEM(basis_in.shape, BF16),
            pltpu.SemaphoreType.DMA((4 + experts,)),
        ],
    )(pin(acts), pin(routes.T), pin(example_ids), pin(basis_in), pin(grads))
    keep, send = call(
        split_in_kernel, "split_in", (rows(half, F32), rows(half, F32)), flops=8 * 10**9
    )(acc)
    got = lax.ppermute(send, "tensor", core)
    early = call(choose_kernel, "choose", jax.ShapeDtypeStruct((wide, EARLY), BF16))(early, pick)
    keep_in, send_in = call(
        pair_in_kernel, "pair_in", (rows(half, F32), rows(half + 16, BF16)), after=[early]
    )(keep, got)
    got_in = lax.ppermute(send_in, "tensor", across)

    acc = call(
        rotate_out_kernel,
        "rotate_out",
        partial,
        [hbm, vmem, vmem, vmem],
        [
            pltpu.VMEM((tokens, 2, grads.shape[2] - EARLY), BF16),
            pltpu.SemaphoreType.DMA((grads.shape[2] // CHUNK + 1,)),
        ],
        after=[send_in],
    )(pin(grads), pick, basis_out, early)
    split = call(split_out_kernel, "split_out", [rows(2 * cap, F32)] * (2 * experts))(acc)
    got = [lax.ppermute(x, "tensor", core) for x in split[experts:]]
    keep, send = call(
        pair_out_kernel, "pair_out", (rows(wide, F32), rows(wide, BF16)), after=[got_in]
    )(*split[:experts], *got)
    got = lax.ppermute(send, "tensor", across)

    slab = half // dp
    pieces = call(round_in_kernel, "round_in", [rows(slab + LABEL_ROWS, BF16)] * dp)(
        keep_in, got_in, label
    )
    own = call(copy_kernel, "own_in", rows(slab, BF16))(pieces[0])
    other = [lax.ppermute(own, "tensor", core)]
    pieces = [pieces[0]] + [swap(pieces[k], k) for k in DISTANCES]
    out = call(round_kernel, "round_out", rows(wide, BF16), after=other)(keep, got)
    outs = [swap(out, k) for k in LATEST]
    mine = call(stack_kernel, "stack_in", [rows(3 * slab // 2, BF16)] * 2)(*pieces[1:])
    other += [lax.ppermute(x, "tensor", core) for x in mine]
    masked = jax.ShapeDtypeStruct((experts, dp * cap // 2, dp * 128), BF16)
    masked_own, divisor = call(
        mask_own_kernel,
        "mask_own",
        (masked, jax.ShapeDtypeStruct((experts, 8, 128), F32)),
        [smem] + [vmem] * dp,
    )(expert_counts, *pieces)
    masked_other = call(mask_other_kernel, "mask_other", masked, after=[divisor])(*other, *pieces)
    result = jax.ShapeDtypeStruct((experts, 128, 128), F32)
    return call(
        blocks_kernel,
        "blocks",
        result,
        scratch=[pltpu.VMEM(result.shape, F32), pltpu.SemaphoreType.DMA((experts,))],
        out_specs=hbm,
    )(divisor, masked_own, masked_other, out, *outs)


EX_DEV = 1


def compact(routes, expert, capacity):
    tok_count = routes.shape[0]
    second_hit = routes[:, 1] == expert
    routed = (routes[:, 0] == expert) | second_hit
    order = jnp.cumsum(routed.astype(jnp.int32)) - 1
    slots = jnp.arange(capacity, dtype=jnp.int32)
    match = routed[None, :] & (order[None, :] == slots[:, None])
    token_index = jnp.arange(tok_count, dtype=jnp.int32)
    positions = jnp.sum(jnp.where(match, token_index[None, :], 0), axis=1)
    filled = jnp.any(match, axis=1)
    return (positions, filled, second_hit[positions])


def general(acts, grads, routes, example_ids, expert_counts, basis_in, basis_out):
    capacity = acts.shape[0] // 2
    experts = basis_in.shape[0]
    parts_in, parts_out, label_rows = ([], [], [])
    for expert in range(experts):
        positions, filled, second = compact(routes, expert, capacity)
        chosen = grads[positions]
        grad_rows = jnp.where(second[:, None], chosen[:, 1, :], chosen[:, 0, :])
        parts_in.append(
            jnp.dot(acts[positions], basis_in[expert], preferred_element_type=jnp.float32)
        )
        parts_out.append(jnp.dot(grad_rows, basis_out[expert], preferred_element_type=jnp.float32))
        label_rows.append(jnp.where(filled, example_ids[positions], -1))
    part_in = jnp.stack(parts_in)
    part_out = jnp.stack(parts_out)
    labels = jnp.stack(label_rows)
    slice_width = basis_out.shape[2] // lax.axis_size("tensor")
    summed_in, summed_out = lax.psum((part_in, part_out), "tensor")
    rot_in = summed_in.astype(jnp.bfloat16)
    rot_out = lax.dynamic_slice_in_dim(
        summed_out.astype(jnp.bfloat16), lax.axis_index("tensor") * slice_width, slice_width, 2
    )
    owned_count = EX_DEV
    wanted = jnp.arange(lax.axis_size("dp") * owned_count, dtype=jnp.int32)
    onehot = (labels[:, :, None] == wanted[None, None, :]).astype(jnp.bfloat16)
    spread = onehot[:, :, :, None] * rot_out[:, :, None, :]
    owned_sums = lax.psum_scatter(
        jnp.einsum("ecnw,eca->newa", spread, rot_in, preferred_element_type=jnp.float32),
        "dp",
        scatter_dimension=0,
        tiled=True,
    )
    squared = jnp.sum(owned_sums * owned_sums, axis=0)
    totals = lax.psum_scatter(squared, "dp", scatter_dimension=2, tiled=True)
    return totals / expert_counts.astype(jnp.float32)[:, None, None]


def shards(*args):
    experts, _, width = args[5].shape
    sizes = (lax.axis_size("dp"), lax.axis_size("tensor"), experts, width)
    fits = sizes == (4, 4, 2, 512) and args[0].shape[0] == 384
    return (fast if fits else general)(*args)


def solution(mesh):
    placed = (
        P(("group", "dp"), "tensor"),
        P(("group", "dp"), None, "tensor"),
        P(("group", "dp"), None),
        P(("group", "dp")),
        P("group"),
        P(None, "tensor", None),
        P(None, "tensor", None),
    )
    return jax.shard_map(
        shards, mesh=mesh, in_specs=placed, out_specs=P("group", "tensor", "dp"), check_vma=False
    )
```
